32 devices in a mesh: win: 8 (over y, x, core), dp: 4 (over z).
Axes of the slice: x: 2, y: 2, z: 4, core: 2. Of those that a mesh axis runs over, the one named last changes fastest.
Arguments:
- patches: bfloat16 [4, 384, 49, 512], P('dp', 'win'), may hold values from -6 to 6
- regional: bfloat16 [4, 384, 512], P('dp', 'win'), may hold values from -6 to 6
- window_image: int32 [4, 384], P('dp'), may hold values from 0 to 2, as said below
- in_gain: bfloat16 [512], replicated, may hold values from 0.25 to 1.75
- in_shift: bfloat16 [512], replicated, may hold values from -4 to 4
- w_qkv: bfloat16 [512, 1536], replicated, may hold values from -0.25 to 0.25
- qkv_bias: bfloat16 [2, 512], replicated, may hold values from -4 to 4
- w_out: bfloat16 [512, 512], replicated, may hold values from -1 to 1
- out_bias: bfloat16 [512], replicated, may hold values from -4 to 4
- mlp_gain: bfloat16 [512], replicated, may hold values from 0.25 to 1.75
- mlp_shift: bfloat16 [512], replicated, may hold values from -4 to 4
- w_up: bfloat16 [512, 2048], replicated, may hold values from -0.25 to 0.25
- up_bias: bfloat16 [2048], replicated, may hold values from -4 to 4
- w_down: bfloat16 [2048, 512], replicated, may hold values from -0.125 to 0.125
- down_bias: bfloat16 [512], replicated, may hold values from -4 to 4
- patch_cot: bfloat16 [4, 384, 49, 512], P('dp', 'win'), may hold values from -6 to 6
- region_cot: bfloat16 [4, 384, 512], P('dp', 'win'), may hold values from -6 to 6
Outputs:
- patch_out: bfloat16 [4, 384, 49, 512], P('dp', 'win')
- region_out: bfloat16 [4, 384, 512], P('dp', 'win')
- patch_grad: bfloat16 [4, 384, 49, 512], P('dp', 'win')
- region_grad: bfloat16 [4, 384, 512], P('dp', 'win')
- in_gain_grad: float32 [512], replicated
- in_shift_grad: float32 [512], replicated
- qkv_grad: float32 [512, 1536], replicated
- qkv_bias_grad: float32 [2, 512], replicated
- out_grad: float32 [512, 512], replicated
- out_bias_grad: float32 [512], replicated
- mlp_gain_grad: float32 [512], replicated
- mlp_shift_grad: float32 [512], replicated
- up_grad: float32 [512, 2048], replicated
- up_bias_grad: float32 [2048], replicated
- down_grad: float32 [2048, 512], replicated
- down_bias_grad: float32 [512], replicated
The draws below stay inside these ranges and needn't reach their ends.
Inputs may be any that keep to these rules, and one draw needn't show every extreme that they name: `window_image`: numbers a group's images from 0; each image but the highest-numbered one holds 49, 81 or 144 windows, and the highest-numbered one holds the rest of the group's windows; an image's windows lie at scattered places of the group, and the group's first and last windows belong to image 0.
All inputs are finite; a program needn't handle non-finite values.
Results may differ from the reference program's by a relative error of at most 0.018.
Values may be sent and summed in bfloat16 or wider, within the bound.
A program may use at most 256 MiB of HBM per device.

```python
import jax
import jax.numpy as jnp
from jax import lax

D = 512
HEADS = 16
HD = 32
FF = 2048
PATCH = 49
RC_SMALL = 49
RC_MID = 81
RC_BIG = 144
GWIN = 384
GROUPS = 4


def draw_window_image(key, part):
    key = jax.random.fold_in(key, 11)
    pick_key, order_key = jax.random.split(key)
    sizes_table = jnp.array([RC_SMALL, RC_MID, RC_BIG], jnp.int32)
    most_images = GWIN // RC_SMALL + 1
    top_image = (GWIN - 1) // RC_BIG
    picked = jax.random.randint(pick_key, (GROUPS, most_images), 0, 3)
    image_sizes = jnp.sum((picked[:, :, None] == jnp.arange(3, dtype=jnp.int32)[None, None, :]).astype(jnp.int32) * sizes_table, axis=2)
    image_ends = jnp.cumsum(image_sizes, axis=1)
    positions = jnp.arange(GWIN, dtype=jnp.int32)
    ordered = jnp.sum((image_ends[:, None, :] <= positions[None, :, None]).astype(jnp.int32), axis=2)
    ordered = jnp.minimum(ordered, top_image)

    def scatter_order(group_key):
        inner_order = jax.random.permutation(group_key, GWIN - 2).astype(jnp.int32) + 2
        return jnp.concatenate([jnp.zeros((1,), jnp.int32), inner_order, jnp.ones((1,), jnp.int32)])
    orders = jax.vmap(scatter_order)(jax.random.split(order_key, GROUPS))
    return jnp.take_along_axis(ordered, orders, axis=1).astype(jnp.int32)


def levels(stream_key, extent, cuts, least, top_value):
    def one(position, blocks):
        draws = jax.random.uniform(jax.random.fold_in(jax.random.fold_in(stream_key, 6), position), (blocks,), jnp.float32, least / len(cuts), top_value / len(cuts))
        return jnp.repeat(jnp.exp(draws), extent[position] // blocks).reshape((-1,) + (1,) * (len(extent) - position - 1))

    loudness = one(*cuts[0])
    for cut in cuts[1:]:
        loudness = loudness * one(*cut)
    return loudness


def noise(rng, dims, width, most, pieces=(), kind=jnp.bfloat16):
    level = levels(rng, dims, pieces, -0.22, 0.18) if pieces else 1.0
    values = jax.random.normal(rng, dims, jnp.float32) * width * level
    return jnp.minimum(jnp.maximum(values, -most), most).astype(kind)


def setup_inputs(seed: int = 0) -> dict:
    key_list = jax.random.split(jax.random.key(seed), 18)
    patches = noise(key_list[0], (GROUPS, GWIN, PATCH, D), 1.0, 6.0, ((0, 4), (1, 8)))
    regional = noise(key_list[1], (GROUPS, GWIN, D), 1.0, 6.0, ((0, 4), (1, 8)))
    window_image = draw_window_image(jax.random.fold_in(key_list[17], 71), 0)
    in_gain = jnp.clip(1.0 + 0.15 * jax.random.normal(key_list[3], (D,), jnp.float32), 0.25, 1.75).astype(jnp.bfloat16)
    in_shift = noise(key_list[4], (D,), 0.3, 4.0)
    w_qkv = noise(key_list[5], (D, 3 * D), D ** -0.5, 0.25)
    qkv_bias = noise(key_list[6], (2, D), 0.3, 4.0)
    w_out = noise(key_list[7], (D, D), (D // 16) ** -0.5, 1.0)
    out_bias = noise(key_list[8], (D,), 0.3, 4.0)
    mlp_gain = jnp.clip(1.0 + 0.15 * jax.random.normal(key_list[9], (D,), jnp.float32), 0.25, 1.75).astype(jnp.bfloat16)
    mlp_shift = noise(key_list[10], (D,), 0.3, 4.0)
    w_up = noise(key_list[11], (D, FF), D ** -0.5, 0.25)
    up_bias = noise(key_list[12], (FF,), 0.3, 4.0)
    w_down = noise(key_list[13], (FF, D), FF ** -0.5, 0.125)
    down_bias = noise(key_list[14], (D,), 0.3, 4.0)
    patch_cot = noise(key_list[15], (GROUPS, GWIN, PATCH, D), 1.0, 6.0, ((0, 4), (1, 8)))
    region_cot = noise(key_list[16], (GROUPS, GWIN, D), 1.0, 6.0, ((0, 4), (1, 8)))
    return {"patches": patches, "regional": regional, "window_image": window_image, "in_gain": in_gain, "in_shift": in_shift, "w_qkv": w_qkv, "qkv_bias": qkv_bias, "w_out": w_out, "out_bias": out_bias, "mlp_gain": mlp_gain, "mlp_shift": mlp_shift, "w_up": w_up, "up_bias": up_bias, "w_down": w_down, "down_bias": down_bias, "patch_cot": patch_cot, "region_cot": region_cot}


EPSILON = 1e-06
MASKED_SCORE = -1e+30
PRECISE = lax.Precision.HIGHEST

@jax.custom_vjp
def low(v):
    return lax.optimization_barrier(v.astype(jnp.bfloat16)).astype(jnp.float32)

@jax.custom_vjp
def low_back(v):
    return v

def low_keep(v):
    return (low(v), None)

def low_pass(kept, grad):
    return (grad,)

def back_keep(v):
    return (v, None)

def back_low(kept, grad):
    return (low(grad),)
low.defvjp(low_keep, low_pass)
low_back.defvjp(back_keep, back_low)

def norm_rows(rows, norm_gain, norm_shift):
    average = lax.optimization_barrier(jnp.mean(rows, axis=-1, keepdims=True))
    centred = rows - average
    spread = lax.optimization_barrier(jnp.mean(centred * centred, axis=-1, keepdims=True))
    return centred * lax.rsqrt(spread + EPSILON) * norm_gain + norm_shift

def project(normed, w_qkv, qkv_bias):
    bias_row = jnp.concatenate([qkv_bias[0], jnp.zeros_like(qkv_bias[0]), qkv_bias[1]])
    return low(low_back(jnp.dot(normed, w_qkv, precision=PRECISE) + bias_row))

def branch_out(merged, w_out, out_bias):
    return low_back(jnp.dot(merged, w_out, precision=PRECISE) + out_bias)

def layer_group(patch_rows, region_rows, weights, same_image):
    in_gain, in_shift, w_qkv, qkv_bias, w_out, out_bias, mlp_gain, mlp_shift, w_up, up_bias, w_down, down_bias = weights
    scaling = HD ** (-0.5)
    region_in = low(norm_rows(region_rows, in_gain, in_shift))
    triple = project(region_in, w_qkv, qkv_bias)
    queries = triple[:, :D].reshape(GWIN, HEADS, HD)
    key_rows = triple[:, D:2 * D].reshape(GWIN, HEADS, HD)
    values = triple[:, 2 * D:].reshape(GWIN, HEADS, HD)
    scores = low_back(jnp.einsum('qhe,khe->hqk', queries, key_rows, precision=PRECISE) * scaling)
    scores = jnp.where(same_image[None], scores, MASKED_SCORE)
    probs = low(jax.nn.softmax(scores, axis=-1))
    merged = low(low_back(jnp.einsum('hqk,khe->qhe', probs, values, precision=PRECISE).reshape(GWIN, D)))
    region_mid = region_rows + branch_out(merged, w_out, out_bias)
    tokens = jnp.concatenate([region_mid[:, None, :], patch_rows], axis=1)
    flat_rows = tokens.reshape(-1, D)
    local_in = low(norm_rows(flat_rows, in_gain, in_shift))
    local_triple = project(local_in, w_qkv, qkv_bias).reshape(GWIN, PATCH + 1, 3, HEADS, HD)
    local_scores = low_back(jnp.einsum('wqhe,wkhe->whqk', local_triple[:, :, 0], local_triple[:, :, 1], precision=PRECISE) * scaling)
    local_probs = low(jax.nn.softmax(local_scores, axis=-1))
    local_merged = jnp.einsum('whqk,wkhe->wqhe', local_probs, local_triple[:, :, 2], precision=PRECISE)
    local_merged = low(low_back(local_merged.reshape(-1, D)))
    middle = flat_rows + branch_out(local_merged, w_out, out_bias)
    mlp_in = low(norm_rows(middle, mlp_gain, mlp_shift))
    hidden = low_back(jnp.dot(mlp_in, w_up, precision=PRECISE) + up_bias)
    active = low(jax.nn.gelu(hidden, approximate=False))
    result = middle + low_back(jnp.dot(active, w_down, precision=PRECISE) + down_bias)
    result = result.reshape(GWIN, PATCH + 1, D)
    return (result[:, 1:], result[:, 0])

def reference(patches, regional, window_image, in_gain, in_shift, w_qkv, qkv_bias, w_out, out_bias, mlp_gain, mlp_shift, w_up, up_bias, w_down, down_bias, patch_cot, region_cot):
    params = tuple((weight.astype(jnp.float32) for weight in (in_gain, in_shift, w_qkv, qkv_bias, w_out, out_bias, mlp_gain, mlp_shift, w_up, up_bias, w_down, down_bias)))

    def one_group(totals, inputs):
        patch_rows, region_rows, image_row, patch_back, region_back = inputs
        same_image = image_row[:, None] == image_row[None, :]

        def forward(patch_in, region_in, *weights):
            return layer_group(patch_in, region_in, weights, same_image)
        outputs, pullback = jax.vjp(forward, patch_rows.astype(jnp.float32), region_rows.astype(jnp.float32), *params)
        gradients = pullback((patch_back.astype(jnp.float32), region_back.astype(jnp.float32)))
        totals = tuple((total + grad_part for total, grad_part in zip(totals, gradients[2:])))
        shown = (outputs[0].astype(jnp.bfloat16), outputs[1].astype(jnp.bfloat16), gradients[0].astype(jnp.bfloat16), gradients[1].astype(jnp.bfloat16))
        return (totals, shown)
    empty_sums = tuple((jnp.zeros_like(weight) for weight in params))
    totals, stacked = lax.scan(one_group, empty_sums, (patches, regional, window_image, patch_cot, region_cot))
    return (stacked[0], stacked[1], stacked[2], stacked[3], totals[0], totals[1], totals[2], totals[3], totals[4], totals[5], totals[6], totals[7], totals[8], totals[9], totals[10], totals[11])
```

```python
import functools

import jax
import jax.numpy as jnp
from jax import lax
from jax.experimental import pallas as pl
from jax.experimental.pallas import tpu as pltpu
from jax.sharding import PartitionSpec as P

D = 512
HEADS = 16
HD = 32
FF = 2048
EPSILON = 1e-06
MASKED_SCORE = -1e30
SCALING = HD ** (-0.5)
LOG2E = 1.4426950408889634
TP = 64
WC = 16
f32 = jnp.float32
bf16 = jnp.bfloat16
VMEM_LIMIT = 60 * 2**20
MESH = pl.DeviceIdType.MESH


def nn(a, b):
    return lax.dot_general(a, b, (((1,), (0,)), ((), ())), preferred_element_type=f32)


def nt(a, b):
    return lax.dot_general(a, b, (((1,), (1,)), ((), ())), preferred_element_type=f32)


def tn(a, b):
    return lax.dot_general(a, b, (((0,), (0,)), ((), ())), preferred_element_type=f32)


def call(body, grid, ins, outs, scratch=(), name=None, collective_id=None):
    def spec(block, index):
        if block is None:
            return pl.BlockSpec(memory_space=pl.ANY)
        if index is None:
            return pl.BlockSpec(block, lambda *_: (0,) * len(block), pipeline_mode=pl.Buffered(1))
        return pl.BlockSpec(block, index)

    return pl.pallas_call(
        body,
        grid=grid,
        in_specs=[spec(b, i) for _, b, i in ins],
        out_specs=[spec(b, i) for _, b, i in outs],
        out_shape=[jax.ShapeDtypeStruct(s, d) for (s, d), _, _ in outs],
        scratch_shapes=list(scratch),
        compiler_params=pltpu.CompilerParams(
            vmem_limit_bytes=VMEM_LIMIT, collective_id=collective_id, has_side_effects=collective_id is not None
        ),
        name=name,
    )(*[a for a, _, _ in ins])


def whole(a):
    return (a, a.shape, None)


def whole_out(shape, dtype):
    return ((shape, dtype), shape, lambda *_: (0,) * len(shape))


def left(a):
    return (a, None, None)


def left_out(shape, dtype):
    return ((shape, dtype), None, None)


def norm_stats(rows):
    average = jnp.mean(rows, axis=-1, keepdims=True)
    centred = rows - average
    spread = jnp.mean(centred * centred, axis=-1, keepdims=True)
    inverse = lax.rsqrt(spread + EPSILON)
    return centred * inverse, inverse


def norm_back(vhat, inverse, gain, grad_out):
    scaled = grad_out * gain
    first = jnp.mean(scaled, axis=-1, keepdims=True)
    second = jnp.mean(scaled * vhat, axis=-1, keepdims=True)
    return inverse * (scaled - first - vhat * second)


def col(x):
    return jnp.sum(x, axis=0, keepdims=True)


class Place:
    def __init__(self, wins, dps):
        self.wins, self.dps = wins, dps
        self.win = lax.axis_index("win")
        self.dp = lax.axis_index("dp")
        self.core = lax.rem(self.win, 2)
        self.chip = self.win // 2
        self.chips = wins // 2

    def other_core(self):
        return {"win": self.chip * 2 + 1 - self.core}

    def at_chip(self, j):
        chip = lax.rem(self.chip + j, self.chips)
        return chip, {"win": chip * 2 + self.core}

    def at_dp(self, j):
        dp = lax.rem(self.dp + j, self.dps)
        return dp, {"dp": dp}

    def greet(self, all_wins=False):
        barrier = pltpu.get_barrier_semaphore()
        if all_wins:
            for j in range(1, self.wins):
                pl.semaphore_signal(barrier, inc=1, device_id={"win": lax.rem(self.win + j, self.wins)}, device_id_type=MESH)
        else:
            pl.semaphore_signal(barrier, inc=1, device_id=self.other_core(), device_id_type=MESH)
            for j in range(1, self.chips):
                pl.semaphore_signal(barrier, inc=1, device_id=self.at_chip(j)[1], device_id_type=MESH)
        for j in range(1, self.dps):
            pl.semaphore_signal(barrier, inc=1, device_id=self.at_dp(j)[1], device_id_type=MESH)

    def greeted(self, all_wins=False):
        near = self.wins - 1 if all_wins else self.chips
        pl.semaphore_wait(pltpu.get_barrier_semaphore(), near + self.dps - 1)


def rows_of(wins, dps):
    half = D // 2
    piece = half // (wins // 2)
    last = piece // dps if piece % (16 * dps) == 0 else piece
    return half, piece, last


def stream_scratch(wins, dps, columns):
    half, piece, last = rows_of(wins, dps)
    chips = wins // 2
    return [
        pltpu.VMEM((half, columns), bf16),
        pltpu.VMEM((half, columns), bf16),
        pltpu.VMEM((max(chips - 1, 1), piece, columns), bf16),
        pltpu.VMEM((piece, columns), bf16),
        pltpu.VMEM((max(dps - 1, 1), last, columns), bf16),
        pltpu.VMEM((piece, columns), bf16),
        pltpu.SemaphoreType.DMA((6 + 4 * chips + 4 * dps,)),
    ]


class Stream:
    PARTS = 7

    def __init__(self, place, source, final, refs, first=None):
        self.p = place
        self.source, self.final = source, final
        self.own, self.r1, self.r2, self.s, self.r3, self.s2, self.sem = refs
        self.half, self.piece, self.last = rows_of(place.wins, place.dps)
        self.split = self.last != self.piece
        self.slabs = self.half // 16
        self.columns = self.own.shape[1]

    def rows(self, start, size):
        return pl.ds(pl.multiple_of(start, 16), size)

    def remote(self, src, dst, to, k):
        return pltpu.make_async_remote_copy(
            src_ref=src, dst_ref=dst, send_sem=self.sem.at[2 * k], recv_sem=self.sem.at[2 * k + 1],
            device_id=to, device_id_type=MESH,
        )

    def _own(self):
        mine = self.rows(self.p.core * self.half, self.half)
        return pltpu.make_async_copy(self.source.at[mine], self.own, self.sem.at[0])

    def _put(self):
        mine = self.rows(self.p.core * self.half + self.p.chip * self.piece, self.piece)
        return pltpu.make_async_copy(self.s2, self.final.at[mine], self.sem.at[1])

    def _cores(self):
        other = self.rows((1 - self.p.core) * self.half, self.half)
        return [self.remote(self.source.at[other], self.r1, self.p.other_core(), 1)]

    def _chips(self):
        out = []
        for j in range(1, self.p.chips):
            chip, to = self.p.at_chip(j)
            out.append(self.remote(self.own.at[self.rows(chip * self.piece, self.piece)], self.r2.at[j - 1], to, 2 + j))
        return out

    def _dps(self):
        out = []
        for j in range(1, self.p.dps):
            dp, to = self.p.at_dp(j)
            src = self.s.at[self.rows(dp * self.last, self.last)] if self.split else self.s
            out.append(self.remote(src, self.r3.at[j - 1], to, 2 + self.p.chips + j))
        return out

    def _dps_back(self):
        out = []
        if self.split:
            for j in range(1, self.p.dps):
                mine = self.s2.at[self.rows(self.p.dp * self.last, self.last)]
                out.append(self.remote(mine, mine, self.p.at_dp(j)[1], 2 + self.p.chips + self.p.dps + j))
        return out

    def _chips_back(self):
        out = []
        for j in range(1, self.p.chips):
            mine = self.final.at[self.rows(self.p.core * self.half + self.p.chip * self.piece, self.piece)]
            out.append(self.remote(self.s2, mine, self.p.at_chip(j)[1], 2 + self.p.chips + 2 * self.p.dps + j))
        return out

    def _cores_back(self):
        mine = self.final.at[self.rows(self.p.core * self.half, self.half)]
        return [self.remote(mine, mine, self.p.other_core(), 2)]

    def start(self, copies):
        for c in copies:
            c.start()

    def wait(self, copies):
        for c in copies:
            c.wait()

    def load(self):
        self._own().start()

    def send_cores(self):
        self.start(self._cores())

    def send_chips(self):
        self._own().wait()
        self.wait(self._cores())

        def add(i, carry):
            at = self.rows(i * 16, 16)
            self.own[at] = (self.own[at].astype(f32) + self.r1[at].astype(f32)).astype(bf16)
            return carry

        lax.fori_loop(0, self.half // 16, add, 0)
        self.start(self._chips())

    def send_dps(self):
        self.wait(self._chips())

        def add(i, carry):
            at = self.rows(i * 16, 16)
            total = self.own[self.rows(self.p.chip * self.piece + i * 16, 16)].astype(f32)
            for j in range(self.p.chips - 1):
                total += self.r2[j, at].astype(f32)
            self.s[at] = total.astype(bf16)
            return carry

        lax.fori_loop(0, self.piece // 16, add, 0)
        self.start(self._dps())

    def send_dps_back(self):
        self.wait(self._dps())

        def add(i, carry):
            mine = self.rows((self.p.dp * self.last if self.split else 0) + i * 16, 16)
            total = self.s[mine].astype(f32)
            for j in range(self.p.dps - 1):
                total += self.r3[j, self.rows(i * 16, 16)].astype(f32)
            self.s2[mine] = total.astype(bf16)
            return carry

        lax.fori_loop(0, self.last // 16, add, 0)
        self.start(self._dps_back())

    def send_chips_back(self):
        self.wait(self._dps_back())
        self._put().start()
        self.start(self._chips_back())

    def send_cores_back(self):
        self._put().wait()
        self.wait(self._chips_back())
        self.start(self._cores_back())

    def finish(self):
        self.wait(self._cores_back())


def region_in_kernel(regional, gain, shift, w_qkv, bias, region_in, triple):
    vhat, _ = norm_stats(regional[...].astype(f32))
    normed = (vhat * gain[...] + shift[...]).astype(bf16)
    region_in[...] = normed
    triple[...] = (nn(normed, w_qkv[...]) + bias[...]).astype(bf16)


def patch_proj_kernel(patches, gain, shift, w_qkv, bias, triple):
    rows = patches.shape[0] * patches.shape[1]
    vhat, _ = norm_stats(patches[...].reshape(rows, D).astype(f32))
    normed = (vhat * gain[...] + shift[...]).astype(bf16)
    out = (nn(normed, w_qkv[...]) + bias[...]).astype(bf16)
    triple[...] = out.reshape(triple.shape)


def expand_group(x, heads):
    lane = lax.broadcasted_iota(jnp.int32, (1, x.shape[1]), 1) // HD
    return jnp.concatenate([jnp.where(lane == i, x, jnp.zeros_like(x)) for i in range(heads)], axis=0)


def fold_group(y, heads):
    rows = y.shape[0] // heads
    lane = lax.broadcasted_iota(jnp.int32, (1, y.shape[1]), 1) // HD
    total = y[(heads - 1) * rows :]
    for i in range(heads - 2, -1, -1):
        total = jnp.where(lane == i, y[i * rows : (i + 1) * rows], total)
    return total


def region_attn_kernel(
    triple, gathered, image_col, image_row, regional, gain, shift, w_qkv, bias, w_out, out_bias,
    probs, merged, region_mid, triple0,
):
    count = triple.shape[0]
    width = 8 * count
    for g in range(2):
        lanes = slice(256 * g, 256 * g + 256)
        queries = expand_group(triple[:, lanes], 8)
        scores = nt(gathered[:, lanes], queries)
        same = image_col[...] == image_row[:, g * width : (g + 1) * width]
        scores = jnp.where(same, scores * SCALING, MASKED_SCORE)
        top = jnp.max(scores, axis=0, keepdims=True)
        exps = jnp.exp2((scores - top) * LOG2E)
        low = (exps * (1.0 / col(exps))).astype(bf16)
        probs[g] = low
        merged[:, lanes] = fold_group(tn(low, gathered[:, D + 256 * g : D + 256 * g + 256]), 8).astype(bf16)
    mid = regional[...].astype(f32) + nn(merged[...], w_out[...]) + out_bias[...]
    region_mid[...] = mid
    vhat, _ = norm_stats(mid)
    normed = (vhat * gain[...] + shift[...]).astype(bf16)
    triple0[...] = (nn(normed, w_qkv[...]) + bias[...]).astype(bf16)


def expand(x):
    lane = lax.broadcasted_iota(jnp.int32, (1, 128), 1) // HD
    return jnp.concatenate([jnp.where(lane == i, x, jnp.zeros_like(x)) for i in range(4)], axis=0)


def query_side(rows, weights):
    lane = lax.broadcasted_iota(jnp.int32, (1, 128), 1) // HD
    out = tn(rows, weights)
    pairs = jnp.concatenate([out[0:64, 0:128], out[64:128, 128:256]], axis=0).T
    return jnp.where(lane % 2 == 0, pairs[0:64], pairs[64:128])


def load_triple(t, triple, triple0, patch):
    for b in range(12):
        lanes = slice(128 * b, 128 * b + 128)
        t[b, 0 : patch * WC] = triple[:, :, lanes].reshape(patch * WC, 128).astype(f32)
        t[b, patch * WC : (patch + 1) * WC] = triple0[:, lanes].astype(f32)
        t[b, (patch + 1) * WC :] = jnp.zeros(((TP - patch - 1) * WC, 128), f32)


def local_fwd_kernel(triple, triple0, merged, probs, t, m):
    patch = triple.shape[0]
    load_triple(t, triple, triple0, patch)
    row = lax.broadcasted_iota(jnp.int32, (TP, 1), 0)

    def one(w):
        for b in range(4):
            q = t[b, pl.ds(w, TP, stride=WC), :].astype(bf16)
            k = t[4 + b, pl.ds(w, TP, stride=WC), :].astype(bf16)
            v = t[8 + b, pl.ds(w, TP, stride=WC), :].astype(bf16)
            scores = nt(k, expand(q))
            scores = jnp.where(row <= patch, scores, MASKED_SCORE)
            top = jnp.max(scores, axis=0, keepdims=True)
            exps = jnp.exp2((scores - top) * (SCALING * LOG2E))
            low = (exps * (1.0 / col(exps))).astype(bf16)
            probs[w, :, 256 * b : 256 * b + 256] = low
            m[b, pl.ds(w, TP, stride=WC), :] = query_side(v, low)

    def body(i, carry):
        for u in range(4):
            one(i * 4 + u)
        return carry

    lax.fori_loop(0, WC // 4, body, 0)
    for b in range(4):
        merged[:, :, 128 * b : 128 * b + 128] = m[b, 0 : (patch + 1) * WC].astype(bf16).reshape(patch + 1, WC, 128)


def local_bwd_step(w, probs, t, d):
    at = pl.ds(w, TP, stride=WC)
    for b in range(4):
        q = t[b, at, :].astype(bf16)
        k = t[4 + b, at, :].astype(bf16)
        v = t[8 + b, at, :].astype(bf16)
        g = t[12 + b, at, :].astype(bf16)
        qx = expand(q)
        gx = expand(g)
        low = probs[w, :, 256 * b : 256 * b + 256]
        high = low.astype(f32)
        scaled = high * nt(v, gx)
        back = (scaled - high * col(scaled)).astype(bf16)
        d[4 + b, at, :] = nn(back, qx) * SCALING
        d[8 + b, at, :] = nn(low, gx)
        d[b, at, :] = query_side(k, back) * SCALING


def back_kernel(
    wins, dps,
    triple, triple0, probs, grad_merged,
    region_triple, gathered, probs_r, merged_r, region_mid, grad_middle0, gain, w_qkv, w_out, out_local,
    up_source, down_source,
    grad_triple, up_sum, down_sum, terms, grad_query, out_grad, sums, out_bias_part, grad_mid,
    t, d, d0, *streams,
):
    step = pl.program_id(0)
    place = Place(wins, dps)
    up = Stream(place, up_source, up_sum, streams[: Stream.PARTS])
    down = Stream(place, down_source, down_sum, streams[Stream.PARTS :])

    @pl.when(step == 0)
    def _():
        place.greet()
        up.load()
        down.load()

    patch = triple.shape[0]
    load_triple(t, triple, triple0, patch)
    rows = (patch + 1) * WC
    for b in range(4):
        t[12 + b, 0:rows] = grad_merged[:, :, 128 * b : 128 * b + 128].reshape(rows, 128).astype(f32)
        t[12 + b, rows:] = jnp.zeros((TP * WC - rows, 128), f32)

    hooks = {
        0: (place.greeted, up.send_cores, down.send_cores),
        1: (up.send_chips,),
        2: (down.send_chips,),
        5: (up.send_dps,),
        8: (up.send_dps_back, down.send_dps),
        11: (up.send_chips_back, down.send_dps_back),
    }

    def body(i, carry):
        for u in range(4):
            local_bwd_step(i * 4 + u, probs, t, d)
        for when, todo in hooks.items():

            @pl.when(step * (WC // 4) + i == when)
            def _(todo=todo):
                for act in todo:
                    act()

        return carry

    lax.fori_loop(0, WC // 4, body, 0)
    at = pl.ds(pl.multiple_of(step * WC, WC), WC)
    for b in range(12):
        lanes = slice(128 * b, 128 * b + 128)
        low = d[b, 0:rows].astype(bf16)
        grad_triple[:, :, lanes] = low.reshape(patch + 1, WC, 128)
        d0[at, lanes] = low[rows - WC :]

    @pl.when(step == pl.num_programs(0) - 1)
    def _():
        vhat, inverse = norm_stats(region_mid[...])
        mid = grad_middle0[0].astype(f32) + norm_back(vhat, inverse, gain[...], nt(d0[...], w_qkv[...]))
        grad_mid[...] = mid
        grad_attn = mid.astype(bf16)
        out_grad[...] = (out_local[...] + tn(merged_r[...], grad_attn)).astype(bf16)
        out_bias_part[...] = col(grad_attn.astype(f32))
        grad_merged_r = nt(grad_attn, w_out[...]).astype(bf16)
        for g in range(2):
            lanes = slice(256 * g, 256 * g + 256)
            value_lanes = slice(D + 256 * g, D + 256 * g + 256)
            qx = expand_group(region_triple[:, lanes], 8)
            gx = expand_group(grad_merged_r[:, lanes], 8)
            low = probs_r[g]
            high = low.astype(f32)
            scaled = high * nt(gathered[:, value_lanes], gx)
            back = (scaled - high * col(scaled)).astype(bf16)
            terms[:, lanes] = (nn(back, qx) * SCALING).astype(bf16)
            terms[:, value_lanes] = nn(low, gx).astype(bf16)
            grad_query[:, lanes] = (fold_group(tn(back, gathered[:, lanes]), 8) * SCALING).astype(bf16)
            if g == 0:
                down.send_chips_back()
        sums[:, :D] = col(grad_query[...].astype(f32))
        sums[:, D:] = col(terms[...].astype(f32))
        up.send_cores_back()
        down.send_cores_back()
        up.finish()
        down.finish()


def gelu_both(v):
    e = jnp.exp2(v * v * (-0.5 * LOG2E))
    cdf = 0.5 + 0.5 * lax.erf(v * (0.5**0.5))
    return v * cdf, cdf + v * e * 0.3989422804014327


def with_region(block, region, last):
    tokens, count, width = block.shape
    head = block[0 : tokens - 1].reshape((tokens - 1) * count, width)
    tail = jnp.where(last, region, block[tokens - 1])
    return jnp.concatenate([head, tail], axis=0)


def mlp_kernel(
    patches, region_mid, merged, patch_cot, region_cot, w_out, out_bias, gain, shift, w_up, up_bias, w_down, down_bias,
    patch_out, region_out, grad_middle, grad_merged, up_grad, down_grad_t, out_grad, vec512, up_bias_grad,
    up_acc, down_acc,
):
    step = pl.program_id(0)
    last = step == pl.num_programs(0) - 1
    tokens, count, _ = patches.shape
    rows = tokens * count

    @pl.when(step == 0)
    def _():
        up_acc[...] = jnp.zeros_like(up_acc)
        down_acc[...] = jnp.zeros_like(down_acc)
        out_grad[...] = jnp.zeros_like(out_grad)
        vec512[...] = jnp.zeros_like(vec512)
        up_bias_grad[...] = jnp.zeros_like(up_bias_grad)

    x = with_region(patches[...].astype(f32), region_mid[...], last)
    grad_result = with_region(patch_cot[...], region_cot[...], last)
    low_merged = merged[...].reshape(rows, D)
    middle = x + nn(low_merged, w_out[...]) + out_bias[...]
    vhat, inverse = norm_stats(middle)
    mlp_in = (vhat * gain[...] + shift[...]).astype(bf16)
    mlp_in_t = mlp_in.T
    grad_result_t = grad_result.T
    result = middle + down_bias[...]
    grad_in = jnp.zeros((rows, D), f32)
    for f in range(FF // 512):
        at = slice(512 * f, 512 * f + 512)
        hidden = nn(mlp_in, w_up[:, at]) + up_bias[:, at]
        active, slope = gelu_both(hidden)
        active = active.astype(bf16)
        grad_hidden = (nt(grad_result, w_down[at, :]) * slope).astype(bf16)
        result += nn(active, w_down[at, :])
        grad_in += nt(grad_hidden, w_up[:, at])
        up_acc[:, at] += nn(mlp_in_t, grad_hidden)
        down_acc[:, at] += nn(grad_result_t, active)
        up_bias_grad[:, at] += col(grad_hidden.astype(f32))
    shown = result.astype(bf16)
    patch_out[...] = shown.reshape(tokens, count, D)
    region_out[...] = shown[rows - count :]
    gm = grad_result.astype(f32) + norm_back(vhat, inverse, gain[...], grad_in)
    low_gm = gm.astype(bf16)
    grad_middle[...] = low_gm.reshape(tokens, count, D)
    out_grad[...] += nn(low_merged.T, low_gm)
    grad_merged[...] = nt(low_gm, w_out[...]).astype(bf16).reshape(tokens, count, D)
    vec512[0:1] += col(grad_in * vhat)
    vec512[1:2] += col(grad_in)
    vec512[2:3] += col(low_gm.astype(f32))
    vec512[3:4] += col(grad_result.astype(f32))

    @pl.when(last)
    def _():
        up_grad[...] = up_acc[...].astype(bf16)
        down_grad_t[...] = down_acc[...].astype(bf16)


def tail_kernel(
    wins, dps,
    patches, grad_triple, grad_middle, region_mid, gain, shift, w_qkv, region_in, region_in_all, terms, grad_query,
    regional, grad_mid, vec_mlp, up_bias_grad, sums, out_bias_part, out_source,
    patch_grad, region_grad, small_sum, out_sum, query_sum, key_sum, value_sum,
    qkv_acc, qkv_low, triple_sums, vec, pieces, piece_sem, pack, near, near_sem, total, far, far_sem, *streams,
):
    step = pl.program_id(0)
    half = pl.num_programs(0) // 2
    tokens, count, _ = patches.shape
    rows = tokens * count
    place = Place(wins, dps)
    parts = [streams[Stream.PARTS * b : Stream.PARTS * (b + 1)] for b in range(4)]
    out = Stream(place, out_source, out_sum, parts[0])
    blocks = [Stream(place, qkv_low.at[b], (query_sum, key_sum, value_sum)[b], parts[b + 1]) for b in range(3)]

    def to_owners():
        copies = []
        for j in range(1, wins):
            win = lax.rem(place.win + j, wins)
            copies.append(pltpu.make_async_remote_copy(
                src_ref=terms.at[pl.ds(pl.multiple_of(win * count, 16), count)], dst_ref=pieces.at[j - 1],
                send_sem=piece_sem.at[2 * j - 2], recv_sem=piece_sem.at[2 * j - 1],
                device_id={"win": win}, device_id_type=MESH,
            ))
        return copies

    def to_near():
        return [pltpu.make_async_remote_copy(
            src_ref=pack, dst_ref=near.at[j - 1], send_sem=near_sem.at[2 * j - 2], recv_sem=near_sem.at[2 * j - 1],
            device_id={"win": lax.rem(place.win + j, wins)}, device_id_type=MESH,
        ) for j in range(1, wins)]

    def to_far():
        return [pltpu.make_async_remote_copy(
            src_ref=total, dst_ref=far.at[j - 1], send_sem=far_sem.at[2 * j - 2], recv_sem=far_sem.at[2 * j - 1],
            device_id=place.at_dp(j)[1], device_id_type=MESH,
        ) for j in range(1, dps)]

    def begin():
        place.greeted(all_wins=True)
        for c in to_owners():
            c.start()
        out.load()
        out.send_cores()

    def region_end():
        for c in to_owners():
            c.wait()
        key_value = terms[pl.ds(pl.multiple_of(place.win * count, 16), count)].astype(f32)
        for j in range(wins - 1):
            key_value += pieces[j].astype(f32)
        vhat, inverse = norm_stats(regional[...].astype(f32))
        grad_in = nt(grad_query[...], w_qkv[:, :D]) + nt(key_value.astype(bf16), w_qkv[:, D:])
        region_grad[...] = (grad_mid[...] + norm_back(vhat, inverse, gain[...], grad_in)).astype(bf16)
        vec[0:1] += col(grad_in * vhat)
        vec[1:2] += col(grad_in)

    def qkv_end():
        qkv_low[0] = (qkv_acc[:, :D] + tn(region_in[...], grad_query[...])).astype(bf16)
        for b in range(1, 3):
            lanes = slice(D * (b - 1), D * b)
            qkv_low[b] = (qkv_acc[:, D * b : D * (b + 1)] + tn(region_in_all[...], terms[:, lanes])).astype(bf16)
        for s in blocks:
            s.load()
            s.send_cores()

    def small_begin():
        pack[0:2] = vec[0:2]
        pack[2:3] = triple_sums[:, :D] + sums[:, :D]
        pack[3:4] = triple_sums[:, 2 * D :] + sums[:, 2 * D :]
        pack[4:5] = vec_mlp[2:3] + out_bias_part[...]
        pack[5:7] = vec_mlp[0:2]
        pack[7:8] = vec_mlp[3:4]
        for b in range(4):
            pack[8 + b : 9 + b] = up_bias_grad[:, D * b : D * (b + 1)]
        pack[12:16] = jnp.zeros((4, D), f32)
        for c in to_near():
            c.start()

    def small_middle():
        for c in to_near():
            c.wait()
        part = pack[...]
        for j in range(wins - 1):
            part += near[j]
        total[...] = part
        for c in to_far():
            c.start()

    def small_end():
        for c in to_far():
            c.wait()
        part = total[...]
        for j in range(dps - 1):
            part += far[j]
        small_sum[...] = part

    @pl.when(step == 0)
    def _():
        place.greet(all_wins=True)
        qkv_acc[...] = jnp.zeros_like(qkv_acc)
        triple_sums[...] = jnp.zeros_like(triple_sums)
        vec[...] = jnp.zeros_like(vec)

    x = with_region(patches[...].astype(f32), region_mid[...], lax.rem(step, half) == half - 1)
    vhat, inverse = norm_stats(x)
    low = grad_triple[...].reshape(rows, 3 * D)

    @pl.when(step < half)
    def _():
        local_in = (vhat * gain[...] + shift[...]).astype(bf16)
        qkv_acc[...] += nn(local_in.T, low)
        triple_sums[...] += col(low.astype(f32))

    @pl.when(step >= half)
    def _():
        grad_in = nt(low, w_qkv[...])
        vec[0:1] += col(grad_in * vhat)
        vec[1:2] += col(grad_in)
        total_rows = grad_middle[...].reshape(rows, D).astype(f32) + norm_back(vhat, inverse, gain[...], grad_in)
        patch_grad[...] = total_rows.astype(bf16).reshape(tokens, count, D)

    query, key, value = blocks
    hooks = {
        0: (begin,),
        1: (out.send_chips,),
        2: (region_end,),
        3: (out.send_dps,),
        half - 1: (qkv_end, out.send_dps_back),
        half: (query.send_chips, key.send_chips),
        half + 1: (value.send_chips, out.send_chips_back),
        half + 2: (query.send_dps, out.send_cores_back),
        half + 3: (key.send_dps,),
        half + 4: (
            small_begin, out.finish, value.send_dps, query.send_dps_back, small_middle, key.send_dps_back,
            value.send_dps_back, query.send_chips_back, small_end, key.send_chips_back, value.send_chips_back,
            query.send_cores_back, key.send_cores_back, value.send_cores_back, query.finish, key.finish, value.finish,
        ),
    }
    for when, todo in hooks.items():

        @pl.when(step == when)
        def _(todo=todo):
            for act in todo:
                act()


def shards(
    wins, dps,
    patches, regional, window_image, in_gain, in_shift, w_qkv, qkv_bias, w_out, out_bias,
    mlp_gain, mlp_shift, w_up, up_bias, w_down, down_bias, patch_cot, region_cot,
):
    _, count, patch, _ = patches.shape
    group = window_image.shape[1]
    row = lambda v: v.astype(f32).reshape(1, -1)
    gain1, shift1, gain2, shift2 = row(in_gain), row(in_shift), row(mlp_gain), row(mlp_shift)
    bias_row = row(jnp.concatenate([qkv_bias[0], jnp.zeros_like(qkv_bias[0]), qkv_bias[1]]))
    out_row, up_row, down_row = row(out_bias), row(up_bias), row(down_bias)
    images = window_image[0]
    own = lax.dynamic_slice_in_dim(images, lax.axis_index("win") * count, count)
    image_row = jnp.tile(own, HEADS)[None]
    image_col = images[:, None]
    x = patches[0].transpose(1, 0, 2)
    cot = patch_cot[0].transpose(1, 0, 2)
    reg = regional[0]
    rcot = region_cot[0]

    region_in, region_triple = call(
        region_in_kernel, (1,), [whole(a) for a in (reg, gain1, shift1, w_qkv, bias_row)],
        [whole_out((count, D), bf16), whole_out((count, 3 * D), bf16)], name="region_in",
    )
    packed = jnp.concatenate([region_triple[:, D:], region_in], axis=1)
    gathered = lax.all_gather(packed, "win", axis=0, tiled=True)
    block = lambda a, n: (a, (n,) + a.shape[1:], lambda i: (i, 0, 0))
    block_out = lambda shape, n, dtype=bf16: ((shape, dtype), (n,) + shape[1:], lambda i: (i, 0, 0))
    (triple,) = call(
        patch_proj_kernel, (pl.cdiv(patch, 7),),
        [block(x, 7)] + [whole(a) for a in (gain1, shift1, w_qkv, bias_row)],
        [block_out((patch, count, 3 * D), 7)], name="patch_proj",
    )
    probs_r, merged_r, region_mid, triple0 = call(
        region_attn_kernel, (1,),
        [whole(a) for a in (region_triple, gathered, image_col, image_row, reg, gain1, shift1, w_qkv, bias_row, w_out, out_row)],
        [whole_out((2, group, 8 * count), bf16), whole_out((count, D), bf16),
         whole_out((count, D), f32), whole_out((count, 3 * D), bf16)], name="region_attn",
    )
    steps = (count // WC,)
    mid = lambda a: (a, (a.shape[0], WC, a.shape[2]), lambda i: (0, i, 0))
    mid_out = lambda shape, dtype=bf16: ((shape, dtype), (shape[0], WC, shape[2]), lambda i: (0, i, 0))
    tail = lambda a: (a, (WC, a.shape[1]), lambda i: (i, 0))
    merged, probs = call(
        local_fwd_kernel, steps, [mid(triple), tail(triple0)],
        [mid_out((patch + 1, count, D)), ((((count, TP, HEADS * TP)), bf16), (WC, TP, HEADS * TP), lambda i: (i, 0, 0))],
        [pltpu.VMEM((12, TP * WC, 128), f32), pltpu.VMEM((4, TP * WC, 128), f32)], name="local_fwd",
    )
    n = 10
    rows_grid = ((patch + 1) // n,)
    patch_out, region_out, grad_middle, grad_merged, up_grad, down_grad_t, out_local, vec_mlp, up_bias_grad = call(
        mlp_kernel, rows_grid,
        [block(x, n), whole(region_mid), block(merged, n), block(cot, n)]
        + [whole(a) for a in (rcot, w_out, out_row, gain2, shift2, w_up, up_row, w_down, down_row)],
        [block_out((patch, count, D), n), whole_out((count, D), bf16),
         block_out((patch + 1, count, D), n), block_out((patch + 1, count, D), n),
         whole_out((D, FF), bf16), whole_out((D, FF), bf16), whole_out((D, D), f32),
         whole_out((8, D), f32), whole_out((1, FF), f32)],
        [pltpu.VMEM((D, FF), f32), pltpu.VMEM((D, FF), f32)], name="mlp",
    )
    const = lambda *arrays: [whole(a) for a in arrays]
    grad_triple, up_sum, down_sum, terms, grad_query, out_grad, sums, out_bias_part, grad_mid = call(
        functools.partial(back_kernel, wins, dps), steps,
        [mid(triple), tail(triple0), (probs, (WC, TP, HEADS * TP), lambda i: (i, 0, 0)), mid(grad_merged)]
        + const(region_triple, gathered, probs_r, merged_r, region_mid)
        + [(grad_middle, (1, count, D), lambda i: (patch, 0, 0))]
        + const(gain1, w_qkv, w_out, out_local) + [left(up_grad), left(down_grad_t)],
        [mid_out((patch + 1, count, 3 * D)), left_out((D, FF), bf16), left_out((D, FF), bf16),
         whole_out((group, 2 * D), bf16), whole_out((count, D), bf16), whole_out((D, D), bf16),
         whole_out((1, 3 * D), f32), whole_out((1, D), f32), whole_out((count, D), f32)],
        [pltpu.VMEM((16, TP * WC, 128), f32), pltpu.VMEM((12, TP * WC, 128), f32), pltpu.VMEM((count, 3 * D), bf16)]
        + stream_scratch(wins, dps, FF) * 2,
        name="back", collective_id=0,
    )
    half = rows_grid[0]
    again = lambda a: (a, (n,) + a.shape[1:], lambda i: (lax.rem(i, half), 0, 0))
    second = lambda a: (a, (n,) + a.shape[1:], lambda i: (lax.max(i - half, 0), 0, 0))
    patch_grad, region_grad, small, out_sum, query_sum, key_sum, value_sum = call(
        functools.partial(tail_kernel, wins, dps), (2 * half,),
        [again(x), again(grad_triple), second(grad_middle)]
        + const(region_mid, gain1, shift1, w_qkv, region_in)
        + [(gathered, (group, D), lambda i: (0, 2))]
        + const(terms, grad_query, reg, grad_mid, vec_mlp, up_bias_grad, sums, out_bias_part) + [left(out_grad)],
        [(((patch, count, D), bf16), (n, count, D), lambda i: (lax.max(i - half, 0), 0, 0)),
         whole_out((count, D), bf16), whole_out((16, D), f32)] + [left_out((D, D), bf16)] * 4,
        [pltpu.VMEM((D, 3 * D), f32), pltpu.VMEM((3, D, D), bf16), pltpu.VMEM((1, 3 * D), f32), pltpu.VMEM((8, D), f32),
         pltpu.VMEM((wins - 1, count, 2 * D), bf16), pltpu.SemaphoreType.DMA((2 * wins,)),
         pltpu.VMEM((16, D), f32), pltpu.VMEM((wins - 1, 16, D), f32), pltpu.SemaphoreType.DMA((2 * wins,)),
         pltpu.VMEM((16, D), f32), pltpu.VMEM((max(dps - 1, 1), 16, D), f32), pltpu.SemaphoreType.DMA((2 * dps,))]
        + stream_scratch(wins, dps, D) * 4,
        name="tail", collective_id=1,
    )
    return (
        patch_out.transpose(1, 0, 2)[None],
        region_out[None],
        patch_grad.transpose(1, 0, 2)[None],
        region_grad[None],
        small[0],
        small[1],
        jnp.concatenate([query_sum, key_sum, value_sum], axis=1).astype(f32),
        small[2:4],
        out_sum.astype(f32),
        small[4],
        small[5],
        small[6],
        up_sum.astype(f32),
        small[8:12].reshape(-1),
        down_sum.T.astype(f32),
        small[7],
    )


def solution(mesh):
    wide = P("dp", "win", None, None)
    narrow = P("dp", "win", None)
    in_specs = (wide, narrow, P("dp", None)) + (P(),) * 12 + (wide, narrow)
    out_specs = (wide, narrow, wide, narrow) + (P(),) * 12
    return jax.shard_map(functools.partial(shards, mesh.shape["win"], mesh.shape["dp"]), mesh=mesh, in_specs=in_specs, out_specs=out_specs, check_vma=False)
```

```python
import functools

import jax
import jax.numpy as jnp
from jax import lax
from jax.experimental import pallas as pl
from jax.experimental.pallas import tpu as pltpu
from jax.sharding import PartitionSpec as P

D = 512
HEADS = 16
HD = 32
FF = 2048
EPSILON = 1e-06
MASKED_SCORE = -1e30
SCALING = HD ** (-0.5)
LOG2E = 1.4426950408889634
TP = 64
WC = 16
f32 = jnp.float32
bf16 = jnp.bfloat16
VMEM_LIMIT = 60 * 2**20
MESH = pl.DeviceIdType.MESH


def nn(a, b):
    return lax.dot_general(a, b, (((1,), (0,)), ((), ())), preferred_element_type=f32)


def nt(a, b):
    return lax.dot_general(a, b, (((1,), (1,)), ((), ())), preferred_element_type=f32)


def tn(a, b):
    return lax.dot_general(a, b, (((0,), (0,)), ((), ())), preferred_element_type=f32)


def call(body, grid, ins, outs, scratch=(), name=None, collective_id=None):
    def spec(block, index):
        if block is None:
            return pl.BlockSpec(memory_space=pl.ANY)
        if index is None:
            return pl.BlockSpec(block, lambda *_: (0,) * len(block), pipeline_mode=pl.Buffered(1))
        return pl.BlockSpec(block, index)

    return pl.pallas_call(
        body,
        grid=grid,
        in_specs=[spec(b, i) for _, b, i in ins],
        out_specs=[spec(b, i) for _, b, i in outs],
        out_shape=[jax.ShapeDtypeStruct(s, d) for (s, d), _, _ in outs],
        scratch_shapes=list(scratch),
        compiler_params=pltpu.CompilerParams(
            vmem_limit_bytes=VMEM_LIMIT, collective_id=collective_id, has_side_effects=collective_id is not None
        ),
        name=name,
    )(*[a for a, _, _ in ins])


def whole(a):
    return (a, a.shape, None)


def whole_out(shape, dtype):
    return ((shape, dtype), shape, lambda *_: (0,) * len(shape))


def left(a):
    return (a, None, None)


def left_out(shape, dtype):
    return ((shape, dtype), None, None)


def norm_stats(rows):
    average = jnp.mean(rows, axis=-1, keepdims=True)
    centred = rows - average
    spread = jnp.mean(centred * centred, axis=-1, keepdims=True)
    inverse = lax.rsqrt(spread + EPSILON)
    return centred * inverse, inverse


def norm_back(vhat, inverse, gain, grad_out):
    scaled = grad_out * gain
    first = jnp.mean(scaled, axis=-1, keepdims=True)
    second = jnp.mean(scaled * vhat, axis=-1, keepdims=True)
    return inverse * (scaled - first - vhat * second)


def col(x):
    return jnp.sum(x, axis=0, keepdims=True)


class Place:
    def __init__(self, wins, dps):
        self.wins, self.dps = wins, dps
        self.win = lax.axis_index("win")
        self.dp = lax.axis_index("dp")
        self.core = lax.rem(self.win, 2)
        self.chip = self.win // 2
        self.chips = wins // 2
        self.square = self.chips == 4
        self.a = self.chip // 2
        self.b = lax.rem(self.chip, 2)

    def other_core(self):
        return {"win": self.chip * 2 + 1 - self.core}

    def other_a(self):
        return {"win": ((1 - self.a) * 2 + self.b) * 2 + self.core}

    def other_b(self):
        return {"win": (self.a * 2 + 1 - self.b) * 2 + self.core}

    def at_chip(self, j):
        chip = lax.rem(self.chip + j, self.chips)
        return chip, {"win": chip * 2 + self.core}

    def at_dp(self, j):
        dp = lax.rem(self.dp + j, self.dps)
        return dp, {"dp": dp}

    def near(self, all_wins):
        if all_wins:
            return [{"win": lax.rem(self.win + j, self.wins)} for j in range(1, self.wins)]
        if self.square:
            return [self.other_core(), self.other_a(), self.other_b()]
        return [self.other_core()] + [self.at_chip(j)[1] for j in range(1, self.chips)]

    def partners(self, all_wins, along):
        return self.near(all_wins) + [self.at_dp(j)[1] for j in range(1, self.dps if along else 1)]

    def greet(self, all_wins=False, along=True):
        barrier = pltpu.get_barrier_semaphore()
        for to in self.partners(all_wins, along):
            pl.semaphore_signal(barrier, inc=1, device_id=to, device_id_type=MESH)

    def greeted(self, all_wins=False, along=True):
        pl.semaphore_wait(pltpu.get_barrier_semaphore(), len(self.partners(all_wins, along)))


def rows_of(wins, dps):
    piece = D // wins
    return piece, piece // dps if piece % (16 * dps) == 0 else piece


def stream_shape(wins, columns):
    return (2, wins // 2, D // wins, columns)


def stream_scratch(wins, dps, columns):
    piece, last = rows_of(wins, dps)
    chips = wins // 2
    landing = (4, 2, piece, columns // 2) if chips == 4 else (max(chips - 1, 1), piece, columns)
    return [
        pltpu.VMEM((chips, piece, columns), bf16),
        pltpu.VMEM((chips, piece, columns), bf16),
        pltpu.VMEM(landing, bf16),
        pltpu.VMEM((piece, columns), bf16),
        pltpu.VMEM((max(dps - 1, 1), last, columns), bf16),
        pltpu.VMEM((piece, columns), bf16),
        pltpu.SemaphoreType.DMA((20 + 4 * chips + 4 * dps,)),
    ]


class Stream:
    PARTS = 7

    def __init__(self, place, source, final, refs):
        self.p = place
        self.source, self.final = source, final
        self.own, self.r1, self.r2, self.s, self.r3, self.s2, self.sem = refs
        self.piece, self.last = rows_of(place.wins, place.dps)
        self.split = self.last != self.piece
        columns = self.own.shape[2]
        self.left, self.right = pl.ds(0, columns // 2), pl.ds(columns // 2, columns // 2)

    def rows(self, start, size):
        return pl.ds(pl.multiple_of(start, 16), size)

    def remote(self, src, dst, to, k):
        return pltpu.make_async_remote_copy(
            src_ref=src, dst_ref=dst, send_sem=self.sem.at[2 * k], recv_sem=self.sem.at[2 * k + 1],
            device_id=to, device_id_type=MESH,
        )

    def _own(self):
        return pltpu.make_async_copy(self.source.at[self.p.core], self.own, self.sem.at[0])

    def _put(self):
        return pltpu.make_async_copy(self.r1, self.final.at[self.p.core], self.sem.at[1])

    def _cores(self):
        return [self.remote(self.source.at[1 - self.p.core], self.r1, self.p.other_core(), 1)]

    def _cores_back(self):
        return [self.remote(self.r1, self.final.at[self.p.core], self.p.other_core(), 2)]

    def _chips_left(self, k):
        p = self.p
        if k == 0:
            return [self.remote(self.own.at[c * 2 + 1 - p.b, :, self.left], self.r2.at[0, c], p.other_b(), 3 + c) for c in range(2)]
        return [self.remote(self.own.at[(1 - p.a) * 2 + p.b, :, self.left], self.r2.at[2, 0], p.other_a(), 5)]

    def _chips_right(self, k):
        p = self.p
        if k == 0:
            return [self.remote(self.own.at[(1 - p.a) * 2 + c, :, self.right], self.r2.at[1, c], p.other_a(), 6 + c) for c in range(2)]
        return [self.remote(self.own.at[p.a * 2 + 1 - p.b, :, self.right], self.r2.at[3, 0], p.other_b(), 8)]

    def _back_left(self, k):
        p = self.p
        mine = self.r1
        if k == 0:
            return [self.remote(self.s2.at[:, self.left], mine.at[p.chip, :, self.left], p.other_a(), 9)]
        rows = [mine.at[c * 2 + p.b, :, self.left] for c in range(2)]
        return [self.remote(rows[c], rows[c], p.other_b(), 10 + c) for c in range(2)]

    def _back_right(self, k):
        p = self.p
        mine = self.r1
        if k == 0:
            return [self.remote(self.s2.at[:, self.right], mine.at[p.chip, :, self.right], p.other_b(), 12)]
        rows = [mine.at[p.a * 2 + c, :, self.right] for c in range(2)]
        return [self.remote(rows[c], rows[c], p.other_a(), 13 + c) for c in range(2)]

    def _chips(self):
        out = []
        for j in range(1, self.p.chips):
            chip, to = self.p.at_chip(j)
            out.append(self.remote(self.own.at[chip], self.r2.at[j - 1], to, 2 + j))
        return out

    def _chips_back(self):
        out = []
        for j in range(1, self.p.chips):
            mine = self.r1.at[self.p.chip]
            out.append(self.remote(self.s2, mine, self.p.at_chip(j)[1], 2 + self.p.chips + j))
        return out

    def _dps(self):
        out = []
        for j in range(1, self.p.dps):
            dp, to = self.p.at_dp(j)
            src = self.s.at[self.rows(dp * self.last, self.last)] if self.split else self.s
            out.append(self.remote(src, self.r3.at[j - 1], to, 8 + 2 * self.p.chips + j))
        return out

    def _dps_back(self):
        out = []
        if self.split:
            for j in range(1, self.p.dps):
                mine = self.s2.at[self.rows(self.p.dp * self.last, self.last)]
                out.append(self.remote(mine, mine, self.p.at_dp(j)[1], 8 + 2 * self.p.chips + self.p.dps + j))
        return out

    def start(self, copies):
        for c in copies:
            c.start()

    def wait(self, copies):
        for c in copies:
            c.wait()

    def load(self):
        self._own().start()

    def send_cores(self):
        self.start(self._cores())

    def send_chips(self):
        self._own().wait()
        self.wait(self._cores())

        def add(i, carry):
            self.own[i] = (self.own[i].astype(f32) + self.r1[i].astype(f32)).astype(bf16)
            return carry

        lax.fori_loop(0, self.p.chips, add, 0)
        if self.p.square:
            self.start(self._chips_left(0))
            self.start(self._chips_right(0))
        else:
            self.start(self._chips())

    def add_square(self, chip, lanes, slot, c):
        self.own[chip, :, lanes] = (self.own[chip, :, lanes].astype(f32) + self.r2[slot, c].astype(f32)).astype(bf16)

    def send_chips_again(self):
        p = self.p
        if p.square:
            self.wait(self._chips_left(0))
            for c in range(2):
                self.add_square(c * 2 + p.b, self.left, 0, c)
            self.start(self._chips_left(1))
            self.wait(self._chips_right(0))
            for c in range(2):
                self.add_square(p.a * 2 + c, self.right, 1, c)
            self.start(self._chips_right(1))

    def send_dps(self):
        p = self.p
        if p.square:
            for lanes, slot, copies in ((self.left, 2, self._chips_left(1)), (self.right, 3, self._chips_right(1))):
                self.wait(copies)
                self.s[:, lanes] = (self.own[p.chip, :, lanes].astype(f32) + self.r2[slot, 0].astype(f32)).astype(bf16)
        else:
            self.wait(self._chips())
            total = self.own[p.chip].astype(f32)
            for j in range(p.chips - 1):
                total += self.r2[j].astype(f32)
            self.s[...] = total.astype(bf16)
        self.start(self._dps())

    def send_dps_back(self):
        self.wait(self._dps())
        mine = self.rows(self.p.dp * self.last if self.split else 0, self.last)
        total = self.s[mine].astype(f32)
        for j in range(self.p.dps - 1):
            total += self.r3[j].astype(f32)
        self.s2[mine] = total.astype(bf16)
        self.start(self._dps_back())

    def send_chips_back(self):
        self.wait(self._dps_back())
        self.r1[self.p.chip] = self.s2[...]
        if self.p.square:
            self.start(self._back_left(0))
            self.start(self._back_right(0))
        else:
            self.start(self._chips_back())

    def send_chips_back_again(self):
        if self.p.square:
            self.wait(self._back_left(0))
            self.start(self._back_left(1))
            self.wait(self._back_right(0))
            self.start(self._back_right(1))
        else:
            self.wait(self._chips_back())

    def send_cores_back(self):
        if self.p.square:
            self.wait(self._back_left(1))
            self.wait(self._back_right(1))
        self.start(self._cores_back())
        self._put().start()

    def finish(self):
        self.wait(self._cores_back())
        self._put().wait()

    STEPS = (
        "send_cores", "send_chips", "send_chips_again", "send_dps", "send_dps_back",
        "send_chips_back", "send_chips_back_again", "send_cores_back", "finish",
    )

    def step(self, k):
        if 0 <= k < len(self.STEPS):
            getattr(self, self.STEPS[k])()


def expand_group(x, heads):
    lane = lax.broadcasted_iota(jnp.int32, (1, x.shape[1]), 1) // HD
    return jnp.concatenate([jnp.where(lane == i, x, jnp.zeros_like(x)) for i in range(heads)], axis=0)


def fold_group(y, heads):
    rows = y.shape[0] // heads
    lane = lax.broadcasted_iota(jnp.int32, (1, y.shape[1]), 1) // HD
    total = y[(heads - 1) * rows :]
    for i in range(heads - 2, -1, -1):
        total = jnp.where(lane == i, y[i * rows : (i + 1) * rows], total)
    return total


GAIN1, SHIFT1, GAIN2, SHIFT2, OUT_BIAS, DOWN_BIAS, QUERY_BIAS, KEY_BIAS, VALUE_BIAS, UP_BIAS = range(10)


def row(vecs, at):
    return vecs[at : at + 1]


def normed_low(vhat, vecs, gain, shift):
    return (vhat * row(vecs, gain) + row(vecs, shift)).astype(bf16)


def front_kernel(
    wins, dps,
    patches, regional, images, in_gain, in_shift, w_qkv, qkv_bias, w_out, out_bias, mlp_gain, mlp_shift, up_bias, down_bias,
    triple, vecs, region_triple, gathered_out, probs, merged, region_mid, triple0,
    gathered, packed, image_col, sem,
):
    step = pl.program_id(0)
    place = Place(wins, dps)
    count = regional.shape[0]
    group = gathered.shape[0]
    mine = pl.ds(pl.multiple_of(place.win * count, 16), count)

    def project(normed):
        out = nn(normed, w_qkv[...])
        return jnp.concatenate(
            [out[:, :D] + row(vecs, QUERY_BIAS), out[:, D : 2 * D], out[:, 2 * D :] + row(vecs, VALUE_BIAS)], axis=1
        ).astype(bf16)

    def sends():
        copies = []
        for j in range(1, wins):
            copies.append(pltpu.make_async_remote_copy(
                src_ref=packed, dst_ref=gathered.at[mine], send_sem=sem.at[2 * j - 2], recv_sem=sem.at[2 * j - 1],
                device_id={"win": lax.rem(place.win + j, wins)}, device_id_type=MESH,
            ))
        return copies

    @pl.when(step == 0)
    def _():
        place.greet(all_wins=True, along=False)
        for at, v in (
            (GAIN1, in_gain), (SHIFT1, in_shift), (GAIN2, mlp_gain), (SHIFT2, mlp_shift), (OUT_BIAS, out_bias), (DOWN_BIAS, down_bias),
        ):
            vecs[at : at + 1] = v[...].astype(f32).reshape(1, D)
        vecs[QUERY_BIAS : QUERY_BIAS + 1] = qkv_bias[0:1].astype(f32)
        vecs[KEY_BIAS : KEY_BIAS + 1] = jnp.zeros((1, D), f32)
        vecs[VALUE_BIAS : VALUE_BIAS + 1] = qkv_bias[1:2].astype(f32)
        up = up_bias[...].astype(f32).reshape(1, FF)
        for b in range(FF // D):
            vecs[UP_BIAS + b : UP_BIAS + b + 1] = up[:, D * b : D * (b + 1)]
        vecs[UP_BIAS + FF // D : 16] = jnp.zeros((16 - UP_BIAS - FF // D, D), f32)
        vhat, _ = norm_stats(regional[...].astype(f32))
        normed = normed_low(vhat, vecs, GAIN1, SHIFT1)
        own = project(normed)
        region_triple[...] = own
        packed[:, : 2 * D] = own[:, D:]
        packed[:, 2 * D :] = normed
        gathered[mine] = packed[...]
        place.greeted(all_wins=True, along=False)
        for c in sends():
            c.start()
        ids = images[...].astype(f32)
        image_col[...] = jnp.broadcast_to(ids, (128, group)).T

    rows = patches.shape[0] * count
    vhat, _ = norm_stats(patches[...].reshape(rows, D).astype(f32))
    triple[...] = project(normed_low(vhat, vecs, GAIN1, SHIFT1)).reshape(triple.shape)

    @pl.when(step == pl.num_programs(0) - 1)
    def _():
        for c in sends():
            c.wait()
        gathered_out[...] = gathered[...]
        own_ids = image_col[mine]
        own_row = jnp.concatenate([own_ids] * 8, axis=0).T[0:1]
        same = image_col[:, 0:1] == own_row
        for g in range(2):
            lanes = slice(256 * g, 256 * g + 256)
            scores = nt(gathered[:, lanes], expand_group(region_triple[:, lanes], 8))
            scores = jnp.where(same, scores * SCALING, MASKED_SCORE)
            top = jnp.max(scores, axis=0, keepdims=True)
            exps = jnp.exp2((scores - top) * LOG2E)
            low = (exps * (1.0 / col(exps))).astype(bf16)
            probs[g] = low
            merged[:, lanes] = fold_group(tn(low, gathered[:, D + 256 * g : D + 256 * g + 256]), 8).astype(bf16)
        mid = regional[...].astype(f32) + nn(merged[...], w_out[...]) + row(vecs, OUT_BIAS)
        region_mid[...] = mid
        vhat_mid, _ = norm_stats(mid)
        triple0[...] = project(normed_low(vhat_mid, vecs, GAIN1, SHIFT1))


def expand(x):
    lane = lax.broadcasted_iota(jnp.int32, (1, 128), 1) // HD
    return jnp.concatenate([jnp.where(lane == i, x, jnp.zeros_like(x)) for i in range(4)], axis=0)


def query_side(rows, weights):
    lane = lax.broadcasted_iota(jnp.int32, (1, 128), 1) // HD
    out = tn(rows, weights)
    pairs = jnp.concatenate([out[0:64, 0:128], out[64:128, 128:256]], axis=0).T
    return jnp.where(lane % 2 == 0, pairs[0:64], pairs[64:128])


def load_triple(t, triple, triple0, patch):
    for b in range(12):
        lanes = slice(128 * b, 128 * b + 128)
        t[b, 0 : patch * WC] = triple[:, :, lanes].reshape(patch * WC, 128).astype(f32)
        t[b, patch * WC : (patch + 1) * WC] = triple0[:, lanes].astype(f32)
        t[b, (patch + 1) * WC :] = jnp.zeros(((TP - patch - 1) * WC, 128), f32)


def local_fwd_kernel(triple, triple0, merged, probs, t, m):
    patch = triple.shape[0]
    load_triple(t, triple, triple0, patch)
    row = lax.broadcasted_iota(jnp.int32, (TP, 1), 0)

    def one(w):
        for b in range(4):
            q = t[b, pl.ds(w, TP, stride=WC), :].astype(bf16)
            k = t[4 + b, pl.ds(w, TP, stride=WC), :].astype(bf16)
            v = t[8 + b, pl.ds(w, TP, stride=WC), :].astype(bf16)
            scores = nt(k, expand(q))
            scores = jnp.where(row <= patch, scores, MASKED_SCORE)
            top = jnp.max(scores, axis=0, keepdims=True)
            exps = jnp.exp2((scores - top) * (SCALING * LOG2E))
            low = (exps * (1.0 / col(exps))).astype(bf16)
            probs[w, :, 256 * b : 256 * b + 256] = low
            m[b, pl.ds(w, TP, stride=WC), :] = query_side(v, low)

    def body(i, carry):
        for u in range(4):
            one(i * 4 + u)
        return carry

    lax.fori_loop(0, WC // 4, body, 0)
    for b in range(4):
        merged[:, :, 128 * b : 128 * b + 128] = m[b, 0 : (patch + 1) * WC].astype(bf16).reshape(patch + 1, WC, 128)


def local_bwd_step(w, probs, t, d):
    at = pl.ds(w, TP, stride=WC)
    for b in range(4):
        q = t[b, at, :].astype(bf16)
        k = t[4 + b, at, :].astype(bf16)
        v = t[8 + b, at, :].astype(bf16)
        g = t[12 + b, at, :].astype(bf16)
        qx = expand(q)
        gx = expand(g)
        low = probs[w, :, 256 * b : 256 * b + 256]
        high = low.astype(f32)
        scaled = high * nt(v, gx)
        back = (scaled - high * col(scaled)).astype(bf16)
        d[4 + b, at, :] = nn(back, qx) * SCALING
        d[8 + b, at, :] = nn(low, gx)
        d[b, at, :] = query_side(k, back) * SCALING


def back_kernel(
    wins, dps,
    triple, triple0, probs, grad_merged,
    region_triple, gathered, probs_r, merged_r, region_mid, grad_middle0, vecs, w_qkv, w_out, out_local,
    up_source, down_source,
    grad_triple, up_sum, down_sum, terms, grad_query, out_grad, sums, out_bias_part, grad_mid,
    t, d, d0, *streams,
):
    step = pl.program_id(0)
    place = Place(wins, dps)
    up = Stream(place, up_source, up_sum, streams[: Stream.PARTS])
    down = Stream(place, down_source, down_sum, streams[Stream.PARTS :])

    @pl.when(step == 0)
    def _():
        place.greet()
        up.load()
        down.load()

    patch = triple.shape[0]
    load_triple(t, triple, triple0, patch)
    rows = (patch + 1) * WC
    for b in range(4):
        t[12 + b, 0:rows] = grad_merged[:, :, 128 * b : 128 * b + 128].reshape(rows, 128).astype(f32)
        t[12 + b, rows:] = jnp.zeros((TP * WC - rows, 128), f32)

    def slot(k):
        if k == 0:
            place.greeted()
        up.step(k)
        down.step(k - 1)

    def body(i, carry):
        for u in range(4):
            local_bwd_step(i * 4 + u, probs, t, d)
        for k in range(6):

            @pl.when(step * (WC // 4) + i == 2 * k)
            def _(k=k):
                slot(k)

        return carry

    lax.fori_loop(0, WC // 4, body, 0)
    at = pl.ds(pl.multiple_of(step * WC, WC), WC)
    for b in range(12):
        lanes = slice(128 * b, 128 * b + 128)
        low = d[b, 0:rows].astype(bf16)
        grad_triple[:, :, lanes] = low.reshape(patch + 1, WC, 128)
        d0[at, lanes] = low[rows - WC :]

    @pl.when(step == pl.num_programs(0) - 1)
    def _():
        vhat, inverse = norm_stats(region_mid[...])
        mid = grad_middle0[0].astype(f32) + norm_back(vhat, inverse, row(vecs, GAIN1), nt(d0[...], w_qkv[...]))
        grad_mid[...] = mid
        grad_attn = mid.astype(bf16)
        out_grad[...] = (out_local[...] + tn(merged_r[...], grad_attn)).astype(bf16)
        out_bias_part[...] = col(grad_attn.astype(f32))
        grad_merged_r = nt(grad_attn, w_out[...]).astype(bf16)
        for g in range(2):
            lanes = slice(256 * g, 256 * g + 256)
            value_lanes = slice(D + 256 * g, D + 256 * g + 256)
            qx = expand_group(region_triple[:, lanes], 8)
            gx = expand_group(grad_merged_r[:, lanes], 8)
            low = probs_r[g]
            high = low.astype(f32)
            scaled = high * nt(gathered[:, value_lanes], gx)
            back = (scaled - high * col(scaled)).astype(bf16)
            terms[:, lanes] = (nn(back, qx) * SCALING).astype(bf16)
            terms[:, value_lanes] = nn(low, gx).astype(bf16)
            grad_query[:, lanes] = (fold_group(tn(back, gathered[:, lanes]), 8) * SCALING).astype(bf16)
            slot(6 + g)
        sums[:, :D] = col(grad_query[...].astype(f32))
        sums[:, D:] = col(terms[...].astype(f32))
        slot(8)
        slot(9)


def gelu_both(v):
    e = jnp.exp2(v * v * (-0.5 * LOG2E))
    cdf = 0.5 + 0.5 * lax.erf(v * (0.5**0.5))
    return v * cdf, cdf + v * e * 0.3989422804014327


def with_region(block, region, last):
    tokens, count, width = block.shape
    head = block[0 : tokens - 1].reshape((tokens - 1) * count, width)
    tail = jnp.where(last, region, block[tokens - 1])
    return jnp.concatenate([head, tail], axis=0)


def mlp_kernel(
    patches, region_mid, merged, patch_cot, region_cot, vecs, w_out, w_up, w_down,
    patch_out, region_out, grad_middle, grad_merged, up_grad, down_grad_t, out_grad, vec512, up_bias_grad,
    up_acc, down_acc,
):
    step = pl.program_id(0)
    last = step == pl.num_programs(0) - 1
    tokens, count, _ = patches.shape
    rows = tokens * count

    @pl.when(step == 0)
    def _():
        up_acc[...] = jnp.zeros_like(up_acc)
        down_acc[...] = jnp.zeros_like(down_acc)
        out_grad[...] = jnp.zeros_like(out_grad)
        vec512[...] = jnp.zeros_like(vec512)
        up_bias_grad[...] = jnp.zeros_like(up_bias_grad)

    x = with_region(patches[...].astype(f32), region_mid[...], last)
    grad_result = with_region(patch_cot[...], region_cot[...], last)
    low_merged = merged[...].reshape(rows, D)
    middle = x + nn(low_merged, w_out[...]) + row(vecs, OUT_BIAS)
    vhat, inverse = norm_stats(middle)
    mlp_in = normed_low(vhat, vecs, GAIN2, SHIFT2)
    mlp_in_t = mlp_in.T
    grad_result_t = grad_result.T
    result = middle + row(vecs, DOWN_BIAS)
    grad_in = jnp.zeros((rows, D), f32)
    for f in range(FF // 512):
        at = slice(512 * f, 512 * f + 512)
        hidden = nn(mlp_in, w_up[:, at]) + row(vecs, UP_BIAS + f)
        active, slope = gelu_both(hidden)
        active = active.astype(bf16)
        grad_hidden = (nt(grad_result, w_down[at, :]) * slope).astype(bf16)
        result += nn(active, w_down[at, :])
        grad_in += nt(grad_hidden, w_up[:, at])
        up_acc[:, at] += nn(mlp_in_t, grad_hidden)
        down_acc[:, at] += nn(grad_result_t, active)
        up_bias_grad[:, at] += col(grad_hidden.astype(f32))
    shown = result.astype(bf16)
    patch_out[...] = shown.reshape(tokens, count, D)
    region_out[...] = shown[rows - count :]
    gm = grad_result.astype(f32) + norm_back(vhat, inverse, row(vecs, GAIN2), grad_in)
    low_gm = gm.astype(bf16)
    grad_middle[...] = low_gm.reshape(tokens, count, D)
    out_grad[...] += nn(low_merged.T, low_gm)
    grad_merged[...] = nt(low_gm, w_out[...]).astype(bf16).reshape(tokens, count, D)
    vec512[0:1] += col(grad_in * vhat)
    vec512[1:2] += col(grad_in)
    vec512[2:3] += col(low_gm.astype(f32))
    vec512[3:4] += col(grad_result.astype(f32))

    @pl.when(last)
    def _():
        up_grad[...] = up_acc[...].astype(bf16)
        down_grad_t[...] = down_acc[...].astype(bf16)


def tail_kernel(
    wins, dps,
    patches, grad_triple, grad_middle, region_mid, vecs, w_qkv, region_in_all, terms, grad_query,
    regional, grad_mid, vec_mlp, up_bias_grad, sums, out_bias_part, out_source,
    patch_grad, region_grad, small_sum, out_sum, query_sum, key_sum, value_sum,
    qkv_acc, qkv_low, triple_sums, vec, pieces, piece_sem, pack, near, near_sem, total, far, far_sem, *streams,
):
    step = pl.program_id(0)
    half = pl.num_programs(0) // 2
    tokens, count, _ = patches.shape
    rows = tokens * count
    place = Place(wins, dps)
    parts = [streams[Stream.PARTS * b : Stream.PARTS * (b + 1)] for b in range(4)]
    out = Stream(place, out_source, out_sum, parts[0])
    blocks = [Stream(place, qkv_low.at[b], (query_sum, key_sum, value_sum)[b], parts[b + 1]) for b in range(3)]

    def to_owners():
        copies = []
        for j in range(1, wins):
            win = lax.rem(place.win + j, wins)
            copies.append(pltpu.make_async_remote_copy(
                src_ref=terms.at[pl.ds(pl.multiple_of(win * count, 16), count)], dst_ref=pieces.at[j - 1],
                send_sem=piece_sem.at[2 * j - 2], recv_sem=piece_sem.at[2 * j - 1],
                device_id={"win": win}, device_id_type=MESH,
            ))
        return copies

    def to_near():
        return [pltpu.make_async_remote_copy(
            src_ref=pack, dst_ref=near.at[j - 1], send_sem=near_sem.at[2 * j - 2], recv_sem=near_sem.at[2 * j - 1],
            device_id={"win": lax.rem(place.win + j, wins)}, device_id_type=MESH,
        ) for j in range(1, wins)]

    def to_far():
        return [pltpu.make_async_remote_copy(
            src_ref=total, dst_ref=far.at[j - 1], send_sem=far_sem.at[2 * j - 2], recv_sem=far_sem.at[2 * j - 1],
            device_id=place.at_dp(j)[1], device_id_type=MESH,
        ) for j in range(1, dps)]

    def begin():
        place.greeted(all_wins=True)
        for c in to_owners():
            c.start()
        out.load()
        out.send_cores()

    def region_end():
        for c in to_owners():
            c.wait()
        key_value = terms[pl.ds(pl.multiple_of(place.win * count, 16), count)].astype(f32)
        for j in range(wins - 1):
            key_value += pieces[j].astype(f32)
        vhat, inverse = norm_stats(regional[...].astype(f32))
        grad_in = nt(grad_query[...], w_qkv[:, :D]) + nt(key_value.astype(bf16), w_qkv[:, D:])
        region_grad[...] = (grad_mid[...] + norm_back(vhat, inverse, row(vecs, GAIN1), grad_in)).astype(bf16)
        vec[0:1] += col(grad_in * vhat)
        vec[1:2] += col(grad_in)

    def qkv_end():
        shape = qkv_low.shape[1:]
        qkv_low[0] = (qkv_acc[:, :D] + tn(region_in_all[pl.ds(pl.multiple_of(place.win * count, 16), count)], grad_query[...])).astype(bf16).reshape(shape)
        for b in range(1, 3):
            lanes = slice(D * (b - 1), D * b)
            qkv_low[b] = (qkv_acc[:, D * b : D * (b + 1)] + tn(region_in_all[...], terms[:, lanes])).astype(bf16).reshape(shape)
        for s in blocks:
            s.load()
            s.send_cores()

    def small_begin():
        pack[0:2] = vec[0:2]
        pack[2:3] = triple_sums[:, :D] + sums[:, :D]
        pack[3:4] = triple_sums[:, 2 * D :] + sums[:, 2 * D :]
        pack[4:5] = vec_mlp[2:3] + out_bias_part[...]
        pack[5:7] = vec_mlp[0:2]
        pack[7:8] = vec_mlp[3:4]
        for b in range(4):
            pack[8 + b : 9 + b] = up_bias_grad[:, D * b : D * (b + 1)]
        pack[12:16] = jnp.zeros((4, D), f32)
        for c in to_near():
            c.start()

    def small_middle():
        for c in to_near():
            c.wait()
        part = pack[...]
        for j in range(wins - 1):
            part += near[j]
        total[...] = part
        for c in to_far():
            c.start()

    def small_end():
        for c in to_far():
            c.wait()
        part = total[...]
        for j in range(dps - 1):
            part += far[j]
        small_sum[...] = part

    @pl.when(step == 0)
    def _():
        place.greet(all_wins=True)
        qkv_acc[...] = jnp.zeros_like(qkv_acc)
        triple_sums[...] = jnp.zeros_like(triple_sums)
        vec[...] = jnp.zeros_like(vec)

    x = with_region(patches[...].astype(f32), region_mid[...], lax.rem(step, half) == half - 1)
    vhat, inverse = norm_stats(x)
    low = grad_triple[...].reshape(rows, 3 * D)

    @pl.when(step < half)
    def _():
        local_in = normed_low(vhat, vecs, GAIN1, SHIFT1)
        qkv_acc[...] += nn(local_in.T, low)
        triple_sums[...] += col(low.astype(f32))

    @pl.when(step >= half)
    def _():
        grad_in = nt(low, w_qkv[...])
        vec[0:1] += col(grad_in * vhat)
        vec[1:2] += col(grad_in)
        total_rows = grad_middle[...].reshape(rows, D).astype(f32) + norm_back(vhat, inverse, row(vecs, GAIN1), grad_in)
        patch_grad[...] = total_rows.astype(bf16).reshape(tokens, count, D)

    def slot(k):
        out.step(k)

    def block_slot(k):
        for s in blocks:
            s.step(k)

    def end():
        small_begin()
        for k in range(5, 7):
            block_slot(k)
        small_middle()
        block_slot(7)
        small_end()
        block_slot(8)

    hooks = {
        0: (begin,),
        1: (lambda: slot(1),),
        2: (lambda: slot(2), region_end),
        3: (lambda: slot(3),),
        half - 1: (qkv_end, lambda: slot(4)),
        half: (lambda: block_slot(1), lambda: slot(5)),
        half + 1: (lambda: block_slot(2), lambda: slot(6)),
        half + 2: (lambda: block_slot(3), lambda: slot(7)),
        half + 3: (lambda: block_slot(4), lambda: slot(8)),
        half + 4: (end,),
    }
    for when, todo in hooks.items():

        @pl.when(step == when)
        def _(todo=todo):
            for act in todo:
                act()


def last_kernel(
    up, down_t, out, query, key, value, small, patch_in, region_in,
    patch_grad, region_grad, in_gain, in_shift, qkv, qkv_bias, out_grad, out_bias, mlp_gain, mlp_shift,
    up_grad, up_bias, down_grad, down_bias,
):
    up_grad[...] = up[...].astype(f32)
    down_grad[...] = down_t[...].T.astype(f32)
    out_grad[...] = out[...].astype(f32)
    for b, part in enumerate((query, key, value)):
        qkv[:, D * b : D * (b + 1)] = part[...].astype(f32)
    patch_grad[...] = patch_in[...]

    @pl.when(pl.program_id(0) == 0)
    def _():
        region_grad[...] = region_in[...]
        for at, v in ((0, in_gain), (1, in_shift), (4, out_bias), (5, mlp_gain), (6, mlp_shift), (7, down_bias)):
            v[...] = small[at : at + 1].reshape(D)
        qkv_bias[...] = small[2:4]
        up_bias[...] = jnp.concatenate([small[8 + b : 9 + b] for b in range(FF // D)], axis=1).reshape(FF)


def shards(
    wins, dps,
    patches, regional, window_image, in_gain, in_shift, w_qkv, qkv_bias, w_out, out_bias,
    mlp_gain, mlp_shift, w_up, up_bias, w_down, down_bias, patch_cot, region_cot,
):
    _, count, patch, _ = patches.shape
    group = window_image.shape[1]
    x = patches[0].transpose(1, 0, 2)
    cot = patch_cot[0].transpose(1, 0, 2)
    reg = regional[0]
    rcot = region_cot[0]
    const = lambda *arrays: [whole(a) for a in arrays]
    block = lambda a, n: (a, (n,) + a.shape[1:], lambda i: (i, 0, 0))
    block_out = lambda shape, n, dtype=bf16: ((shape, dtype), (n,) + shape[1:], lambda i: (i, 0, 0))
    triple, vecs, region_triple, gathered, probs_r, merged_r, region_mid, triple0 = call(
        functools.partial(front_kernel, wins, dps), (pl.cdiv(patch, 7),),
        [block(x, 7)]
        + const(reg, window_image, in_gain, in_shift, w_qkv, qkv_bias, w_out, out_bias, mlp_gain, mlp_shift, up_bias, down_bias),
        [block_out((patch, count, 3 * D), 7), whole_out((16, D), f32), whole_out((count, 3 * D), bf16),
         whole_out((group, 3 * D), bf16), whole_out((2, group, 8 * count), bf16), whole_out((count, D), bf16),
         whole_out((count, D), f32), whole_out((count, 3 * D), bf16)],
        [pltpu.VMEM((group, 3 * D), bf16), pltpu.VMEM((count, 3 * D), bf16), pltpu.VMEM((group, 128), f32),
         pltpu.SemaphoreType.DMA((2 * wins,))],
        name="front", collective_id=2,
    )
    steps = (count // WC,)
    mid = lambda a: (a, (a.shape[0], WC, a.shape[2]), lambda i: (0, i, 0))
    mid_out = lambda shape, dtype=bf16: ((shape, dtype), (shape[0], WC, shape[2]), lambda i: (0, i, 0))
    tail = lambda a: (a, (WC, a.shape[1]), lambda i: (i, 0))
    merged, probs = call(
        local_fwd_kernel, steps, [mid(triple), tail(triple0)],
        [mid_out((patch + 1, count, D)), ((((count, TP, HEADS * TP)), bf16), (WC, TP, HEADS * TP), lambda i: (i, 0, 0))],
        [pltpu.VMEM((12, TP * WC, 128), f32), pltpu.VMEM((4, TP * WC, 128), f32)], name="local_fwd",
    )
    n = 10
    rows_grid = ((patch + 1) // n,)
    patch_out, region_out, grad_middle, grad_merged, up_grad, down_grad_t, out_local, vec_mlp, up_bias_grad = call(
        mlp_kernel, rows_grid,
        [block(x, n), whole(region_mid), block(merged, n), block(cot, n)]
        + const(rcot, vecs, w_out, w_up, w_down),
        [block_out((patch, count, D), n), whole_out((count, D), bf16),
         block_out((patch + 1, count, D), n), block_out((patch + 1, count, D), n),
         whole_out((D, FF), bf16), whole_out((D, FF), bf16), whole_out((D, D), f32),
         whole_out((8, D), f32), whole_out((1, FF), f32)],
        [pltpu.VMEM((D, FF), f32), pltpu.VMEM((D, FF), f32)], name="mlp",
    )
    grad_triple, up_sum, down_sum, terms, grad_query, out_grad, sums, out_bias_part, grad_mid = call(
        functools.partial(back_kernel, wins, dps), steps,
        [mid(triple), tail(triple0), (probs, (WC, TP, HEADS * TP), lambda i: (i, 0, 0)), mid(grad_merged)]
        + const(region_triple, gathered, probs_r, merged_r, region_mid)
        + [(grad_middle, (1, count, D), lambda i: (patch, 0, 0))]
        + const(vecs, w_qkv, w_out, out_local) + [left(a.reshape(stream_shape(wins, FF))) for a in (up_grad, down_grad_t)],
        [mid_out((patch + 1, count, 3 * D)), left_out(stream_shape(wins, FF), bf16), left_out(stream_shape(wins, FF), bf16),
         whole_out((group, 2 * D), bf16), whole_out((count, D), bf16), whole_out((D, D), bf16),
         whole_out((1, 3 * D), f32), whole_out((1, D), f32), whole_out((count, D), f32)],
        [pltpu.VMEM((16, TP * WC, 128), f32), pltpu.VMEM((12, TP * WC, 128), f32), pltpu.VMEM((count, 3 * D), bf16)]
        + stream_scratch(wins, dps, FF) * 2,
        name="back", collective_id=0,
    )
    half = rows_grid[0]
    again = lambda a: (a, (n,) + a.shape[1:], lambda i: (lax.rem(i, half), 0, 0))
    second = lambda a: (a, (n,) + a.shape[1:], lambda i: (lax.max(i - half, 0), 0, 0))
    patch_grad, region_grad, small, out_sum, query_sum, key_sum, value_sum = call(
        functools.partial(tail_kernel, wins, dps), (2 * half,),
        [again(x), again(grad_triple), second(grad_middle)]
        + const(region_mid, vecs, w_qkv)
        + [(gathered, (group, D), lambda i: (0, 2))]
        + const(terms, grad_query, reg, grad_mid, vec_mlp, up_bias_grad, sums, out_bias_part) + [left(out_grad.reshape(stream_shape(wins, D)))],
        [(((patch, count, D), bf16), (n, count, D), lambda i: (lax.max(i - half, 0), 0, 0)),
         whole_out((count, D), bf16), whole_out((16, D), f32)] + [left_out(stream_shape(wins, D), bf16)] * 4,
        [pltpu.VMEM((D, 3 * D), f32), pltpu.VMEM((3,) + stream_shape(wins, D), bf16), pltpu.VMEM((1, 3 * D), f32), pltpu.VMEM((8, D), f32),
         pltpu.VMEM((wins - 1, count, 2 * D), bf16), pltpu.SemaphoreType.DMA((2 * wins,)),
         pltpu.VMEM((16, D), f32), pltpu.VMEM((wins - 1, 16, D), f32), pltpu.SemaphoreType.DMA((2 * wins,)),
         pltpu.VMEM((16, D), f32), pltpu.VMEM((max(dps - 1, 1), 16, D), f32), pltpu.SemaphoreType.DMA((2 * dps,))]
        + stream_scratch(wins, dps, D) * 4,
        name="tail", collective_id=1,
    )
    up_sum, down_sum = up_sum.reshape(D, FF), down_sum.reshape(D, FF)
    out_sum, query_sum, key_sum, value_sum = (a.reshape(D, D) for a in (out_sum, query_sum, key_sum, value_sum))
    n = 8
    down = lambda i: (i, 0)
    vector = lambda size: ((((size,), f32)), (size,), lambda i: (0,))
    token = -(-patch // n)
    tokens = lambda i: (lax.min(i, (patch - 1) // token), 0, 0)
    (
        patch_grad, region_grad, in_gain_grad, in_shift_grad, qkv_grad, qkv_bias_grad, out_grad, out_bias_grad,
        mlp_gain_grad, mlp_shift_grad, up_grad, up_bias_grad, down_grad, down_bias_grad,
    ) = call(
        last_kernel, (n,),
        [(up_sum, (D // n, FF), down), (down_sum, (D, FF // n), lambda i: (0, i))]
        + [(a, (D // n, D), down) for a in (out_sum, query_sum, key_sum, value_sum)]
        + [whole(small), (patch_grad, (token, count, D), tokens), whole(region_grad)],
        [(((patch, count, D), bf16), (token, count, D), tokens), whole_out((count, D), bf16), vector(D), vector(D),
         (((D, 3 * D), f32), (D // n, 3 * D), down), whole_out((2, D), f32), (((D, D), f32), (D // n, D), down), vector(D),
         vector(D), vector(D), (((D, FF), f32), (D // n, FF), down), vector(FF), (((FF, D), f32), (FF // n, D), down), vector(D)],
        name="last",
    )
    return (
        patch_out.transpose(1, 0, 2)[None], region_out[None], patch_grad.transpose(1, 0, 2)[None], region_grad[None],
        in_gain_grad, in_shift_grad, qkv_grad, qkv_bias_grad, out_grad, out_bias_grad,
        mlp_gain_grad, mlp_shift_grad, up_grad, up_bias_grad, down_grad, down_bias_grad,
    )


def solution(mesh):
    wide = P("dp", "win", None, None)
    narrow = P("dp", "win", None)
    in_specs = (wide, narrow, P("dp", None)) + (P(),) * 12 + (wide, narrow)
    out_specs = (wide, narrow, wide, narrow) + (P(),) * 12
    return jax.shard_map(functools.partial(shards, mesh.shape["win"], mesh.shape["dp"]), mesh=mesh, in_specs=in_specs, out_specs=out_specs, check_vma=False)
```

```python
import functools

import jax
import jax.numpy as jnp
from jax import lax
from jax.experimental import pallas as pl
from jax.experimental.pallas import tpu as pltpu
from jax.sharding import PartitionSpec as P

D = 512
HEADS = 16
HD = 32
FF = 2048
EPSILON = 1e-06
MASKED_SCORE = -1e30
SCALING = HD ** (-0.5)
LOG2E = 1.4426950408889634
TP = 64
WC = 16
f32 = jnp.float32
bf16 = jnp.bfloat16
VMEM_LIMIT = 60 * 2**20
MESH = pl.DeviceIdType.MESH
BACK_SLOTS = (0, 1, 5, 8)


def nn(a, b):
    return lax.dot_general(a, b, (((1,), (0,)), ((), ())), preferred_element_type=f32)


def nt(a, b):
    return lax.dot_general(a, b, (((1,), (1,)), ((), ())), preferred_element_type=f32)


def tn(a, b):
    return lax.dot_general(a, b, (((0,), (0,)), ((), ())), preferred_element_type=f32)


def call(body, grid, ins, outs, scratch=(), name=None, collective_id=None):
    def spec(block, index, *single):
        if block is None:
            return pl.BlockSpec(memory_space=pl.ANY)
        if index is None:
            return pl.BlockSpec(block, lambda *_: (0,) * len(block), pipeline_mode=pl.Buffered(1))
        return pl.BlockSpec(block, index, pipeline_mode=pl.Buffered(1) if any(single) else None)

    return pl.pallas_call(
        body,
        grid=grid,
        in_specs=[spec(*entry[1:]) for entry in ins],
        out_specs=[spec(b, i) for _, b, i in outs],
        out_shape=[jax.ShapeDtypeStruct(s, d) for (s, d), _, _ in outs],
        scratch_shapes=list(scratch),
        compiler_params=pltpu.CompilerParams(
            vmem_limit_bytes=VMEM_LIMIT, collective_id=collective_id, has_side_effects=collective_id is not None
        ),
        name=name,
    )(*[entry[0] for entry in ins])


def whole(a):
    return (a, a.shape, None)


def whole_out(shape, dtype):
    return ((shape, dtype), shape, None)


def left(a):
    return (a, None, None)


def left_out(shape, dtype):
    return ((shape, dtype), None, None)


def norm_stats(rows):
    average = jnp.mean(rows, axis=-1, keepdims=True)
    centred = rows - average
    spread = jnp.mean(centred * centred, axis=-1, keepdims=True)
    inverse = lax.rsqrt(spread + EPSILON)
    return centred * inverse, inverse


def norm_back(vhat, inverse, gain, grad_out):
    scaled = grad_out * gain
    first = jnp.mean(scaled, axis=-1, keepdims=True)
    second = jnp.mean(scaled * vhat, axis=-1, keepdims=True)
    return inverse * (scaled - first - vhat * second)


def col(x):
    return jnp.sum(x, axis=0, keepdims=True)


class Place:
    def __init__(self, wins, dps):
        self.wins, self.dps = wins, dps
        self.win = lax.axis_index("win")
        self.dp = lax.axis_index("dp")
        self.core = lax.rem(self.win, 2)
        self.chip = self.win // 2
        self.chips = wins // 2
        self.square = self.chips == 4
        self.a = self.chip // 2
        self.b = lax.rem(self.chip, 2)

    def other_core(self):
        return {"win": self.chip * 2 + 1 - self.core}

    def other_a(self):
        return {"win": ((1 - self.a) * 2 + self.b) * 2 + self.core}

    def other_b(self):
        return {"win": (self.a * 2 + 1 - self.b) * 2 + self.core}

    def at_chip(self, j):
        chip = lax.rem(self.chip + j, self.chips)
        return chip, {"win": chip * 2 + self.core}

    def at_dp(self, j):
        dp = lax.rem(self.dp + j, self.dps)
        return dp, {"dp": dp}

    def near(self, all_wins):
        if all_wins:
            return [{"win": lax.rem(self.win + j, self.wins)} for j in range(1, self.wins)]
        if self.square:
            return [self.other_core(), self.other_a(), self.other_b()]
        return [self.other_core()] + [self.at_chip(j)[1] for j in range(1, self.chips)]

    def partners(self, all_wins, along):
        return self.near(all_wins) + [self.at_dp(j)[1] for j in range(1, self.dps if along else 1)]

    def greet(self, all_wins=False, along=True):
        barrier = pltpu.get_barrier_semaphore()
        for to in self.partners(all_wins, along):
            pl.semaphore_signal(barrier, inc=1, device_id=to, device_id_type=MESH)

    def greeted(self, all_wins=False, along=True):
        pl.semaphore_wait(pltpu.get_barrier_semaphore(), len(self.partners(all_wins, along)))


def rows_of(wins, dps):
    piece = D // wins
    return piece, piece // dps if piece % (16 * dps) == 0 else piece


def stream_shape(wins, columns):
    return (2, wins // 2, D // wins, columns)


def stream_scratch(wins, dps, columns, kind="whole"):
    piece, last = rows_of(wins, dps)
    chips = wins // 2
    landing = (4, 2, piece, columns // 2) if chips == 4 else (max(chips - 1, 1), piece, columns)
    half, part, some = pltpu.VMEM((chips, piece, columns), bf16), pltpu.VMEM((piece, columns), bf16), pltpu.VMEM((16, 128), bf16)
    down = kind != "back"
    return [
        half if down else some,
        half,
        pltpu.VMEM(landing, bf16) if down else some,
        part if down else some,
        pltpu.VMEM((max(dps - 1, 1), last, columns), bf16) if down else some,
        some if kind == "down" else part,
        pltpu.SemaphoreType.DMA((20 + 4 * chips + 4 * dps,)),
    ]


def columns_of(refs):
    return refs[1].shape[2]


class Stream:
    PARTS = 7

    def __init__(self, place, source, final, refs):
        self.p = place
        self.source, self.final = source, final
        self.own, self.r1, self.r2, self.s, self.r3, self.s2, self.sem = refs
        self.piece, self.last = rows_of(place.wins, place.dps)
        self.split = self.last != self.piece
        columns = columns_of(refs)
        self.left, self.right = pl.ds(0, columns // 2), pl.ds(columns // 2, columns // 2)

    def rows(self, start, size):
        return pl.ds(pl.multiple_of(start, 16), size)

    def remote(self, src, dst, to, k):
        return pltpu.make_async_remote_copy(
            src_ref=src, dst_ref=dst, send_sem=self.sem.at[2 * k], recv_sem=self.sem.at[2 * k + 1],
            device_id=to, device_id_type=MESH,
        )

    def _own(self):
        return pltpu.make_async_copy(self.source.at[self.p.core], self.own, self.sem.at[0])

    def _put(self):
        return pltpu.make_async_copy(self.r1, self.final.at[self.p.core], self.sem.at[1])

    def _cores(self):
        return [self.remote(self.source.at[1 - self.p.core], self.r1, self.p.other_core(), 1)]

    def _cores_back(self):
        return [self.remote(self.r1, self.final.at[self.p.core], self.p.other_core(), 2)]

    def _chips_left(self, k):
        p = self.p
        if k == 0:
            return [self.remote(self.own.at[c * 2 + 1 - p.b, :, self.left], self.r2.at[0, c], p.other_b(), 3 + c) for c in range(2)]
        return [self.remote(self.own.at[(1 - p.a) * 2 + p.b, :, self.left], self.r2.at[2, 0], p.other_a(), 5)]

    def _chips_right(self, k):
        p = self.p
        if k == 0:
            return [self.remote(self.own.at[(1 - p.a) * 2 + c, :, self.right], self.r2.at[1, c], p.other_a(), 6 + c) for c in range(2)]
        return [self.remote(self.own.at[p.a * 2 + 1 - p.b, :, self.right], self.r2.at[3, 0], p.other_b(), 8)]

    def _back_left(self, k):
        p = self.p
        mine = self.r1
        if k == 0:
            return [self.remote(self.s2.at[:, self.left], mine.at[p.chip, :, self.left], p.other_a(), 9)]
        rows = [mine.at[c * 2 + p.b, :, self.left] for c in range(2)]
        return [self.remote(rows[c], rows[c], p.other_b(), 10 + c) for c in range(2)]

    def _back_right(self, k):
        p = self.p
        mine = self.r1
        if k == 0:
            return [self.remote(self.s2.at[:, self.right], mine.at[p.chip, :, self.right], p.other_b(), 12)]
        rows = [mine.at[p.a * 2 + c, :, self.right] for c in range(2)]
        return [self.remote(rows[c], rows[c], p.other_a(), 13 + c) for c in range(2)]

    def _chips(self):
        out = []
        for j in range(1, self.p.chips):
            chip, to = self.p.at_chip(j)
            out.append(self.remote(self.own.at[chip], self.r2.at[j - 1], to, 2 + j))
        return out

    def _chips_back(self):
        out = []
        for j in range(1, self.p.chips):
            mine = self.r1.at[self.p.chip]
            out.append(self.remote(self.s2, mine, self.p.at_chip(j)[1], 2 + self.p.chips + j))
        return out

    def _dps(self):
        out = []
        for j in range(1, self.p.dps):
            dp, to = self.p.at_dp(j)
            src = self.s.at[self.rows(dp * self.last, self.last)] if self.split else self.s
            out.append(self.remote(src, self.r3.at[j - 1], to, 8 + 2 * self.p.chips + j))
        return out

    def _dps_back(self):
        out = []
        if self.split:
            for j in range(1, self.p.dps):
                mine = self.s2.at[self.rows(self.p.dp * self.last, self.last)]
                out.append(self.remote(mine, mine, self.p.at_dp(j)[1], 8 + 2 * self.p.chips + self.p.dps + j))
        return out

    def start(self, copies):
        for c in copies:
            c.start()

    def wait(self, copies):
        for c in copies:
            c.wait()

    def load(self):
        self._own().start()

    def send_cores(self):
        self.start(self._cores())

    def send_chips(self):
        self._own().wait()
        self.wait(self._cores())

        def add(i, carry):
            self.own[i] = (self.own[i].astype(f32) + self.r1[i].astype(f32)).astype(bf16)
            return carry

        lax.fori_loop(0, self.p.chips, add, 0)
        if self.p.square:
            self.start(self._chips_left(0))
            self.start(self._chips_right(0))
        else:
            self.start(self._chips())

    def add_square(self, chip, lanes, slot, c):
        self.own[chip, :, lanes] = (self.own[chip, :, lanes].astype(f32) + self.r2[slot, c].astype(f32)).astype(bf16)

    def send_chips_again(self):
        p = self.p
        if p.square:
            self.wait(self._chips_left(0))
            for c in range(2):
                self.add_square(c * 2 + p.b, self.left, 0, c)
            self.start(self._chips_left(1))
            self.wait(self._chips_right(0))
            for c in range(2):
                self.add_square(p.a * 2 + c, self.right, 1, c)
            self.start(self._chips_right(1))

    def send_dps(self):
        p = self.p
        if p.square:
            for lanes, slot, copies in ((self.left, 2, self._chips_left(1)), (self.right, 3, self._chips_right(1))):
                self.wait(copies)
                self.s[:, lanes] = (self.own[p.chip, :, lanes].astype(f32) + self.r2[slot, 0].astype(f32)).astype(bf16)
        else:
            self.wait(self._chips())
            total = self.own[p.chip].astype(f32)
            for j in range(p.chips - 1):
                total += self.r2[j].astype(f32)
            self.s[...] = total.astype(bf16)
        self.start(self._dps())

    def sum_dps(self, out, at):
        self.wait(self._dps())
        mine = self.part()
        total = self.s[mine].astype(f32)
        for j in range(self.p.dps - 1):
            total += self.r3[j].astype(f32)
        out[at] = total.astype(bf16)

    def part(self):
        return self.rows(self.p.dp * self.last if self.split else 0, self.last)

    def send_dps_back(self):
        self.sum_dps(self.s2, self.part())
        self.start(self._dps_back())

    def end_dps_back(self):
        self.wait(self._dps_back())

    def begin_back(self, part):
        self.s2[self.part()] = part[...]
        self.start(self._dps_back())

    def send_chips_back(self):
        self.end_dps_back()
        self.start_chips_back()

    def start_chips_back(self):
        self.r1[self.p.chip] = self.s2[...]
        if self.p.square:
            self.start(self._back_left(0))
            self.start(self._back_right(0))
        else:
            self.start(self._chips_back())

    def send_chips_back_again(self):
        if self.p.square:
            self.wait(self._back_left(0))
            self.start(self._back_left(1))
            self.wait(self._back_right(0))
            self.start(self._back_right(1))
        else:
            self.wait(self._chips_back())

    def send_cores_back(self):
        if self.p.square:
            self.wait(self._back_left(1))
            self.wait(self._back_right(1))
        self.start(self._cores_back())
        self._put().start()

    def finish(self):
        self.wait(self._cores_back())
        self._put().wait()

    STEPS = (
        "send_cores", "send_chips", "send_chips_again", "send_dps", "send_dps_back",
        "send_chips_back", "send_chips_back_again", "send_cores_back", "finish",
    )

    def step(self, k):
        if 0 <= k < len(self.STEPS):
            getattr(self, self.STEPS[k])()


def expand_group(x, heads):
    lane = lax.broadcasted_iota(jnp.int32, (1, x.shape[1]), 1) // HD
    return jnp.concatenate([jnp.where(lane == i, x, jnp.zeros_like(x)) for i in range(heads)], axis=0)


def fold_group(y, heads):
    rows = y.shape[0] // heads
    lane = lax.broadcasted_iota(jnp.int32, (1, y.shape[1]), 1) // HD
    total = y[(heads - 1) * rows :]
    for i in range(heads - 2, -1, -1):
        total = jnp.where(lane == i, y[i * rows : (i + 1) * rows], total)
    return total


GAIN1, SHIFT1, GAIN2, SHIFT2, OUT_BIAS, DOWN_BIAS, QUERY_BIAS, KEY_BIAS, VALUE_BIAS, UP_BIAS = range(10)


def row(vecs, at):
    return vecs[at : at + 1]


def normed_low(vhat, vecs, gain, shift):
    return (vhat * row(vecs, gain) + row(vecs, shift)).astype(bf16)


def front_kernel(
    wins, dps,
    patches, regional, images, in_gain, in_shift, w_qkv, qkv_bias, w_out, out_bias, mlp_gain, mlp_shift, up_bias, down_bias,
    triple, local_in, vecs, region_triple, gathered_out, probs, merged, region_mid, triple0, local_in0,
    gathered, packed, image_col, sem,
):
    step = pl.program_id(0)
    place = Place(wins, dps)
    count = regional.shape[0]
    group = gathered.shape[0]
    mine = pl.ds(pl.multiple_of(place.win * count, 16), count)

    def project(normed):
        out = nn(normed, w_qkv[...])
        return jnp.concatenate(
            [out[:, :D] + row(vecs, QUERY_BIAS), out[:, D : 2 * D], out[:, 2 * D :] + row(vecs, VALUE_BIAS)], axis=1
        ).astype(bf16)

    def sends():
        copies = []
        for j in range(1, wins):
            copies.append(pltpu.make_async_remote_copy(
                src_ref=packed, dst_ref=gathered.at[mine], send_sem=sem.at[2 * j - 2], recv_sem=sem.at[2 * j - 1],
                device_id={"win": lax.rem(place.win + j, wins)}, device_id_type=MESH,
            ))
        return copies

    @pl.when(step == 0)
    def _():
        place.greet(all_wins=True, along=False)
        for at, v in (
            (GAIN1, in_gain), (SHIFT1, in_shift), (GAIN2, mlp_gain), (SHIFT2, mlp_shift), (OUT_BIAS, out_bias), (DOWN_BIAS, down_bias),
        ):
            vecs[at : at + 1] = v[...].astype(f32).reshape(1, D)
        vecs[QUERY_BIAS : QUERY_BIAS + 1] = qkv_bias[0:1].astype(f32)
        vecs[KEY_BIAS : KEY_BIAS + 1] = jnp.zeros((1, D), f32)
        vecs[VALUE_BIAS : VALUE_BIAS + 1] = qkv_bias[1:2].astype(f32)
        up = up_bias[...].astype(f32).reshape(1, FF)
        for b in range(FF // D):
            vecs[UP_BIAS + b : UP_BIAS + b + 1] = up[:, D * b : D * (b + 1)]
        vecs[UP_BIAS + FF // D : 16] = jnp.zeros((16 - UP_BIAS - FF // D, D), f32)
        vhat, _ = norm_stats(regional[...].astype(f32))
        normed = normed_low(vhat, vecs, GAIN1, SHIFT1)
        own = project(normed)
        region_triple[...] = own
        packed[:, : 2 * D] = own[:, D:]
        packed[:, 2 * D :] = normed
        gathered[mine] = packed[...]
        place.greeted(all_wins=True, along=False)
        for c in sends():
            c.start()
        ids = images[...].astype(f32)
        image_col[...] = jnp.broadcast_to(ids, (128, group)).T

    rows = patches.shape[0] * count
    vhat, _ = norm_stats(patches[...].reshape(rows, D).astype(f32))
    normed_rows = normed_low(vhat, vecs, GAIN1, SHIFT1)
    local_in[...] = normed_rows.reshape(local_in.shape)
    triple[...] = project(normed_rows).reshape(triple.shape)

    @pl.when(step == pl.num_programs(0) - 1)
    def _():
        for c in sends():
            c.wait()
        gathered_out[...] = gathered[...]
        own_ids = image_col[mine]
        own_row = jnp.concatenate([own_ids] * 8, axis=0).T[0:1]
        same = image_col[:, 0:1] == own_row
        for g in range(2):
            lanes = slice(256 * g, 256 * g + 256)
            scores = nt(gathered[:, lanes], expand_group(region_triple[:, lanes], 8))
            scores = jnp.where(same, scores * SCALING, MASKED_SCORE)
            top = jnp.max(scores, axis=0, keepdims=True)
            exps = jnp.exp2((scores - top) * LOG2E)
            low = (exps * (1.0 / col(exps))).astype(bf16)
            probs[g] = low
            merged[:, lanes] = fold_group(tn(low, gathered[:, D + 256 * g : D + 256 * g + 256]), 8).astype(bf16)
        mid = regional[...].astype(f32) + nn(merged[...], w_out[...]) + row(vecs, OUT_BIAS)
        region_mid[...] = mid
        vhat_mid, _ = norm_stats(mid)
        normed_mid = normed_low(vhat_mid, vecs, GAIN1, SHIFT1)
        local_in0[...] = normed_mid
        triple0[...] = project(normed_mid)


def expand(x):
    lane = lax.broadcasted_iota(jnp.int32, (1, 128), 1) // HD
    return jnp.concatenate([jnp.where(lane == i, x, jnp.zeros_like(x)) for i in range(4)], axis=0)


def query_side(rows, weights):
    lane = lax.broadcasted_iota(jnp.int32, (1, 128), 1) // HD
    out = tn(rows, weights)
    pairs = jnp.concatenate([out[0:64, 0:128], out[64:128, 128:256]], axis=0).T
    return jnp.where(lane % 2 == 0, pairs[0:64], pairs[64:128])


def load_triple(t, triple, triple0, patch):
    for b in range(12):
        lanes = slice(128 * b, 128 * b + 128)
        t[b, 0 : patch * WC] = triple[:, :, lanes].reshape(patch * WC, 128).astype(f32)
        t[b, patch * WC : (patch + 1) * WC] = triple0[:, lanes].astype(f32)
        t[b, (patch + 1) * WC :] = jnp.zeros(((TP - patch - 1) * WC, 128), f32)


def local_fwd_kernel(triple, triple0, merged, probs, t, m):
    patch = triple.shape[0]
    load_triple(t, triple, triple0, patch)
    row = lax.broadcasted_iota(jnp.int32, (TP, 1), 0)

    def one(w):
        for b in range(4):
            q = t[b, pl.ds(w, TP, stride=WC), :].astype(bf16)
            k = t[4 + b, pl.ds(w, TP, stride=WC), :].astype(bf16)
            v = t[8 + b, pl.ds(w, TP, stride=WC), :].astype(bf16)
            scores = nt(k, expand(q))
            scores = jnp.where(row <= patch, scores, MASKED_SCORE)
            top = jnp.max(scores, axis=0, keepdims=True)
            exps = jnp.exp2((scores - top) * (SCALING * LOG2E))
            low = (exps * (1.0 / col(exps))).astype(bf16)
            probs[w, :, 256 * b : 256 * b + 256] = low
            m[b, pl.ds(w, TP, stride=WC), :] = query_side(v, low)

    def body(i, carry):
        for u in range(4):
            one(i * 4 + u)
        return carry

    lax.fori_loop(0, WC // 4, body, 0)
    for b in range(4):
        merged[:, :, 128 * b : 128 * b + 128] = m[b, 0 : (patch + 1) * WC].astype(bf16).reshape(patch + 1, WC, 128)


def local_bwd_step(w, probs, t, d):
    at = pl.ds(w, TP, stride=WC)
    for b in range(4):
        q = t[b, at, :].astype(bf16)
        k = t[4 + b, at, :].astype(bf16)
        v = t[8 + b, at, :].astype(bf16)
        g = t[12 + b, at, :].astype(bf16)
        qx = expand(q)
        gx = expand(g)
        low = probs[w, :, 256 * b : 256 * b + 256]
        high = low.astype(f32)
        scaled = high * nt(v, gx)
        back = (scaled - high * col(scaled)).astype(bf16)
        d[4 + b, at, :] = nn(back, qx) * SCALING
        d[8 + b, at, :] = nn(low, gx)
        d[b, at, :] = query_side(k, back) * SCALING


def back_kernel(
    wins, dps,
    triple, triple0, probs, grad_merged, local_in, local_in0,
    region_triple, gathered, probs_r, merged_r, region_mid, grad_middle0, vecs, w_qkv, w_out, out_local,
    up_source, down_source,
    grad_triple, up_part, down_part, terms, grad_query, low_first, low_second, sums, out_bias_part, grad_mid,
    t, d, d0, qkv_acc, grad_merged_s, *streams,
):
    step = pl.program_id(0)
    place = Place(wins, dps)
    up = Stream(place, up_source, None, streams[: Stream.PARTS])
    down = Stream(place, down_source, None, streams[Stream.PARTS :])

    @pl.when(step == 0)
    def _():
        place.greet()
        up.load()
        down.load()
        qkv_acc[...] = jnp.zeros_like(qkv_acc)
        sums[...] = jnp.zeros_like(sums)

    patch = triple.shape[0]
    load_triple(t, triple, triple0, patch)
    rows = (patch + 1) * WC
    for b in range(4):
        t[12 + b, 0:rows] = grad_merged[:, :, 128 * b : 128 * b + 128].reshape(rows, 128).astype(f32)
        t[12 + b, rows:] = jnp.zeros((TP * WC - rows, 128), f32)

    def slot(k):
        if k == 0:
            place.greeted()
        for s in (up, down):
            if k < 4:
                s.step(k)
            else:
                s.sum_dps(up_part if s is up else down_part, slice(None))

    def body(i, carry):
        for u in range(4):
            local_bwd_step(i * 4 + u, probs, t, d)
        for k, when in enumerate(BACK_SLOTS):

            @pl.when(step * (WC // 4) + i == when)
            def _(k=k):
                slot(k)

        return carry

    lax.fori_loop(0, WC // 4, body, 0)
    at = pl.ds(pl.multiple_of(step * WC, WC), WC)
    for b in range(12):
        lanes = slice(128 * b, 128 * b + 128)
        low = d[b, 0:rows].astype(bf16)
        grad_triple[:, :, lanes] = low.reshape(patch + 1, WC, 128)
        d0[at, lanes] = low[rows - WC :]
        sums[:, lanes] += col(low.astype(f32))
    normed = jnp.concatenate([local_in[...].reshape(patch * WC, D), local_in0[...]], axis=0).T
    for b in range(3):
        lanes = slice(D * b, D * (b + 1))
        qkv_acc[:, lanes] += nn(normed, grad_triple[:, :, lanes].reshape(rows, D))

    @pl.when(step == pl.num_programs(0) - 1)
    def _():
        vhat, inverse = norm_stats(region_mid[...])
        mid = grad_middle0[0].astype(f32) + norm_back(vhat, inverse, row(vecs, GAIN1), nt(d0[...], w_qkv[...]))
        grad_mid[...] = mid
        grad_attn = mid.astype(bf16)
        out_low = (out_local[...] + tn(merged_r[...], grad_attn)).astype(bf16)
        out_bias_part[...] = col(grad_attn.astype(f32))
        grad_merged_r = nt(grad_attn, w_out[...]).astype(bf16)
        grad_merged_s[...] = grad_merged_r

        keys = gathered.shape[0]
        width = 8 * region_triple.shape[0]
        blocks = max(keys // width, 1) if keys % width == 0 else 1
        size = keys // blocks

        def group_half(g, carry):
            lanes = pl.ds(pl.multiple_of(256 * g, 256), 256)
            value_lanes = pl.ds(pl.multiple_of(D + 256 * g, 256), 256)
            qx = expand_group(region_triple[:, lanes], 8)
            gx = expand_group(grad_merged_s[:, lanes], 8)

            def scaled_at(at):
                high = probs_r[g, at].astype(f32)
                return high, high * nt(gathered[at, value_lanes], gx)

            def finish(at, row_terms, scaled=None):
                high, scaled = scaled_at(at) if scaled is None else scaled
                back = (scaled - high * row_terms).astype(bf16)
                terms[at, lanes] = (nn(back, qx) * SCALING).astype(bf16)
                terms[at, value_lanes] = nn(probs_r[g, at], gx).astype(bf16)
                return tn(back, gathered[at, lanes])

            if blocks == 1:
                both = scaled_at(pl.ds(0, keys))
                total = finish(pl.ds(0, keys), col(both[1]), both)
            else:
                at = lambda i: pl.ds(pl.multiple_of(i * size, 16), size)
                row_terms = lax.fori_loop(
                    0, blocks, lambda i, r: r + col(scaled_at(at(i))[1]), jnp.zeros((1, width), f32)
                )
                total = lax.fori_loop(
                    0, blocks, lambda i, q: q + finish(at(i), row_terms), jnp.zeros((width, 256), f32)
                )
            grad_query[:, lanes] = (fold_group(total, 8) * SCALING).astype(bf16)
            return carry

        if blocks == 1:
            group_half(0, 0)
            group_half(1, 0)
        else:
            lax.fori_loop(0, 2, group_half, 0)
        sums[:, :D] += col(grad_query[...].astype(f32))
        sums[:, D:] += col(terms[...].astype(f32))
        region_in_all = gathered[:, 2 * D :]
        own_in = gathered[pl.ds(pl.multiple_of(place.win * region_triple.shape[0], 16), region_triple.shape[0]), 2 * D :]
        shape = low_first.shape[:3] + (D,)
        low_first[:, :, :, :D] = (qkv_acc[:, :D] + tn(own_in, grad_query[...])).astype(bf16).reshape(shape)
        low_first[:, :, :, D:] = (qkv_acc[:, D : 2 * D] + tn(region_in_all, terms[:, :D])).astype(bf16).reshape(shape)
        low_second[:, :, :, :D] = (qkv_acc[:, 2 * D :] + tn(region_in_all, terms[:, D:])).astype(bf16).reshape(shape)
        low_second[:, :, :, D:] = out_low.reshape(shape)
        slot(4)


def gelu_both(v):
    e = jnp.exp2(v * v * (-0.5 * LOG2E))
    cdf = 0.5 + 0.5 * lax.erf(v * (0.5**0.5))
    return v * cdf, cdf + v * e * 0.3989422804014327


def with_region(block, region, last):
    tokens, count, width = block.shape
    head = block[0 : tokens - 1].reshape((tokens - 1) * count, width)
    tail = jnp.where(last, region, block[tokens - 1])
    return jnp.concatenate([head, tail], axis=0)


def mlp_kernel(
    patches, region_mid, merged, patch_cot, region_cot, vecs, w_out, w_up, w_down,
    patch_out, region_out, grad_middle, grad_merged, up_grad, down_grad_t, out_grad, vec512, up_bias_grad,
    up_acc, down_acc,
):
    step = pl.program_id(0)
    last = step == pl.num_programs(0) - 1
    tokens, count, _ = patches.shape
    rows = tokens * count

    @pl.when(step == 0)
    def _():
        up_acc[...] = jnp.zeros_like(up_acc)
        down_acc[...] = jnp.zeros_like(down_acc)
        out_grad[...] = jnp.zeros_like(out_grad)
        vec512[...] = jnp.zeros_like(vec512)
        up_bias_grad[...] = jnp.zeros_like(up_bias_grad)

    x = with_region(patches[...].astype(f32), region_mid[...], last)
    grad_result = with_region(patch_cot[...], region_cot[...], last)
    low_merged = merged[...].reshape(rows, D)
    middle = x + nn(low_merged, w_out[...]) + row(vecs, OUT_BIAS)
    vhat, inverse = norm_stats(middle)
    mlp_in = normed_low(vhat, vecs, GAIN2, SHIFT2)
    mlp_in_t = mlp_in.T
    grad_result_t = grad_result.T
    result = middle + row(vecs, DOWN_BIAS)
    grad_in = jnp.zeros((rows, D), f32)
    for f in range(FF // 512):
        at = slice(512 * f, 512 * f + 512)
        hidden = nn(mlp_in, w_up[:, at]) + row(vecs, UP_BIAS + f)
        active, slope = gelu_both(hidden)
        active = active.astype(bf16)
        grad_hidden = (nt(grad_result, w_down[at, :]) * slope).astype(bf16)
        result += nn(active, w_down[at, :])
        grad_in += nt(grad_hidden, w_up[:, at])
        up_acc[:, at] += nn(mlp_in_t, grad_hidden)
        down_acc[:, at] += nn(grad_result_t, active)
        up_bias_grad[:, at] += col(grad_hidden.astype(f32))
    shown = result.astype(bf16)
    patch_out[...] = shown.reshape(tokens, count, D)
    region_out[...] = shown[rows - count :]
    gm = grad_result.astype(f32) + norm_back(vhat, inverse, row(vecs, GAIN2), grad_in)
    low_gm = gm.astype(bf16)
    grad_middle[...] = low_gm.reshape(tokens, count, D)
    out_grad[...] += nn(low_merged.T, low_gm)
    grad_merged[...] = nt(low_gm, w_out[...]).astype(bf16).reshape(tokens, count, D)
    vec512[0:1] += col(grad_in * vhat)
    vec512[1:2] += col(grad_in)
    vec512[2:3] += col(low_gm.astype(f32))
    vec512[3:4] += col(grad_result.astype(f32))

    @pl.when(last)
    def _():
        up_grad[...] = up_acc[...].astype(bf16)
        down_grad_t[...] = down_acc[...].astype(bf16)


def tail_kernel(
    wins, dps,
    patches, grad_triple, grad_middle, region_mid, vecs, w_qkv, terms, grad_query,
    regional, grad_mid, vec_mlp, up_bias_grad, sums, out_bias_part, up_part, down_part, first_source, second_source,
    patch_grad, region_grad, small_sum, up_sum, down_sum, first_sum, second_sum,
    vec, halves, half_sem, summed, pieces, piece_sem, pack, near, near_sem, total, far, far_sem, *streams,
):
    step = pl.program_id(0)
    tokens, count, _ = patches.shape
    rows = tokens * count
    place = Place(wins, dps)
    parts = [streams[Stream.PARTS * b : Stream.PARTS * (b + 1)] for b in range(4)]
    late = (Stream(place, first_source, first_sum, parts[0]), Stream(place, second_source, second_sum, parts[1]))
    early = (Stream(place, None, up_sum, parts[2]), Stream(place, None, down_sum, parts[3]))

    def window_rows(chip, core):
        return pl.ds(pl.multiple_of((chip * 2 + core) * count, 16), count)

    def to_core():
        return [pltpu.make_async_remote_copy(
            src_ref=terms.at[window_rows(chip, 1 - place.core)], dst_ref=halves.at[chip],
            send_sem=half_sem.at[2 * chip], recv_sem=half_sem.at[2 * chip + 1],
            device_id=place.other_core(), device_id_type=MESH,
        ) for chip in range(place.chips)]

    def to_owners():
        copies = []
        for j in range(1, place.chips):
            chip, to = place.at_chip(j)
            copies.append(pltpu.make_async_remote_copy(
                src_ref=summed.at[chip], dst_ref=pieces.at[j - 1],
                send_sem=piece_sem.at[2 * j - 2], recv_sem=piece_sem.at[2 * j - 1], device_id=to, device_id_type=MESH,
            ))
        return copies

    def to_near():
        return [pltpu.make_async_remote_copy(
            src_ref=pack, dst_ref=near.at[j - 1], send_sem=near_sem.at[2 * j - 2], recv_sem=near_sem.at[2 * j - 1],
            device_id={"win": lax.rem(place.win + j, wins)}, device_id_type=MESH,
        ) for j in range(1, wins)]

    def to_far():
        return [pltpu.make_async_remote_copy(
            src_ref=total, dst_ref=far.at[j - 1], send_sem=far_sem.at[2 * j - 2], recv_sem=far_sem.at[2 * j - 1],
            device_id=place.at_dp(j)[1], device_id_type=MESH,
        ) for j in range(1, dps)]

    def late_step(k):
        for s in late:
            s.step(k)

    def early_step(k):
        for s in early:
            s.step(k)

    def begin():
        place.greeted(all_wins=True)
        late_step(0)
        for c in to_core():
            c.start()
        for s, part in zip(early, (up_part, down_part)):
            s.begin_back(part)

    def owners_begin():
        for c in to_core():
            c.wait()

        def add(chip, carry):
            own = terms[window_rows(chip, place.core)].astype(f32)
            summed[chip] = (own + halves[chip].astype(f32)).astype(bf16)
            return carry

        lax.fori_loop(0, place.chips, add, 0)
        for c in to_owners():
            c.start()

    def region_end():
        for c in to_owners():
            c.wait()
        key_value = summed[place.chip].astype(f32)
        for j in range(place.chips - 1):
            key_value += pieces[j].astype(f32)
        vhat, inverse = norm_stats(regional[...].astype(f32))
        grad_in = nt(grad_query[...], w_qkv[:, :D]) + nt(key_value.astype(bf16), w_qkv[:, D:])
        region_grad[...] = (grad_mid[...] + norm_back(vhat, inverse, row(vecs, GAIN1), grad_in)).astype(bf16)
        vec[0:1] += col(grad_in * vhat)
        vec[1:2] += col(grad_in)

    def small_begin():
        pack[0:2] = vec[0:2]
        pack[2:3] = sums[:, :D]
        pack[3:4] = sums[:, 2 * D :]
        pack[4:5] = vec_mlp[2:3] + out_bias_part[...]
        pack[5:7] = vec_mlp[0:2]
        pack[7:8] = vec_mlp[3:4]
        for b in range(4):
            pack[8 + b : 9 + b] = up_bias_grad[:, D * b : D * (b + 1)]
        pack[12:16] = jnp.zeros((4, D), f32)
        for c in to_near():
            c.start()

    def small_middle():
        for c in to_near():
            c.wait()
        part = pack[...]
        for j in range(wins - 1):
            part += near[j]
        total[...] = part
        for c in to_far():
            c.start()

    def small_end():
        for c in to_far():
            c.wait()
        part = total[...]
        for j in range(dps - 1):
            part += far[j]
        small_sum[...] = part

    @pl.when(step == 0)
    def _():
        place.greet(all_wins=True)
        for s in late:
            s.load()
        vec[...] = jnp.zeros_like(vec)
        begin()

    x = with_region(patches[...].astype(f32), region_mid[...], step == pl.num_programs(0) - 1)
    vhat, inverse = norm_stats(x)
    grad_in = nt(grad_triple[...].reshape(rows, 3 * D), w_qkv[...])
    vec[0:1] += col(grad_in * vhat)
    vec[1:2] += col(grad_in)
    total_rows = grad_middle[...].reshape(rows, D).astype(f32) + norm_back(vhat, inverse, row(vecs, GAIN1), grad_in)
    patch_grad[...] = total_rows.astype(bf16).reshape(tokens, count, D)

    def end():
        late_step(3)
        owners_begin()
        early_step(5)
        late_step(4)
        early_step(6)
        region_end()
        small_begin()
        late_step(5)
        small_middle()
        late_step(6)
        early_step(7)
        small_end()
        late_step(7)
        early_step(8)
        late_step(8)

    hooks = {
        0: lambda: late_step(1),
        3: lambda: late_step(2),
        4: end,
    }
    for when, todo in hooks.items():
        pl.when(step == when)(todo)


def last_kernel(
    up, down_t, first, second, small, patch_in, region_in,
    patch_grad, region_grad, in_gain, in_shift, qkv, qkv_bias, out_grad, out_bias, mlp_gain, mlp_shift,
    up_grad, up_bias, down_grad, down_bias,
):
    up_grad[...] = up[...].astype(f32)
    down_grad[...] = down_t[...].T.astype(f32)
    qkv[:, : 2 * D] = first[...].astype(f32)
    qkv[:, 2 * D :] = second[:, :D].astype(f32)
    out_grad[...] = second[:, D:].astype(f32)
    patch_grad[...] = patch_in[...]

    @pl.when(pl.program_id(0) == 0)
    def _():
        region_grad[...] = region_in[...]
        for at, v in ((0, in_gain), (1, in_shift), (4, out_bias), (5, mlp_gain), (6, mlp_shift), (7, down_bias)):
            v[...] = small[at : at + 1].reshape(D)
        qkv_bias[...] = small[2:4]
        up_bias[...] = jnp.concatenate([small[8 + b : 9 + b] for b in range(FF // D)], axis=1).reshape(FF)


def shards(
    wins, dps,
    patches, regional, window_image, in_gain, in_shift, w_qkv, qkv_bias, w_out, out_bias,
    mlp_gain, mlp_shift, w_up, up_bias, w_down, down_bias, patch_cot, region_cot,
):
    _, count, patch, _ = patches.shape
    group = window_image.shape[1]
    x = patches[0].transpose(1, 0, 2)
    cot = patch_cot[0].transpose(1, 0, 2)
    reg = regional[0]
    rcot = region_cot[0]
    const = lambda *arrays: [whole(a) for a in arrays]
    block = lambda a, n: (a, (n,) + a.shape[1:], lambda i: (i, 0, 0))
    block_out = lambda shape, n, dtype=bf16: ((shape, dtype), (n,) + shape[1:], lambda i: (i, 0, 0))
    triple, local_in, vecs, region_triple, gathered, probs_r, merged_r, region_mid, triple0, local_in0 = call(
        functools.partial(front_kernel, wins, dps), (pl.cdiv(patch, 7),),
        [block(x, 7)]
        + const(reg, window_image, in_gain, in_shift, w_qkv, qkv_bias, w_out, out_bias, mlp_gain, mlp_shift, up_bias, down_bias),
        [block_out((patch, count, 3 * D), 7), block_out((patch, count, D), 7), whole_out((16, D), f32), whole_out((count, 3 * D), bf16),
         whole_out((group, 3 * D), bf16), whole_out((2, group, 8 * count), bf16), whole_out((count, D), bf16),
         whole_out((count, D), f32), whole_out((count, 3 * D), bf16), whole_out((count, D), bf16)],
        [pltpu.VMEM((group, 3 * D), bf16), pltpu.VMEM((count, 3 * D), bf16), pltpu.VMEM((group, 128), f32),
         pltpu.SemaphoreType.DMA((2 * wins,))],
        name="front", collective_id=2,
    )
    steps = (count // WC,)
    mid = lambda a: (a, (a.shape[0], WC, a.shape[2]), lambda i: (0, i, 0))
    mid_out = lambda shape, dtype=bf16: ((shape, dtype), (shape[0], WC, shape[2]), lambda i: (0, i, 0))
    tail = lambda a: (a, (WC, a.shape[1]), lambda i: (i, 0))
    merged, probs = call(
        local_fwd_kernel, steps, [mid(triple), tail(triple0)],
        [mid_out((patch + 1, count, D)), ((((count, TP, HEADS * TP)), bf16), (WC, TP, HEADS * TP), lambda i: (i, 0, 0))],
        [pltpu.VMEM((12, TP * WC, 128), f32), pltpu.VMEM((4, TP * WC, 128), f32)], name="local_fwd",
    )
    n = 10
    rows_grid = ((patch + 1) // n,)
    patch_out, region_out, grad_middle, grad_merged, up_grad, down_grad_t, out_local, vec_mlp, up_bias_grad = call(
        mlp_kernel, rows_grid,
        [block(x, n), whole(region_mid), block(merged, n), block(cot, n)]
        + const(rcot, vecs, w_out, w_up, w_down),
        [block_out((patch, count, D), n), whole_out((count, D), bf16),
         block_out((patch + 1, count, D), n), block_out((patch + 1, count, D), n),
         whole_out((D, FF), bf16), whole_out((D, FF), bf16), whole_out((D, D), f32),
         whole_out((8, D), f32), whole_out((1, FF), f32)],
        [pltpu.VMEM((D, FF), f32), pltpu.VMEM((D, FF), f32)], name="mlp",
    )
    last_rows = rows_of(wins, dps)[1]
    grad_triple, up_part, down_part, terms, grad_query, low_first, low_second, sums, out_bias_part, grad_mid = call(
        functools.partial(back_kernel, wins, dps), steps,
        [mid(triple), tail(triple0), (probs, (WC, TP, HEADS * TP), lambda i: (i, 0, 0), group > 512), mid(grad_merged), mid(local_in), tail(local_in0)]
        + const(region_triple, gathered, probs_r, merged_r, region_mid)
        + [(grad_middle, (1, count, D), lambda i: (patch, 0, 0))]
        + const(vecs, w_qkv, w_out, out_local) + [left(a.reshape(stream_shape(wins, FF))) for a in (up_grad, down_grad_t)],
        [mid_out((patch + 1, count, 3 * D)), whole_out((last_rows, FF), bf16), whole_out((last_rows, FF), bf16),
         whole_out((group, 2 * D), bf16), whole_out((count, D), bf16), whole_out(stream_shape(wins, 2 * D), bf16),
         whole_out(stream_shape(wins, 2 * D), bf16),
         whole_out((1, 3 * D), f32), whole_out((1, D), f32), whole_out((count, D), f32)],
        [pltpu.VMEM((16, TP * WC, 128), f32), pltpu.VMEM((12, TP * WC, 128), f32), pltpu.VMEM((count, 3 * D), bf16),
         pltpu.VMEM((D, 3 * D), f32), pltpu.VMEM((count, D), bf16)]
        + stream_scratch(wins, dps, FF, "down") * 2,
        name="back", collective_id=0,
    )
    patch_grad, region_grad, small, up_sum, down_sum, first_sum, second_sum = call(
        functools.partial(tail_kernel, wins, dps), rows_grid,
        [block(x, n), block(grad_triple, n), block(grad_middle, n)]
        + const(region_mid, vecs, w_qkv, terms, grad_query, reg, grad_mid, vec_mlp, up_bias_grad, sums, out_bias_part, up_part, down_part)
        + [left(low_first), left(low_second)],
        [block_out((patch, count, D), n), whole_out((count, D), bf16), whole_out((16, D), f32)]
        + [left_out(stream_shape(wins, FF), bf16)] * 2 + [left_out(stream_shape(wins, 2 * D), bf16)] * 2,
        [pltpu.VMEM((8, D), f32),
         pltpu.VMEM((wins // 2, count, 2 * D), bf16), pltpu.SemaphoreType.DMA((wins,)), pltpu.VMEM((wins // 2, count, 2 * D), bf16),
         pltpu.VMEM((wins // 2, count, 2 * D), bf16), pltpu.SemaphoreType.DMA((wins,)),
         pltpu.VMEM((16, D), f32), pltpu.VMEM((wins - 1, 16, D), f32), pltpu.SemaphoreType.DMA((2 * wins,)),
         pltpu.VMEM((16, D), f32), pltpu.VMEM((max(dps - 1, 1), 16, D), f32), pltpu.SemaphoreType.DMA((2 * dps,))]
        + stream_scratch(wins, dps, 2 * D) * 2 + stream_scratch(wins, dps, FF, "back") * 2,
        name="tail", collective_id=1,
    )
    up_sum, down_sum = up_sum.reshape(D, FF), down_sum.reshape(D, FF)
    first_sum, second_sum = first_sum.reshape(D, 2 * D), second_sum.reshape(D, 2 * D)
    n = 8
    down = lambda i: (i, 0)
    vector = lambda size: ((((size,), f32)), (size,), lambda i: (0,))
    token = -(-patch // n)
    tokens = lambda i: (lax.min(i, (patch - 1) // token), 0, 0)
    (
        patch_grad, region_grad, in_gain_grad, in_shift_grad, qkv_grad, qkv_bias_grad, out_grad, out_bias_grad,
        mlp_gain_grad, mlp_shift_grad, up_grad, up_bias_grad, down_grad, down_bias_grad,
    ) = call(
        last_kernel, (n,),
        [(up_sum, (D // n, FF), down), (down_sum, (D, FF // n), lambda i: (0, i))]
        + [(a, (D // n, 2 * D), down) for a in (first_sum, second_sum)]
        + [whole(small), (patch_grad, (token, count, D), tokens), whole(region_grad)],
        [(((patch, count, D), bf16), (token, count, D), tokens), whole_out((count, D), bf16), vector(D), vector(D),
         (((D, 3 * D), f32), (D // n, 3 * D), down), whole_out((2, D), f32), (((D, D), f32), (D // n, D), down), vector(D),
         vector(D), vector(D), (((D, FF), f32), (D // n, FF), down), vector(FF), (((FF, D), f32), (FF // n, D), down), vector(D)],
        name="last",
    )
    return (
        patch_out.transpose(1, 0, 2)[None], region_out[None], patch_grad.transpose(1, 0, 2)[None], region_grad[None],
        in_gain_grad, in_shift_grad, qkv_grad, qkv_bias_grad, out_grad, out_bias_grad,
        mlp_gain_grad, mlp_shift_grad, up_grad, up_bias_grad, down_grad, down_bias_grad,
    )


def solution(mesh):
    wide = P("dp", "win", None, None)
    narrow = P("dp", "win", None)
    in_specs = (wide, narrow, P("dp", None)) + (P(),) * 12 + (wide, narrow)
    out_specs = (wide, narrow, wide, narrow) + (P(),) * 12
    return jax.shard_map(functools.partial(shards, mesh.shape["win"], mesh.shape["dp"]), mesh=mesh, in_specs=in_specs, out_specs=out_specs, check_vma=False)
```

```python
import functools

import jax
import jax.numpy as jnp
from jax import lax
from jax.experimental import pallas as pl
from jax.experimental.pallas import tpu as pltpu
from jax.sharding import PartitionSpec as P

D = 512
HEADS = 16
HD = 32
FF = 2048
EPSILON = 1e-06
MASKED_SCORE = -1e30
SCALING = HD ** (-0.5)
LOG2E = 1.4426950408889634
TP = 64
FB = 2048
WC = 16
f32 = jnp.float32
bf16 = jnp.bfloat16
VMEM_LIMIT = 60 * 2**20
MESH = pl.DeviceIdType.MESH
BACK_SLOTS = (
    (0, 0, (0,), (0,)), (0, 6, (1,), ()), (0, 16, (), (1,)), (1, 7, (2,), ()), (1, 16, (3,), (2,)), (2, 7, (), (3,)),
)


def nn(a, b):
    return lax.dot_general(a, b, (((1,), (0,)), ((), ())), preferred_element_type=f32)


def nt(a, b):
    return lax.dot_general(a, b, (((1,), (1,)), ((), ())), preferred_element_type=f32)


def tn(a, b):
    return lax.dot_general(a, b, (((0,), (0,)), ((), ())), preferred_element_type=f32)


def call(body, grid, ins, outs, scratch=(), name=None, collective_id=None, limit=VMEM_LIMIT):
    def spec(block, index, *single):
        if block is None:
            return pl.BlockSpec(memory_space=pl.ANY)
        if index is None:
            return pl.BlockSpec(block, lambda *_: (0,) * len(block), pipeline_mode=pl.Buffered(1))
        return pl.BlockSpec(block, index, pipeline_mode=pl.Buffered(1) if any(single) else None)

    return pl.pallas_call(
        body,
        grid=grid,
        in_specs=[spec(*entry[1:]) for entry in ins],
        out_specs=[spec(b, i) for _, b, i in outs],
        out_shape=[jax.ShapeDtypeStruct(s, d) for (s, d), _, _ in outs],
        scratch_shapes=list(scratch),
        compiler_params=pltpu.CompilerParams(
            vmem_limit_bytes=limit, collective_id=collective_id, has_side_effects=collective_id is not None
        ),
        name=name,
    )(*[entry[0] for entry in ins])


def whole(a):
    return (a, a.shape, None)


def whole_out(shape, dtype):
    return ((shape, dtype), shape, None)


def left(a):
    return (a, None, None)


def left_out(shape, dtype):
    return ((shape, dtype), None, None)


def norm_stats(rows):
    average = jnp.mean(rows, axis=-1, keepdims=True)
    centred = rows - average
    spread = jnp.mean(centred * centred, axis=-1, keepdims=True)
    inverse = lax.rsqrt(spread + EPSILON)
    return centred * inverse, inverse


def norm_back(vhat, inverse, gain, grad_out):
    scaled = grad_out * gain
    first = jnp.mean(scaled, axis=-1, keepdims=True)
    second = jnp.mean(scaled * vhat, axis=-1, keepdims=True)
    return inverse * (scaled - first - vhat * second)


def col(x):
    return jnp.sum(x, axis=0, keepdims=True)


class Place:
    def __init__(self, wins, dps):
        self.wins, self.dps = wins, dps
        self.win = lax.axis_index("win")
        self.dp = lax.axis_index("dp")
        self.core = lax.rem(self.win, 2)
        self.chip = self.win // 2
        self.chips = wins // 2
        self.square = self.chips == 4
        self.a = self.chip // 2
        self.b = lax.rem(self.chip, 2)

    def other_core(self):
        return {"win": self.chip * 2 + 1 - self.core}

    def other_a(self):
        return {"win": ((1 - self.a) * 2 + self.b) * 2 + self.core}

    def other_b(self):
        return {"win": (self.a * 2 + 1 - self.b) * 2 + self.core}

    def at_chip(self, j):
        chip = lax.rem(self.chip + j, self.chips)
        return chip, {"win": chip * 2 + self.core}

    def at_dp(self, j):
        dp = lax.rem(self.dp + j, self.dps)
        return dp, {"dp": dp}

    def near(self, all_wins):
        if all_wins:
            return [{"win": lax.rem(self.win + j, self.wins)} for j in range(1, self.wins)]
        if self.square:
            return [self.other_core(), self.other_a(), self.other_b()]
        return [self.other_core()] + [self.at_chip(j)[1] for j in range(1, self.chips)]

    def partners(self, all_wins, along):
        return self.near(all_wins) + [self.at_dp(j)[1] for j in range(1, self.dps if along else 1)]

    def greet(self, all_wins=False, along=True):
        barrier = pltpu.get_barrier_semaphore()
        for to in self.partners(all_wins, along):
            pl.semaphore_signal(barrier, inc=1, device_id=to, device_id_type=MESH)

    def greeted(self, all_wins=False, along=True):
        pl.semaphore_wait(pltpu.get_barrier_semaphore(), len(self.partners(all_wins, along)))


def rows_of(wins, dps):
    piece = D // wins
    return piece, piece // dps if piece % (16 * dps) == 0 else piece


def stream_shape(wins, columns):
    return (2, wins // 2, D // wins, columns)


def stream_scratch(wins, dps, columns, kind="whole"):
    piece, last = rows_of(wins, dps)
    chips = wins // 2
    landing = (4, 2, piece, columns // 2) if chips == 4 else (max(chips - 1, 1), piece, columns)
    half, part, some = pltpu.VMEM((chips, piece, columns), bf16), pltpu.VMEM((piece, columns), bf16), pltpu.VMEM((16, 128), bf16)
    down = kind != "back"
    return [
        half if down else some,
        half,
        pltpu.VMEM(landing, bf16) if down else some,
        part if down else some,
        pltpu.VMEM((max(dps - 1, 1), last, columns), bf16) if down else some,
        some if kind == "down" else part,
        pltpu.SemaphoreType.DMA((20 + 4 * chips + 4 * dps,)),
    ]


def columns_of(refs):
    return refs[1].shape[2]


class Stream:
    PARTS = 7

    def __init__(self, place, source, final, refs):
        self.p = place
        self.source, self.final = source, final
        self.own, self.r1, self.r2, self.s, self.r3, self.s2, self.sem = refs
        self.piece, self.last = rows_of(place.wins, place.dps)
        self.split = self.last != self.piece
        columns = columns_of(refs)
        self.left, self.right = pl.ds(0, columns // 2), pl.ds(columns // 2, columns // 2)

    def rows(self, start, size):
        return pl.ds(pl.multiple_of(start, 16), size)

    def remote(self, src, dst, to, k):
        return pltpu.make_async_remote_copy(
            src_ref=src, dst_ref=dst, send_sem=self.sem.at[2 * k], recv_sem=self.sem.at[2 * k + 1],
            device_id=to, device_id_type=MESH,
        )

    def _own(self):
        return pltpu.make_async_copy(self.source.at[self.p.core], self.own, self.sem.at[0])

    def _put(self):
        return pltpu.make_async_copy(self.r1, self.final.at[self.p.core], self.sem.at[1])

    def _cores(self):
        return [self.remote(self.source.at[1 - self.p.core], self.r1, self.p.other_core(), 1)]

    def _cores_back(self):
        return [self.remote(self.r1, self.final.at[self.p.core], self.p.other_core(), 2)]

    def _chips_left(self, k):
        p = self.p
        if k == 0:
            return [self.remote(self.own.at[c * 2 + 1 - p.b, :, self.left], self.r2.at[0, c], p.other_b(), 3 + c) for c in range(2)]
        return [self.remote(self.own.at[(1 - p.a) * 2 + p.b, :, self.left], self.r2.at[2, 0], p.other_a(), 5)]

    def _chips_right(self, k):
        p = self.p
        if k == 0:
            return [self.remote(self.own.at[(1 - p.a) * 2 + c, :, self.right], self.r2.at[1, c], p.other_a(), 6 + c) for c in range(2)]
        return [self.remote(self.own.at[p.a * 2 + 1 - p.b, :, self.right], self.r2.at[3, 0], p.other_b(), 8)]

    def _back_left(self, k):
        p = self.p
        mine = self.r1
        if k == 0:
            return [self.remote(self.s2.at[:, self.left], mine.at[p.chip, :, self.left], p.other_a(), 9)]
        rows = [mine.at[c * 2 + p.b, :, self.left] for c in range(2)]
        return [self.remote(rows[c], rows[c], p.other_b(), 10 + c) for c in range(2)]

    def _back_right(self, k):
        p = self.p
        mine = self.r1
        if k == 0:
            return [self.remote(self.s2.at[:, self.right], mine.at[p.chip, :, self.right], p.other_b(), 12)]
        rows = [mine.at[p.a * 2 + c, :, self.right] for c in range(2)]
        return [self.remote(rows[c], rows[c], p.other_a(), 13 + c) for c in range(2)]

    def _chips(self):
        out = []
        for j in range(1, self.p.chips):
            chip, to = self.p.at_chip(j)
            out.append(self.remote(self.own.at[chip], self.r2.at[j - 1], to, 2 + j))
        return out

    def _chips_back(self):
        out = []
        for j in range(1, self.p.chips):
            mine = self.r1.at[self.p.chip]
            out.append(self.remote(self.s2, mine, self.p.at_chip(j)[1], 2 + self.p.chips + j))
        return out

    def _dps(self):
        out = []
        for j in range(1, self.p.dps):
            dp, to = self.p.at_dp(j)
            src = self.s.at[self.rows(dp * self.last, self.last)] if self.split else self.s
            out.append(self.remote(src, self.r3.at[j - 1], to, 8 + 2 * self.p.chips + j))
        return out

    def _dps_back(self):
        out = []
        if self.split:
            for j in range(1, self.p.dps):
                mine = self.s2.at[self.rows(self.p.dp * self.last, self.last)]
                out.append(self.remote(mine, mine, self.p.at_dp(j)[1], 8 + 2 * self.p.chips + self.p.dps + j))
        return out

    def start(self, copies):
        for c in copies:
            c.start()

    def wait(self, copies):
        for c in copies:
            c.wait()

    def load(self):
        self._own().start()

    def send_cores(self):
        self.start(self._cores())

    def send_chips(self):
        self._own().wait()
        self.wait(self._cores())

        def add(i, carry):
            self.own[i] = (self.own[i].astype(f32) + self.r1[i].astype(f32)).astype(bf16)
            return carry

        lax.fori_loop(0, self.p.chips, add, 0)
        if self.p.square:
            self.start(self._chips_left(0))
            self.start(self._chips_right(0))
        else:
            self.start(self._chips())

    def add_square(self, chip, lanes, slot, c):
        self.own[chip, :, lanes] = (self.own[chip, :, lanes].astype(f32) + self.r2[slot, c].astype(f32)).astype(bf16)

    def send_chips_again(self):
        p = self.p
        if p.square:
            self.wait(self._chips_left(0))
            for c in range(2):
                self.add_square(c * 2 + p.b, self.left, 0, c)
            self.start(self._chips_left(1))
            self.wait(self._chips_right(0))
            for c in range(2):
                self.add_square(p.a * 2 + c, self.right, 1, c)
            self.start(self._chips_right(1))

    def send_dps(self):
        p = self.p
        if p.square:
            for lanes, slot, copies in ((self.left, 2, self._chips_left(1)), (self.right, 3, self._chips_right(1))):
                self.wait(copies)
                self.s[:, lanes] = (self.own[p.chip, :, lanes].astype(f32) + self.r2[slot, 0].astype(f32)).astype(bf16)
        else:
            self.wait(self._chips())
            total = self.own[p.chip].astype(f32)
            for j in range(p.chips - 1):
                total += self.r2[j].astype(f32)
            self.s[...] = total.astype(bf16)
        self.start(self._dps())

    def sum_dps(self, out, at):
        self.wait(self._dps())
        mine = self.part()
        total = self.s[mine].astype(f32)
        for j in range(self.p.dps - 1):
            total += self.r3[j].astype(f32)
        out[at] = total.astype(bf16)

    def part(self):
        return self.rows(self.p.dp * self.last if self.split else 0, self.last)

    def send_dps_back(self):
        self.sum_dps(self.s2, self.part())
        self.start(self._dps_back())

    def end_dps_back(self):
        self.wait(self._dps_back())

    def begin_back(self, part):
        self.s2[self.part()] = part[...]
        self.start(self._dps_back())

    def send_chips_back(self):
        self.end_dps_back()
        self.start_chips_back()

    def start_chips_back(self):
        self.r1[self.p.chip] = self.s2[...]
        if self.p.square:
            self.start(self._back_left(0))
            self.start(self._back_right(0))
        else:
            self.start(self._chips_back())

    def send_chips_back_again(self):
        if self.p.square:
            self.wait(self._back_left(0))
            self.start(self._back_left(1))
            self.wait(self._back_right(0))
            self.start(self._back_right(1))
        else:
            self.wait(self._chips_back())

    def send_cores_back(self):
        if self.p.square:
            self.wait(self._back_left(1))
            self.wait(self._back_right(1))
        self.start(self._cores_back())
        self._put().start()

    def finish(self):
        self.wait(self._cores_back())
        self._put().wait()

    STEPS = (
        "send_cores", "send_chips", "send_chips_again", "send_dps", "send_dps_back",
        "send_chips_back", "send_chips_back_again", "send_cores_back", "finish",
    )

    def step(self, k):
        if 0 <= k < len(self.STEPS):
            getattr(self, self.STEPS[k])()


def expand_group(x, heads):
    lane = lax.broadcasted_iota(jnp.int32, (1, x.shape[1]), 1) // HD
    return jnp.concatenate([jnp.where(lane == i, x, jnp.zeros_like(x)) for i in range(heads)], axis=0)


def fold_group(y, heads):
    rows = y.shape[0] // heads
    lane = lax.broadcasted_iota(jnp.int32, (1, y.shape[1]), 1) // HD
    total = y[(heads - 1) * rows :]
    for i in range(heads - 2, -1, -1):
        total = jnp.where(lane == i, y[i * rows : (i + 1) * rows], total)
    return total


GAIN1, SHIFT1, GAIN2, SHIFT2, OUT_BIAS, DOWN_BIAS, QUERY_BIAS, KEY_BIAS, VALUE_BIAS, UP_BIAS = range(10)


def row(vecs, at):
    return vecs[at : at + 1]


def normed_low(vhat, vecs, gain, shift):
    return (vhat * row(vecs, gain) + row(vecs, shift)).astype(bf16)


def front_kernel(
    wins, dps,
    patches, regional, images, in_gain, in_shift, w_qkv, qkv_bias, w_out, out_bias, mlp_gain, mlp_shift, up_bias, down_bias,
    triple, local_in, vecs, region_triple, gathered_out, probs, merged, region_mid, triple0, local_in0,
    gathered, packed, image_col, sem,
):
    step = pl.program_id(0)
    place = Place(wins, dps)
    count = regional.shape[0]
    group = gathered.shape[0]
    mine = pl.ds(pl.multiple_of(place.win * count, 16), count)

    def project(normed):
        out = nn(normed, w_qkv[...])
        return jnp.concatenate(
            [out[:, :D] + row(vecs, QUERY_BIAS), out[:, D : 2 * D], out[:, 2 * D :] + row(vecs, VALUE_BIAS)], axis=1
        ).astype(bf16)

    def sends():
        copies = []
        for j in range(1, wins):
            copies.append(pltpu.make_async_remote_copy(
                src_ref=packed, dst_ref=gathered.at[mine], send_sem=sem.at[2 * j - 2], recv_sem=sem.at[2 * j - 1],
                device_id={"win": lax.rem(place.win + j, wins)}, device_id_type=MESH,
            ))
        return copies

    @pl.when(step == 0)
    def _():
        place.greet(all_wins=True, along=False)
        for at, v in (
            (GAIN1, in_gain), (SHIFT1, in_shift), (GAIN2, mlp_gain), (SHIFT2, mlp_shift), (OUT_BIAS, out_bias), (DOWN_BIAS, down_bias),
        ):
            vecs[at : at + 1] = v[...].astype(f32).reshape(1, D)
        vecs[QUERY_BIAS : QUERY_BIAS + 1] = qkv_bias[0:1].astype(f32)
        vecs[KEY_BIAS : KEY_BIAS + 1] = jnp.zeros((1, D), f32)
        vecs[VALUE_BIAS : VALUE_BIAS + 1] = qkv_bias[1:2].astype(f32)
        up = up_bias[...].astype(f32).reshape(1, FF)
        for b in range(FF // D):
            vecs[UP_BIAS + b : UP_BIAS + b + 1] = up[:, D * b : D * (b + 1)]
        vecs[UP_BIAS + FF // D : 16] = jnp.zeros((16 - UP_BIAS - FF // D, D), f32)
        vhat, _ = norm_stats(regional[...].astype(f32))
        normed = normed_low(vhat, vecs, GAIN1, SHIFT1)
        own = project(normed)
        region_triple[...] = own
        packed[:, : 2 * D] = own[:, D:]
        packed[:, 2 * D :] = normed
        gathered[mine] = packed[...]
        place.greeted(all_wins=True, along=False)
        for c in sends():
            c.start()
        ids = images[...].astype(f32)
        image_col[...] = jnp.broadcast_to(ids, (128, group)).T

    rows = patches.shape[0] * count
    vhat, _ = norm_stats(patches[...].reshape(rows, D).astype(f32))
    normed_rows = normed_low(vhat, vecs, GAIN1, SHIFT1)
    local_in[...] = normed_rows.reshape(local_in.shape)
    triple[...] = project(normed_rows).reshape(triple.shape)

    @pl.when(step == pl.num_programs(0) - 1)
    def _():
        for c in sends():
            c.wait()
        gathered_out[...] = gathered[...]
        own_ids = image_col[mine]
        own_row = jnp.concatenate([own_ids] * 8, axis=0).T[0:1]
        same = image_col[:, 0:1] == own_row
        for g in range(2):
            lanes = slice(256 * g, 256 * g + 256)
            scores = nt(gathered[:, lanes], expand_group(region_triple[:, lanes], 8))
            scores = jnp.where(same, scores * SCALING, MASKED_SCORE)
            top = jnp.max(scores, axis=0, keepdims=True)
            exps = jnp.exp2((scores - top) * LOG2E)
            low = (exps * (1.0 / col(exps))).astype(bf16)
            probs[g] = low
            merged[:, lanes] = fold_group(tn(low, gathered[:, D + 256 * g : D + 256 * g + 256]), 8).astype(bf16)
        mid = regional[...].astype(f32) + nn(merged[...], w_out[...]) + row(vecs, OUT_BIAS)
        region_mid[...] = mid
        vhat_mid, _ = norm_stats(mid)
        normed_mid = normed_low(vhat_mid, vecs, GAIN1, SHIFT1)
        local_in0[...] = normed_mid
        triple0[...] = project(normed_mid)


def expand(x):
    lane = lax.broadcasted_iota(jnp.int32, (1, 128), 1) // HD
    return jnp.concatenate([jnp.where(lane == i, x, jnp.zeros_like(x)) for i in range(4)], axis=0)


def query_side(rows, weights):
    lane = lax.broadcasted_iota(jnp.int32, (1, 128), 1) // HD
    out = tn(rows, weights)
    pairs = jnp.concatenate([out[0:64, 0:128], out[64:128, 128:256]], axis=0).T
    return jnp.where(lane % 2 == 0, pairs[0:64], pairs[64:128])


def load_triple(t, triple, triple0, patch):
    for b in range(12):
        lanes = slice(128 * b, 128 * b + 128)
        t[b, 0 : patch * WC] = triple[:, :, lanes].reshape(patch * WC, 128).astype(f32)
        t[b, patch * WC : (patch + 1) * WC] = triple0[:, lanes].astype(f32)
        t[b, (patch + 1) * WC :] = jnp.zeros(((TP - patch - 1) * WC, 128), f32)


def local_fwd_kernel(triple, triple0, merged, probs, t, m):
    patch = triple.shape[0]
    load_triple(t, triple, triple0, patch)
    row = lax.broadcasted_iota(jnp.int32, (TP, 1), 0)

    def one(w):
        for b in range(4):
            q = t[b, pl.ds(w, TP, stride=WC), :].astype(bf16)
            k = t[4 + b, pl.ds(w, TP, stride=WC), :].astype(bf16)
            v = t[8 + b, pl.ds(w, TP, stride=WC), :].astype(bf16)
            scores = nt(k, expand(q))
            scores = jnp.where(row <= patch, scores, MASKED_SCORE)
            top = jnp.max(scores, axis=0, keepdims=True)
            exps = jnp.exp2((scores - top) * (SCALING * LOG2E))
            low = (exps * (1.0 / col(exps))).astype(bf16)
            probs[w, :, 256 * b : 256 * b + 256] = low
            m[b, pl.ds(w, TP, stride=WC), :] = query_side(v, low)

    for w in range(WC):
        one(w)
    for b in range(4):
        merged[:, :, 128 * b : 128 * b + 128] = m[b, 0 : (patch + 1) * WC].astype(bf16).reshape(patch + 1, WC, 128)


def local_bwd_step(w, probs, t, d):
    at = pl.ds(w, TP, stride=WC)
    for b in range(4):
        q = t[b, at, :].astype(bf16)
        k = t[4 + b, at, :].astype(bf16)
        v = t[8 + b, at, :].astype(bf16)
        g = t[12 + b, at, :].astype(bf16)
        qx = expand(q)
        gx = expand(g)
        low = probs[w, :, 256 * b : 256 * b + 256]
        high = low.astype(f32)
        scaled = high * nt(v, gx)
        back = (scaled - high * col(scaled)).astype(bf16)
        d[4 + b, at, :] = nn(back, qx) * SCALING
        d[8 + b, at, :] = nn(low, gx)
        d[b, at, :] = query_side(k, back) * SCALING


def back_kernel(
    wins, dps,
    triple, triple0, probs, grad_merged, local_in, local_in0,
    region_triple, gathered, probs_r, merged_r, region_mid, grad_middle0, vecs, w_qkv, w_out, out_local,
    up_source, down_source,
    grad_triple, up_part, down_part, terms, grad_query, low_first, low_second, sums, out_bias_part, grad_mid,
    t, d, d0, qkv_acc, grad_merged_s, *streams,
):
    step = pl.program_id(0)
    place = Place(wins, dps)
    up = Stream(place, up_source, None, streams[: Stream.PARTS])
    down = Stream(place, down_source, None, streams[Stream.PARTS :])

    @pl.when(step == 0)
    def _():
        place.greet()
        up.load()
        down.load()
        qkv_acc[...] = jnp.zeros_like(qkv_acc)
        sums[...] = jnp.zeros_like(sums)

    patch = triple.shape[0]
    load_triple(t, triple, triple0, patch)
    rows = (patch + 1) * WC
    for b in range(4):
        t[12 + b, 0:rows] = grad_merged[:, :, 128 * b : 128 * b + 128].reshape(rows, 128).astype(f32)
        t[12 + b, rows:] = jnp.zeros((TP * WC - rows, 128), f32)

    def end():
        for s, part in ((up, up_part), (down, down_part)):
            s.sum_dps(part, slice(None))

    def reached(w):
        if w == 0:
            pl.when(step == 0)(place.greeted)
        for when, after, ups, downs in BACK_SLOTS:
            if after == w:

                @pl.when(step == when)
                def _(ups=ups, downs=downs):
                    for k in ups:
                        up.step(k)
                    for k in downs:
                        down.step(k)

    for w in range(WC):
        local_bwd_step(w, probs, t, d)
        reached(w)
    at = pl.ds(pl.multiple_of(step * WC, WC), WC)
    for b in range(12):
        lanes = slice(128 * b, 128 * b + 128)
        low = d[b, 0:rows].astype(bf16)
        grad_triple[:, :, lanes] = low.reshape(patch + 1, WC, 128)
        d0[at, lanes] = low[rows - WC :]
        sums[:, lanes] += col(low.astype(f32))
    normed = jnp.concatenate([local_in[...].reshape(patch * WC, D), local_in0[...]], axis=0).T
    for b in range(3):
        lanes = slice(D * b, D * (b + 1))
        qkv_acc[:, lanes] += nn(normed, grad_triple[:, :, lanes].reshape(rows, D))

    reached(WC)

    @pl.when(step == pl.num_programs(0) - 1)
    def _():
        vhat, inverse = norm_stats(region_mid[...])
        mid = grad_middle0[0].astype(f32) + norm_back(vhat, inverse, row(vecs, GAIN1), nt(d0[...], w_qkv[...]))
        grad_mid[...] = mid
        grad_attn = mid.astype(bf16)
        out_low = (out_local[...] + tn(merged_r[...], grad_attn)).astype(bf16)
        out_bias_part[...] = col(grad_attn.astype(f32))
        grad_merged_r = nt(grad_attn, w_out[...]).astype(bf16)
        grad_merged_s[...] = grad_merged_r

        keys = gathered.shape[0]
        width = 8 * region_triple.shape[0]
        blocks = max(keys // width, 1) if keys % width == 0 else 1
        size = keys // blocks

        def group_half(g, carry):
            lanes = pl.ds(pl.multiple_of(256 * g, 256), 256)
            value_lanes = pl.ds(pl.multiple_of(D + 256 * g, 256), 256)
            qx = expand_group(region_triple[:, lanes], 8)
            gx = expand_group(grad_merged_s[:, lanes], 8)

            def scaled_at(at):
                high = probs_r[g, at].astype(f32)
                return high, high * nt(gathered[at, value_lanes], gx)

            def finish(at, row_terms, scaled=None):
                high, scaled = scaled_at(at) if scaled is None else scaled
                back = (scaled - high * row_terms).astype(bf16)
                terms[at, lanes] = (nn(back, qx) * SCALING).astype(bf16)
                terms[at, value_lanes] = nn(probs_r[g, at], gx).astype(bf16)
                return tn(back, gathered[at, lanes])

            if blocks == 1:
                both = scaled_at(pl.ds(0, keys))
                total = finish(pl.ds(0, keys), col(both[1]), both)
            else:
                at = lambda i: pl.ds(pl.multiple_of(i * size, 16), size)
                row_terms = lax.fori_loop(
                    0, blocks, lambda i, r: r + col(scaled_at(at(i))[1]), jnp.zeros((1, width), f32)
                )
                total = lax.fori_loop(
                    0, blocks, lambda i, q: q + finish(at(i), row_terms), jnp.zeros((width, 256), f32)
                )
            grad_query[:, lanes] = (fold_group(total, 8) * SCALING).astype(bf16)
            return carry

        if blocks == 1:
            group_half(0, 0)
            group_half(1, 0)
        else:
            lax.fori_loop(0, 2, group_half, 0)
        sums[:, :D] += col(grad_query[...].astype(f32))
        sums[:, D:] += col(terms[...].astype(f32))
        region_in_all = gathered[:, 2 * D :]
        own_in = gathered[pl.ds(pl.multiple_of(place.win * region_triple.shape[0], 16), region_triple.shape[0]), 2 * D :]
        shape = low_first.shape[:3] + (D,)
        low_first[:, :, :, :D] = (qkv_acc[:, :D] + tn(own_in, grad_query[...])).astype(bf16).reshape(shape)
        low_first[:, :, :, D:] = (qkv_acc[:, D : 2 * D] + tn(region_in_all, terms[:, :D])).astype(bf16).reshape(shape)
        low_second[:, :, :, :D] = (qkv_acc[:, 2 * D :] + tn(region_in_all, terms[:, D:])).astype(bf16).reshape(shape)
        low_second[:, :, :, D:] = out_low.reshape(shape)
        end()


def gelu_both(v):
    e = jnp.exp2(v * v * (-0.5 * LOG2E))
    cdf = 0.5 + 0.5 * lax.erf(v * (0.5**0.5))
    return v * cdf, cdf + v * e * 0.3989422804014327


def with_region(block, region, last):
    tokens, count, width = block.shape
    head = block[0 : tokens - 1].reshape((tokens - 1) * count, width)
    tail = jnp.where(last, region, block[tokens - 1])
    return jnp.concatenate([head, tail], axis=0)


def mlp_kernel(
    patches, region_mid, merged, patch_cot, region_cot, vecs, w_out, w_up, w_down,
    patch_out, region_out, grad_middle, grad_merged, up_grad, down_grad_t, out_grad, vec512, up_bias_grad,
    up_acc, down_acc,
):
    step = pl.program_id(0)
    last = step == pl.num_programs(0) - 1
    tokens, count, _ = patches.shape
    rows = tokens * count

    @pl.when(step == 0)
    def _():
        up_acc[...] = jnp.zeros_like(up_acc)
        down_acc[...] = jnp.zeros_like(down_acc)
        out_grad[...] = jnp.zeros_like(out_grad)
        vec512[...] = jnp.zeros_like(vec512)
        up_bias_grad[...] = jnp.zeros_like(up_bias_grad)

    x = with_region(patches[...].astype(f32), region_mid[...], last)
    grad_result = with_region(patch_cot[...], region_cot[...], last)
    low_merged = merged[...].reshape(rows, D)
    middle = x + nn(low_merged, w_out[...]) + row(vecs, OUT_BIAS)
    vhat, inverse = norm_stats(middle)
    mlp_in = normed_low(vhat, vecs, GAIN2, SHIFT2)
    mlp_in_t = mlp_in.T
    grad_result_t = grad_result.T
    result = middle + row(vecs, DOWN_BIAS)
    grad_in = jnp.zeros((rows, D), f32)
    up_row = jnp.concatenate([row(vecs, UP_BIAS + b) for b in range(FF // D)], axis=1)
    for f in range(FF // FB):
        at = slice(FB * f, FB * f + FB)
        hidden = nn(mlp_in, w_up[:, at]) + up_row[:, at]
        active, slope = gelu_both(hidden)
        active = active.astype(bf16)
        grad_hidden = (nt(grad_result, w_down[at, :]) * slope).astype(bf16)
        result += nn(active, w_down[at, :])
        grad_in += nt(grad_hidden, w_up[:, at])
        up_acc[:, at] += nn(mlp_in_t, grad_hidden)
        down_acc[:, at] += nn(grad_result_t, active)
        up_bias_grad[:, at] += col(grad_hidden.astype(f32))
    shown = result.astype(bf16)
    patch_out[...] = shown.reshape(tokens, count, D)
    region_out[...] = shown[rows - count :]
    gm = grad_result.astype(f32) + norm_back(vhat, inverse, row(vecs, GAIN2), grad_in)
    low_gm = gm.astype(bf16)
    grad_middle[...] = low_gm.reshape(tokens, count, D)
    out_grad[...] += nn(low_merged.T, low_gm)
    grad_merged[...] = nt(low_gm, w_out[...]).astype(bf16).reshape(tokens, count, D)
    vec512[0:1] += col(grad_in * vhat)
    vec512[1:2] += col(grad_in)
    vec512[2:3] += col(low_gm.astype(f32))
    vec512[3:4] += col(grad_result.astype(f32))

    @pl.when(last)
    def _():
        up_grad[...] = up_acc[...].astype(bf16)
        down_grad_t[...] = down_acc[...].astype(bf16)


def tail_kernel(
    wins, dps,
    patches, grad_triple, grad_middle, region_mid, vecs, w_qkv, terms, grad_query,
    regional, grad_mid, vec_mlp, up_bias_grad, sums, out_bias_part, up_part, down_part, first_source, second_source,
    patch_grad, region_grad, small_sum, up_sum, down_sum, first_sum, second_sum,
    vec, halves, half_sem, summed, pieces, piece_sem, pack, near, near_sem, total, far, far_sem, *streams,
):
    step = pl.program_id(0)
    tokens, count, _ = patches.shape
    rows = tokens * count
    place = Place(wins, dps)
    parts = [streams[Stream.PARTS * b : Stream.PARTS * (b + 1)] for b in range(4)]
    late = (Stream(place, first_source, first_sum, parts[0]), Stream(place, second_source, second_sum, parts[1]))
    early = (Stream(place, None, up_sum, parts[2]), Stream(place, None, down_sum, parts[3]))

    def window_rows(chip, core):
        return pl.ds(pl.multiple_of((chip * 2 + core) * count, 16), count)

    def to_core():
        return [pltpu.make_async_remote_copy(
            src_ref=terms.at[window_rows(chip, 1 - place.core)], dst_ref=halves.at[chip],
            send_sem=half_sem.at[2 * chip], recv_sem=half_sem.at[2 * chip + 1],
            device_id=place.other_core(), device_id_type=MESH,
        ) for chip in range(place.chips)]

    def to_owners():
        copies = []
        for j in range(1, place.chips):
            chip, to = place.at_chip(j)
            copies.append(pltpu.make_async_remote_copy(
                src_ref=summed.at[chip], dst_ref=pieces.at[j - 1],
                send_sem=piece_sem.at[2 * j - 2], recv_sem=piece_sem.at[2 * j - 1], device_id=to, device_id_type=MESH,
            ))
        return copies

    def to_near():
        return [pltpu.make_async_remote_copy(
            src_ref=pack, dst_ref=near.at[j - 1], send_sem=near_sem.at[2 * j - 2], recv_sem=near_sem.at[2 * j - 1],
            device_id={"win": lax.rem(place.win + j, wins)}, device_id_type=MESH,
        ) for j in range(1, wins)]

    def to_far():
        return [pltpu.make_async_remote_copy(
            src_ref=total, dst_ref=far.at[j - 1], send_sem=far_sem.at[2 * j - 2], recv_sem=far_sem.at[2 * j - 1],
            device_id=place.at_dp(j)[1], device_id_type=MESH,
        ) for j in range(1, dps)]

    def late_step(k):
        for s in late:
            s.step(k)

    def early_step(k):
        for s in early:
            s.step(k)

    def begin():
        place.greeted(all_wins=True)
        late_step(0)
        for c in to_core():
            c.start()
        for s, part in zip(early, (up_part, down_part)):
            s.begin_back(part)

    def owners_begin():
        for c in to_core():
            c.wait()

        def add(chip, carry):
            own = terms[window_rows(chip, place.core)].astype(f32)
            summed[chip] = (own + halves[chip].astype(f32)).astype(bf16)
            return carry

        lax.fori_loop(0, place.chips, add, 0)
        for c in to_owners():
            c.start()

    def region_end():
        for c in to_owners():
            c.wait()
        key_value = summed[place.chip].astype(f32)
        for j in range(place.chips - 1):
            key_value += pieces[j].astype(f32)
        vhat, inverse = norm_stats(regional[...].astype(f32))
        grad_in = nt(grad_query[...], w_qkv[:, :D]) + nt(key_value.astype(bf16), w_qkv[:, D:])
        region_grad[...] = (grad_mid[...] + norm_back(vhat, inverse, row(vecs, GAIN1), grad_in)).astype(bf16)
        vec[0:1] += col(grad_in * vhat)
        vec[1:2] += col(grad_in)

    def small_begin():
        pack[0:2] = vec[0:2]
        pack[2:3] = sums[:, :D]
        pack[3:4] = sums[:, 2 * D :]
        pack[4:5] = vec_mlp[2:3] + out_bias_part[...]
        pack[5:7] = vec_mlp[0:2]
        pack[7:8] = vec_mlp[3:4]
        for b in range(4):
            pack[8 + b : 9 + b] = up_bias_grad[:, D * b : D * (b + 1)]
        pack[12:16] = jnp.zeros((4, D), f32)
        for c in to_near():
            c.start()

    def small_middle():
        for c in to_near():
            c.wait()
        part = pack[...]
        for j in range(wins - 1):
            part += near[j]
        total[...] = part
        for c in to_far():
            c.start()

    def small_end():
        for c in to_far():
            c.wait()
        part = total[...]
        for j in range(dps - 1):
            part += far[j]
        small_sum[...] = part

    @pl.when(step == 0)
    def _():
        place.greet(all_wins=True)
        for s in late:
            s.load()
        vec[...] = jnp.zeros_like(vec)
        begin()

    x = with_region(patches[...].astype(f32), region_mid[...], step == pl.num_programs(0) - 1)
    vhat, inverse = norm_stats(x)
    grad_in = nt(grad_triple[...].reshape(rows, 3 * D), w_qkv[...])
    vec[0:1] += col(grad_in * vhat)
    vec[1:2] += col(grad_in)
    total_rows = grad_middle[...].reshape(rows, D).astype(f32) + norm_back(vhat, inverse, row(vecs, GAIN1), grad_in)
    patch_grad[...] = total_rows.astype(bf16).reshape(tokens, count, D)

    def end():
        late_step(3)
        owners_begin()
        early_step(5)
        late_step(4)
        early_step(6)
        region_end()
        small_begin()
        late_step(5)
        small_middle()
        late_step(6)
        early_step(7)
        small_end()
        late_step(7)
        early_step(8)
        late_step(8)

    hooks = {
        0: lambda: late_step(1),
        3: lambda: late_step(2),
        4: end,
    }
    for when, todo in hooks.items():
        pl.when(step == when)(todo)


def last_kernel(
    up, down_t, first, second, small, patch_in, region_in,
    patch_grad, region_grad, in_gain, in_shift, qkv, qkv_bias, out_grad, out_bias, mlp_gain, mlp_shift,
    up_grad, up_bias, down_grad, down_bias,
):
    up_grad[...] = up[...].astype(f32)
    down_grad[...] = down_t[...].T.astype(f32)
    qkv[:, : 2 * D] = first[...].astype(f32)
    qkv[:, 2 * D :] = second[:, :D].astype(f32)
    out_grad[...] = second[:, D:].astype(f32)
    patch_grad[...] = patch_in[...]

    @pl.when(pl.program_id(0) == 0)
    def _():
        region_grad[...] = region_in[...]
        for at, v in ((0, in_gain), (1, in_shift), (4, out_bias), (5, mlp_gain), (6, mlp_shift), (7, down_bias)):
            v[...] = small[at : at + 1].reshape(D)
        qkv_bias[...] = small[2:4]
        up_bias[...] = jnp.concatenate([small[8 + b : 9 + b] for b in range(FF // D)], axis=1).reshape(FF)


def shards(
    wins, dps,
    patches, regional, window_image, in_gain, in_shift, w_qkv, qkv_bias, w_out, out_bias,
    mlp_gain, mlp_shift, w_up, up_bias, w_down, down_bias, patch_cot, region_cot,
):
    _, count, patch, _ = patches.shape
    group = window_image.shape[1]
    x = patches[0].transpose(1, 0, 2)
    cot = patch_cot[0].transpose(1, 0, 2)
    reg = regional[0]
    rcot = region_cot[0]
    const = lambda *arrays: [whole(a) for a in arrays]
    block = lambda a, n: (a, (n,) + a.shape[1:], lambda i: (i, 0, 0))
    block_out = lambda shape, n, dtype=bf16: ((shape, dtype), (n,) + shape[1:], lambda i: (i, 0, 0))
    triple, local_in, vecs, region_triple, gathered, probs_r, merged_r, region_mid, triple0, local_in0 = call(
        functools.partial(front_kernel, wins, dps), (pl.cdiv(patch, 7),),
        [block(x, 7)]
        + const(reg, window_image, in_gain, in_shift, w_qkv, qkv_bias, w_out, out_bias, mlp_gain, mlp_shift, up_bias, down_bias),
        [block_out((patch, count, 3 * D), 7), block_out((patch, count, D), 7), whole_out((16, D), f32), whole_out((count, 3 * D), bf16),
         whole_out((group, 3 * D), bf16), whole_out((2, group, 8 * count), bf16), whole_out((count, D), bf16),
         whole_out((count, D), f32), whole_out((count, 3 * D), bf16), whole_out((count, D), bf16)],
        [pltpu.VMEM((group, 3 * D), bf16), pltpu.VMEM((count, 3 * D), bf16), pltpu.VMEM((group, 128), f32),
         pltpu.SemaphoreType.DMA((2 * wins,))],
        name="front", collective_id=2,
    )
    steps = (count // WC,)
    mid = lambda a: (a, (a.shape[0], WC, a.shape[2]), lambda i: (0, i, 0))
    mid_out = lambda shape, dtype=bf16: ((shape, dtype), (shape[0], WC, shape[2]), lambda i: (0, i, 0))
    tail = lambda a: (a, (WC, a.shape[1]), lambda i: (i, 0))
    merged, probs = call(
        local_fwd_kernel, steps, [mid(triple), tail(triple0)],
        [mid_out((patch + 1, count, D)), ((((count, TP, HEADS * TP)), bf16), (WC, TP, HEADS * TP), lambda i: (i, 0, 0))],
        [pltpu.VMEM((12, TP * WC, 128), f32), pltpu.VMEM((4, TP * WC, 128), f32)], name="local_fwd",
    )
    n = 10
    rows_grid = ((patch + 1) // n,)
    patch_out, region_out, grad_middle, grad_merged, up_grad, down_grad_t, out_local, vec_mlp, up_bias_grad = call(
        mlp_kernel, rows_grid,
        [block(x, n), whole(region_mid), block(merged, n), block(cot, n)]
        + const(rcot, vecs, w_out, w_up, w_down),
        [block_out((patch, count, D), n), whole_out((count, D), bf16),
         block_out((patch + 1, count, D), n), block_out((patch + 1, count, D), n),
         whole_out((D, FF), bf16), whole_out((D, FF), bf16), whole_out((D, D), f32),
         whole_out((8, D), f32), whole_out((1, FF), f32)],
        [pltpu.VMEM((D, FF), f32), pltpu.VMEM((D, FF), f32)], name="mlp",
    )
    last_rows = rows_of(wins, dps)[1]
    grad_triple, up_part, down_part, terms, grad_query, low_first, low_second, sums, out_bias_part, grad_mid = call(
        functools.partial(back_kernel, wins, dps), steps,
        [mid(triple), tail(triple0), (probs, (WC, TP, HEADS * TP), lambda i: (i, 0, 0), group > 512), mid(grad_merged), mid(local_in), tail(local_in0)]
        + const(region_triple, gathered, probs_r, merged_r, region_mid)
        + [(grad_middle, (1, count, D), lambda i: (patch, 0, 0))]
        + const(vecs, w_qkv, w_out, out_local) + [left(a.reshape(stream_shape(wins, FF))) for a in (up_grad, down_grad_t)],
        [mid_out((patch + 1, count, 3 * D)), whole_out((last_rows, FF), bf16), whole_out((last_rows, FF), bf16),
         whole_out((group, 2 * D), bf16), whole_out((count, D), bf16), whole_out(stream_shape(wins, 2 * D), bf16),
         whole_out(stream_shape(wins, 2 * D), bf16),
         whole_out((1, 3 * D), f32), whole_out((1, D), f32), whole_out((count, D), f32)],
        [pltpu.VMEM((16, TP * WC, 128), f32), pltpu.VMEM((12, TP * WC, 128), f32), pltpu.VMEM((count, 3 * D), bf16),
         pltpu.VMEM((D, 3 * D), f32), pltpu.VMEM((count, D), bf16)]
        + stream_scratch(wins, dps, FF, "down") * 2,
        name="back", collective_id=0,
    )
    patch_grad, region_grad, small, up_sum, down_sum, first_sum, second_sum = call(
        functools.partial(tail_kernel, wins, dps), rows_grid,
        [block(x, n), block(grad_triple, n), block(grad_middle, n)]
        + const(region_mid, vecs, w_qkv, terms, grad_query, reg, grad_mid, vec_mlp, up_bias_grad, sums, out_bias_part, up_part, down_part)
        + [left(low_first), left(low_second)],
        [block_out((patch, count, D), n), whole_out((count, D), bf16), whole_out((16, D), f32)]
        + [left_out(stream_shape(wins, FF), bf16)] * 2 + [left_out(stream_shape(wins, 2 * D), bf16)] * 2,
        [pltpu.VMEM((8, D), f32),
         pltpu.VMEM((wins // 2, count, 2 * D), bf16), pltpu.SemaphoreType.DMA((wins,)), pltpu.VMEM((wins // 2, count, 2 * D), bf16),
         pltpu.VMEM((wins // 2, count, 2 * D), bf16), pltpu.SemaphoreType.DMA((wins,)),
         pltpu.VMEM((16, D), f32), pltpu.VMEM((wins - 1, 16, D), f32), pltpu.SemaphoreType.DMA((2 * wins,)),
         pltpu.VMEM((16, D), f32), pltpu.VMEM((max(dps - 1, 1), 16, D), f32), pltpu.SemaphoreType.DMA((2 * dps,))]
        + stream_scratch(wins, dps, 2 * D) * 2 + stream_scratch(wins, dps, FF, "back") * 2,
        name="tail", collective_id=1,
    )
    up_sum, down_sum = up_sum.reshape(D, FF), down_sum.reshape(D, FF)
    first_sum, second_sum = first_sum.reshape(D, 2 * D), second_sum.reshape(D, 2 * D)
    n = 4
    down = lambda i: (i, 0)
    vector = lambda size: ((((size,), f32)), (size,), lambda i: (0,))
    token = -(-patch // n)
    tokens = lambda i: (lax.min(i, (patch - 1) // token), 0, 0)
    (
        patch_grad, region_grad, in_gain_grad, in_shift_grad, qkv_grad, qkv_bias_grad, out_grad, out_bias_grad,
        mlp_gain_grad, mlp_shift_grad, up_grad, up_bias_grad, down_grad, down_bias_grad,
    ) = call(
        last_kernel, (n,),
        [(up_sum, (D // n, FF), down), (down_sum, (D, FF // n), lambda i: (0, i))]
        + [(a, (D // n, 2 * D), down) for a in (first_sum, second_sum)]
        + [whole(small), (patch_grad, (token, count, D), tokens), whole(region_grad)],
        [(((patch, count, D), bf16), (token, count, D), tokens), whole_out((count, D), bf16), vector(D), vector(D),
         (((D, 3 * D), f32), (D // n, 3 * D), down), whole_out((2, D), f32), (((D, D), f32), (D // n, D), down), vector(D),
         vector(D), vector(D), (((D, FF), f32), (D // n, FF), down), vector(FF), (((FF, D), f32), (FF // n, D), down), vector(D)],
        name="last",
    )
    return (
        patch_out.transpose(1, 0, 2)[None], region_out[None], patch_grad.transpose(1, 0, 2)[None], region_grad[None],
        in_gain_grad, in_shift_grad, qkv_grad, qkv_bias_grad, out_grad, out_bias_grad,
        mlp_gain_grad, mlp_shift_grad, up_grad, up_bias_grad, down_grad, down_bias_grad,
    )


def solution(mesh):
    wide = P("dp", "win", None, None)
    narrow = P("dp", "win", None)
    in_specs = (wide, narrow, P("dp", None)) + (P(),) * 12 + (wide, narrow)
    out_specs = (wide, narrow, wide, narrow) + (P(),) * 12
    return jax.shard_map(functools.partial(shards, mesh.shape["win"], mesh.shape["dp"]), mesh=mesh, in_specs=in_specs, out_specs=out_specs, check_vma=False)
```

```python
import functools

import jax
import jax.numpy as jnp
from jax import lax
from jax.experimental import pallas as pl
from jax.experimental.pallas import tpu as pltpu
from jax.sharding import PartitionSpec as P

D = 512
HEADS = 16
HD = 32
FF = 2048
EPSILON = 1e-06
MASKED_SCORE = -1e30
SCALING = HD ** (-0.5)
LOG2E = 1.4426950408889634
TP = 64
FB = 2048
WC = 16
f32 = jnp.float32
bf16 = jnp.bfloat16
VMEM_LIMIT = 60 * 2**20
MESH = pl.DeviceIdType.MESH
FRONT_SLOTS = (5, 6)
BACK_SLOTS = (
    (0, 0, (0,), (0,)), (0, 6, (1,), ()), (0, 16, (), (1,)), (1, 7, (2,), ()), (1, 16, (3,), (2,)), (2, 7, (), (3,)),
)


def nn(a, b):
    return lax.dot_general(a, b, (((1,), (0,)), ((), ())), preferred_element_type=f32)


def nt(a, b):
    return lax.dot_general(a, b, (((1,), (1,)), ((), ())), preferred_element_type=f32)


def tn(a, b):
    return lax.dot_general(a, b, (((0,), (0,)), ((), ())), preferred_element_type=f32)


def call(body, grid, ins, outs, scratch=(), name=None, collective_id=None, limit=VMEM_LIMIT):
    def spec(block, index, *single):
        if block is None:
            return pl.BlockSpec(memory_space=pl.ANY)
        if index is None:
            return pl.BlockSpec(block, lambda *_: (0,) * len(block), pipeline_mode=pl.Buffered(1))
        return pl.BlockSpec(block, index, pipeline_mode=pl.Buffered(1) if any(single) else None)

    return pl.pallas_call(
        body,
        grid=grid,
        in_specs=[spec(*entry[1:]) for entry in ins],
        out_specs=[spec(b, i) for _, b, i in outs],
        out_shape=[jax.ShapeDtypeStruct(s, d) for (s, d), _, _ in outs],
        scratch_shapes=list(scratch),
        compiler_params=pltpu.CompilerParams(
            vmem_limit_bytes=limit, collective_id=collective_id, has_side_effects=collective_id is not None
        ),
        name=name,
    )(*[entry[0] for entry in ins])


def whole(a):
    return (a, a.shape, None)


def whole_out(shape, dtype):
    return ((shape, dtype), shape, None)


def left(a):
    return (a, None, None)


def left_out(shape, dtype):
    return ((shape, dtype), None, None)


def norm_stats(rows):
    average = jnp.mean(rows, axis=-1, keepdims=True)
    centred = rows - average
    spread = jnp.mean(centred * centred, axis=-1, keepdims=True)
    inverse = lax.rsqrt(spread + EPSILON)
    return centred * inverse, inverse


def norm_back(vhat, inverse, gain, grad_out):
    scaled = grad_out * gain
    first = jnp.mean(scaled, axis=-1, keepdims=True)
    second = jnp.mean(scaled * vhat, axis=-1, keepdims=True)
    return inverse * (scaled - first - vhat * second)


def col(x):
    return jnp.sum(x, axis=0, keepdims=True)


class Place:
    def __init__(self, wins, dps):
        self.wins, self.dps = wins, dps
        self.win = lax.axis_index("win")
        self.dp = lax.axis_index("dp")
        self.core = lax.rem(self.win, 2)
        self.chip = self.win // 2
        self.chips = wins // 2
        self.square = self.chips == 4
        self.a = self.chip // 2
        self.b = lax.rem(self.chip, 2)

    def other_core(self):
        return {"win": self.chip * 2 + 1 - self.core}

    def other_a(self):
        return {"win": ((1 - self.a) * 2 + self.b) * 2 + self.core}

    def other_b(self):
        return {"win": (self.a * 2 + 1 - self.b) * 2 + self.core}

    def at_chip(self, j):
        chip = lax.rem(self.chip + j, self.chips)
        return chip, {"win": chip * 2 + self.core}

    def at_dp(self, j):
        dp = lax.rem(self.dp + j, self.dps)
        return dp, {"dp": dp}

    def near(self, all_wins, around=False):
        if all_wins:
            return [{"win": lax.rem(self.win + j, self.wins)} for j in range(1, self.wins)]
        if self.square and not around:
            return [self.other_core(), self.other_a(), self.other_b()]
        return [self.other_core()] + [self.at_chip(j)[1] for j in range(1, self.chips)]

    def partners(self, all_wins, along, around):
        return self.near(all_wins, around) + [self.at_dp(j)[1] for j in range(1, self.dps if along else 1)]

    def greet(self, all_wins=False, along=True, around=False):
        barrier = pltpu.get_barrier_semaphore()
        for to in self.partners(all_wins, along, around):
            pl.semaphore_signal(barrier, inc=1, device_id=to, device_id_type=MESH)

    def greeted(self, all_wins=False, along=True, around=False):
        pl.semaphore_wait(pltpu.get_barrier_semaphore(), len(self.partners(all_wins, along, around)))


def rows_of(wins, dps):
    piece = D // wins
    return piece, piece // dps if piece % (16 * dps) == 0 else piece


def stream_shape(wins, columns):
    return (2, wins // 2, D // wins, columns)


def stream_scratch(wins, dps, columns, kind="whole"):
    piece, last = rows_of(wins, dps)
    chips = wins // 2
    landing = (4, 2, piece, columns // 2) if chips == 4 else (max(chips - 1, 1), piece, columns)
    half, part, some = pltpu.VMEM((chips, piece, columns), bf16), pltpu.VMEM((piece, columns), bf16), pltpu.VMEM((16, 128), bf16)
    down = kind != "back"
    return [
        half if down else some,
        half,
        pltpu.VMEM(landing, bf16) if down else some,
        part if down else some,
        pltpu.VMEM((max(dps - 1, 1), last, columns), bf16) if down else some,
        some if kind == "down" else part,
        pltpu.SemaphoreType.DMA((20 + 4 * chips + 4 * dps,)),
    ]


def columns_of(refs):
    return refs[1].shape[2]


class Stream:
    PARTS = 7

    def __init__(self, place, source, final, refs):
        self.p = place
        self.source, self.final = source, final
        self.own, self.r1, self.r2, self.s, self.r3, self.s2, self.sem = refs
        self.piece, self.last = rows_of(place.wins, place.dps)
        self.split = self.last != self.piece
        columns = columns_of(refs)
        self.left, self.right = pl.ds(0, columns // 2), pl.ds(columns // 2, columns // 2)

    def rows(self, start, size):
        return pl.ds(pl.multiple_of(start, 16), size)

    def remote(self, src, dst, to, k):
        return pltpu.make_async_remote_copy(
            src_ref=src, dst_ref=dst, send_sem=self.sem.at[2 * k], recv_sem=self.sem.at[2 * k + 1],
            device_id=to, device_id_type=MESH,
        )

    def _own(self):
        return pltpu.make_async_copy(self.source.at[self.p.core], self.own, self.sem.at[0])

    def _put(self):
        return pltpu.make_async_copy(self.r1, self.final.at[self.p.core], self.sem.at[1])

    def _cores(self):
        return [self.remote(self.source.at[1 - self.p.core], self.r1, self.p.other_core(), 1)]

    def _cores_back(self):
        return [self.remote(self.r1, self.final.at[self.p.core], self.p.other_core(), 2)]

    def _chips_left(self, k):
        p = self.p
        if k == 0:
            return [self.remote(self.own.at[c * 2 + 1 - p.b, :, self.left], self.r2.at[0, c], p.other_b(), 3 + c) for c in range(2)]
        return [self.remote(self.own.at[(1 - p.a) * 2 + p.b, :, self.left], self.r2.at[2, 0], p.other_a(), 5)]

    def _chips_right(self, k):
        p = self.p
        if k == 0:
            return [self.remote(self.own.at[(1 - p.a) * 2 + c, :, self.right], self.r2.at[1, c], p.other_a(), 6 + c) for c in range(2)]
        return [self.remote(self.own.at[p.a * 2 + 1 - p.b, :, self.right], self.r2.at[3, 0], p.other_b(), 8)]

    def _back_left(self, k):
        p = self.p
        mine = self.r1
        if k == 0:
            return [self.remote(self.s2.at[:, self.left], mine.at[p.chip, :, self.left], p.other_a(), 9)]
        rows = [mine.at[c * 2 + p.b, :, self.left] for c in range(2)]
        return [self.remote(rows[c], rows[c], p.other_b(), 10 + c) for c in range(2)]

    def _back_right(self, k):
        p = self.p
        mine = self.r1
        if k == 0:
            return [self.remote(self.s2.at[:, self.right], mine.at[p.chip, :, self.right], p.other_b(), 12)]
        rows = [mine.at[p.a * 2 + c, :, self.right] for c in range(2)]
        return [self.remote(rows[c], rows[c], p.other_a(), 13 + c) for c in range(2)]

    def _chips(self):
        out = []
        for j in range(1, self.p.chips):
            chip, to = self.p.at_chip(j)
            out.append(self.remote(self.own.at[chip], self.r2.at[j - 1], to, 2 + j))
        return out

    def _chips_back(self):
        out = []
        for j in range(1, self.p.chips):
            mine = self.r1.at[self.p.chip]
            out.append(self.remote(self.s2, mine, self.p.at_chip(j)[1], 2 + self.p.chips + j))
        return out

    def _dps(self):
        out = []
        for j in range(1, self.p.dps):
            dp, to = self.p.at_dp(j)
            src = self.s.at[self.rows(dp * self.last, self.last)] if self.split else self.s
            out.append(self.remote(src, self.r3.at[j - 1], to, 8 + 2 * self.p.chips + j))
        return out

    def _dps_back(self):
        out = []
        if self.split:
            for j in range(1, self.p.dps):
                mine = self.s2.at[self.rows(self.p.dp * self.last, self.last)]
                out.append(self.remote(mine, mine, self.p.at_dp(j)[1], 8 + 2 * self.p.chips + self.p.dps + j))
        return out

    def start(self, copies):
        for c in copies:
            c.start()

    def wait(self, copies):
        for c in copies:
            c.wait()

    def load(self):
        self._own().start()

    def send_cores(self):
        self.start(self._cores())

    def send_chips(self):
        self._own().wait()
        self.wait(self._cores())

        def add(i, carry):
            self.own[i] = (self.own[i].astype(f32) + self.r1[i].astype(f32)).astype(bf16)
            return carry

        lax.fori_loop(0, self.p.chips, add, 0)
        if self.p.square:
            self.start(self._chips_left(0))
            self.start(self._chips_right(0))
        else:
            self.start(self._chips())

    def add_square(self, chip, lanes, slot, c):
        self.own[chip, :, lanes] = (self.own[chip, :, lanes].astype(f32) + self.r2[slot, c].astype(f32)).astype(bf16)

    def send_chips_again(self):
        p = self.p
        if p.square:
            self.wait(self._chips_left(0))
            for c in range(2):
                self.add_square(c * 2 + p.b, self.left, 0, c)
            self.start(self._chips_left(1))
            self.wait(self._chips_right(0))
            for c in range(2):
                self.add_square(p.a * 2 + c, self.right, 1, c)
            self.start(self._chips_right(1))

    def send_dps(self):
        p = self.p
        if p.square:
            for lanes, slot, copies in ((self.left, 2, self._chips_left(1)), (self.right, 3, self._chips_right(1))):
                self.wait(copies)
                self.s[:, lanes] = (self.own[p.chip, :, lanes].astype(f32) + self.r2[slot, 0].astype(f32)).astype(bf16)
        else:
            self.wait(self._chips())
            total = self.own[p.chip].astype(f32)
            for j in range(p.chips - 1):
                total += self.r2[j].astype(f32)
            self.s[...] = total.astype(bf16)
        self.start(self._dps())

    def sum_dps(self, out, at):
        self.wait(self._dps())
        mine = self.part()
        total = self.s[mine].astype(f32)
        for j in range(self.p.dps - 1):
            total += self.r3[j].astype(f32)
        out[at] = total.astype(bf16)

    def part(self):
        return self.rows(self.p.dp * self.last if self.split else 0, self.last)

    def send_dps_back(self):
        self.sum_dps(self.s2, self.part())
        self.start(self._dps_back())

    def end_dps_back(self):
        self.wait(self._dps_back())

    def begin_back(self, part):
        self.s2[self.part()] = part[...]
        self.start(self._dps_back())

    def send_chips_back(self):
        self.end_dps_back()
        self.start_chips_back()

    def start_chips_back(self):
        self.r1[self.p.chip] = self.s2[...]
        if self.p.square:
            self.start(self._back_left(0))
            self.start(self._back_right(0))
        else:
            self.start(self._chips_back())

    def send_chips_back_again(self):
        if self.p.square:
            self.wait(self._back_left(0))
            self.start(self._back_left(1))
            self.wait(self._back_right(0))
            self.start(self._back_right(1))
        else:
            self.wait(self._chips_back())

    def send_cores_back(self):
        if self.p.square:
            self.wait(self._back_left(1))
            self.wait(self._back_right(1))
        self.start(self._cores_back())
        self._put().start()

    def finish(self):
        self.wait(self._cores_back())
        self._put().wait()

    STEPS = (
        "send_cores", "send_chips", "send_chips_again", "send_dps", "send_dps_back",
        "send_chips_back", "send_chips_back_again", "send_cores_back", "finish",
    )

    def step(self, k):
        if 0 <= k < len(self.STEPS):
            getattr(self, self.STEPS[k])()


def expand_group(x, heads):
    lane = lax.broadcasted_iota(jnp.int32, (1, x.shape[1]), 1) // HD
    return jnp.concatenate([jnp.where(lane == i, x, jnp.zeros_like(x)) for i in range(heads)], axis=0)


def fold_group(y, heads):
    rows = y.shape[0] // heads
    lane = lax.broadcasted_iota(jnp.int32, (1, y.shape[1]), 1) // HD
    total = y[(heads - 1) * rows :]
    for i in range(heads - 2, -1, -1):
        total = jnp.where(lane == i, y[i * rows : (i + 1) * rows], total)
    return total


GAIN1, SHIFT1, GAIN2, SHIFT2, OUT_BIAS, DOWN_BIAS, QUERY_BIAS, KEY_BIAS, VALUE_BIAS, UP_BIAS = range(10)


def row(vecs, at):
    return vecs[at : at + 1]


def normed_low(vhat, vecs, gain, shift):
    return (vhat * row(vecs, gain) + row(vecs, shift)).astype(bf16)


def front_kernel(
    wins, dps,
    patches, regional, images, in_gain, in_shift, w_qkv, qkv_bias, w_out, out_bias, mlp_gain, mlp_shift, up_bias, down_bias,
    triple, local_in, vecs, region_triple, gathered_out, probs, merged, region_mid, triple0, local_in0,
    gathered, packed, image_col, sem,
):
    step = pl.program_id(0)
    place = Place(wins, dps)
    count = regional.shape[0]
    group = gathered.shape[0]
    mine = pl.ds(pl.multiple_of(place.win * count, 16), count)

    def project(normed):
        out = nn(normed, w_qkv[...])
        return jnp.concatenate(
            [out[:, :D] + row(vecs, QUERY_BIAS), out[:, D : 2 * D], out[:, 2 * D :] + row(vecs, VALUE_BIAS)], axis=1
        ).astype(bf16)

    parts = (pl.ds(0, 2 * D), pl.ds(2 * D, D))

    def remote(src, dst, to, k):
        return pltpu.make_async_remote_copy(
            src_ref=src, dst_ref=dst, send_sem=sem.at[2 * k], recv_sem=sem.at[2 * k + 1], device_id=to, device_id_type=MESH
        )

    def direct(part):
        lanes, first = parts[part], 2 * place.chips * part
        targets = [place.other_core()] + [place.at_chip(j)[1] for j in range(1, place.chips)]
        return [remote(packed.at[:, lanes], gathered.at[mine, lanes], to, first + j) for j, to in enumerate(targets)]

    def onward(part):
        lanes, first = parts[part], 2 * place.chips * part + place.chips
        copies = []
        for j in range(1, place.chips):
            chip = lax.rem(place.chip - j + place.chips, place.chips)
            theirs = gathered.at[pl.ds(pl.multiple_of((chip * 2 + place.core) * count, 16), count), lanes]
            copies.append(remote(theirs, theirs, place.other_core(), first + j))
        return copies

    def pass_on(part):
        for c in direct(part):
            c.wait()
        for c in onward(part):
            c.start()

    @pl.when(step == 0)
    def _():
        place.greet(around=True, along=False)
        for at, v in (
            (GAIN1, in_gain), (SHIFT1, in_shift), (GAIN2, mlp_gain), (SHIFT2, mlp_shift), (OUT_BIAS, out_bias), (DOWN_BIAS, down_bias),
        ):
            vecs[at : at + 1] = v[...].astype(f32).reshape(1, D)
        vecs[QUERY_BIAS : QUERY_BIAS + 1] = qkv_bias[0:1].astype(f32)
        vecs[KEY_BIAS : KEY_BIAS + 1] = jnp.zeros((1, D), f32)
        vecs[VALUE_BIAS : VALUE_BIAS + 1] = qkv_bias[1:2].astype(f32)
        up = up_bias[...].astype(f32).reshape(1, FF)
        for b in range(FF // D):
            vecs[UP_BIAS + b : UP_BIAS + b + 1] = up[:, D * b : D * (b + 1)]
        vecs[UP_BIAS + FF // D : 16] = jnp.zeros((16 - UP_BIAS - FF // D, D), f32)
        vhat, _ = norm_stats(regional[...].astype(f32))
        normed = normed_low(vhat, vecs, GAIN1, SHIFT1)
        own = project(normed)
        region_triple[...] = own
        packed[:, : 2 * D] = own[:, D:]
        packed[:, 2 * D :] = normed
        gathered[mine] = packed[...]
        place.greeted(around=True, along=False)
        for part in range(2):
            for c in direct(part):
                c.start()
        ids = images[...].astype(f32)
        image_col[...] = jnp.broadcast_to(ids, (128, group)).T

    rows = patches.shape[0] * count
    vhat, _ = norm_stats(patches[...].reshape(rows, D).astype(f32))
    normed_rows = normed_low(vhat, vecs, GAIN1, SHIFT1)
    local_in[...] = normed_rows.reshape(local_in.shape)
    triple[...] = project(normed_rows).reshape(triple.shape)

    for part, when in enumerate(FRONT_SLOTS):
        pl.when(step == when)(functools.partial(pass_on, part))

    @pl.when(step == pl.num_programs(0) - 1)
    def _():
        for c in onward(0):
            c.wait()
        own_ids = image_col[mine]
        own_row = jnp.concatenate([own_ids] * 8, axis=0).T[0:1]
        same = image_col[:, 0:1] == own_row
        for g in range(2):
            lanes = slice(256 * g, 256 * g + 256)
            scores = nt(gathered[:, lanes], expand_group(region_triple[:, lanes], 8))
            scores = jnp.where(same, scores * SCALING, MASKED_SCORE)
            top = jnp.max(scores, axis=0, keepdims=True)
            exps = jnp.exp2((scores - top) * LOG2E)
            low = (exps * (1.0 / col(exps))).astype(bf16)
            probs[g] = low
            merged[:, lanes] = fold_group(tn(low, gathered[:, D + 256 * g : D + 256 * g + 256]), 8).astype(bf16)
        mid = regional[...].astype(f32) + nn(merged[...], w_out[...]) + row(vecs, OUT_BIAS)
        region_mid[...] = mid
        vhat_mid, _ = norm_stats(mid)
        normed_mid = normed_low(vhat_mid, vecs, GAIN1, SHIFT1)
        local_in0[...] = normed_mid
        triple0[...] = project(normed_mid)
        for c in onward(1):
            c.wait()
        gathered_out[...] = gathered[...]


def expand(x):
    lane = lax.broadcasted_iota(jnp.int32, (1, 128), 1) // HD
    return jnp.concatenate([jnp.where(lane == i, x, jnp.zeros_like(x)) for i in range(4)], axis=0)


def query_side(rows, weights):
    lane = lax.broadcasted_iota(jnp.int32, (1, 128), 1) // HD
    out = tn(rows, weights)
    pairs = jnp.concatenate([out[0:64, 0:128], out[64:128, 128:256]], axis=0).T
    return jnp.where(lane % 2 == 0, pairs[0:64], pairs[64:128])


def load_triple(t, triple, triple0, patch):
    for b in range(12):
        lanes = slice(128 * b, 128 * b + 128)
        t[b, 0 : patch * WC] = triple[:, :, lanes].reshape(patch * WC, 128).astype(f32)
        t[b, patch * WC : (patch + 1) * WC] = triple0[:, lanes].astype(f32)
        t[b, (patch + 1) * WC :] = jnp.zeros(((TP - patch - 1) * WC, 128), f32)


def local_fwd_kernel(triple, triple0, merged, probs, t, m):
    patch = triple.shape[0]
    load_triple(t, triple, triple0, patch)
    row = lax.broadcasted_iota(jnp.int32, (TP, 1), 0)

    def one(w):
        for b in range(4):
            q = t[b, pl.ds(w, TP, stride=WC), :].astype(bf16)
            k = t[4 + b, pl.ds(w, TP, stride=WC), :].astype(bf16)
            v = t[8 + b, pl.ds(w, TP, stride=WC), :].astype(bf16)
            scores = nt(k, expand(q))
            scores = jnp.where(row <= patch, scores, MASKED_SCORE)
            top = jnp.max(scores, axis=0, keepdims=True)
            exps = jnp.exp2((scores - top) * (SCALING * LOG2E))
            low = (exps * (1.0 / col(exps))).astype(bf16)
            probs[w, :, 256 * b : 256 * b + 256] = low
            m[b, pl.ds(w, TP, stride=WC), :] = query_side(v, low)

    for w in range(WC):
        one(w)
    for b in range(4):
        merged[:, :, 128 * b : 128 * b + 128] = m[b, 0 : (patch + 1) * WC].astype(bf16).reshape(patch + 1, WC, 128)


def local_bwd_step(w, probs, t, d):
    at = pl.ds(w, TP, stride=WC)
    for b in range(4):
        q = t[b, at, :].astype(bf16)
        k = t[4 + b, at, :].astype(bf16)
        v = t[8 + b, at, :].astype(bf16)
        g = t[12 + b, at, :].astype(bf16)
        qx = expand(q)
        gx = expand(g)
        low = probs[w, :, 256 * b : 256 * b + 256]
        high = low.astype(f32)
        scaled = high * nt(v, gx)
        back = (scaled - high * col(scaled)).astype(bf16)
        d[4 + b, at, :] = nn(back, qx) * SCALING
        d[8 + b, at, :] = nn(low, gx)
        d[b, at, :] = query_side(k, back) * SCALING


def back_kernel(
    wins, dps,
    triple, triple0, probs, grad_merged, local_in, local_in0,
    region_triple, gathered, probs_r, merged_r, region_mid, grad_middle0, vecs, w_qkv, w_out, out_local,
    up_source, down_source,
    grad_triple, up_part, down_part, terms, grad_query, low_first, low_second, sums, out_bias_part, grad_mid,
    t, d, d0, qkv_acc, grad_merged_s, *streams,
):
    step = pl.program_id(0)
    place = Place(wins, dps)
    up = Stream(place, up_source, None, streams[: Stream.PARTS])
    down = Stream(place, down_source, None, streams[Stream.PARTS :])

    @pl.when(step == 0)
    def _():
        place.greet()
        up.load()
        down.load()
        qkv_acc[...] = jnp.zeros_like(qkv_acc)
        sums[...] = jnp.zeros_like(sums)

    patch = triple.shape[0]
    load_triple(t, triple, triple0, patch)
    rows = (patch + 1) * WC
    for b in range(4):
        t[12 + b, 0:rows] = grad_merged[:, :, 128 * b : 128 * b + 128].reshape(rows, 128).astype(f32)
        t[12 + b, rows:] = jnp.zeros((TP * WC - rows, 128), f32)

    def end():
        for s, part in ((up, up_part), (down, down_part)):
            s.sum_dps(part, slice(None))

    def reached(w):
        if w == 0:
            pl.when(step == 0)(place.greeted)
        for when, after, ups, downs in BACK_SLOTS:
            if after == w:

                @pl.when(step == when)
                def _(ups=ups, downs=downs):
                    for k in ups:
                        up.step(k)
                    for k in downs:
                        down.step(k)

    for w in range(WC):
        local_bwd_step(w, probs, t, d)
        reached(w)
    at = pl.ds(pl.multiple_of(step * WC, WC), WC)
    for b in range(12):
        lanes = slice(128 * b, 128 * b + 128)
        low = d[b, 0:rows].astype(bf16)
        grad_triple[:, :, lanes] = low.reshape(patch + 1, WC, 128)
        d0[at, lanes] = low[rows - WC :]
        sums[:, lanes] += col(low.astype(f32))
    normed = jnp.concatenate([local_in[...].reshape(patch * WC, D), local_in0[...]], axis=0).T
    for b in range(3):
        lanes = slice(D * b, D * (b + 1))
        qkv_acc[:, lanes] += nn(normed, grad_triple[:, :, lanes].reshape(rows, D))

    reached(WC)

    @pl.when(step == pl.num_programs(0) - 1)
    def _():
        vhat, inverse = norm_stats(region_mid[...])
        mid = grad_middle0[0].astype(f32) + norm_back(vhat, inverse, row(vecs, GAIN1), nt(d0[...], w_qkv[...]))
        grad_mid[...] = mid
        grad_attn = mid.astype(bf16)
        out_low = (out_local[...] + tn(merged_r[...], grad_attn)).astype(bf16)
        out_bias_part[...] = col(grad_attn.astype(f32))
        grad_merged_r = nt(grad_attn, w_out[...]).astype(bf16)
        grad_merged_s[...] = grad_merged_r

        keys = gathered.shape[0]
        width = 8 * region_triple.shape[0]
        blocks = max(keys // width, 1) if keys % width == 0 else 1
        size = keys // blocks

        def group_half(g, carry):
            lanes = pl.ds(pl.multiple_of(256 * g, 256), 256)
            value_lanes = pl.ds(pl.multiple_of(D + 256 * g, 256), 256)
            qx = expand_group(region_triple[:, lanes], 8)
            gx = expand_group(grad_merged_s[:, lanes], 8)

            def scaled_at(at):
                high = probs_r[g, at].astype(f32)
                return high, high * nt(gathered[at, value_lanes], gx)

            def finish(at, row_terms, scaled=None):
                high, scaled = scaled_at(at) if scaled is None else scaled
                back = (scaled - high * row_terms).astype(bf16)
                terms[at, lanes] = (nn(back, qx) * SCALING).astype(bf16)
                terms[at, value_lanes] = nn(probs_r[g, at], gx).astype(bf16)
                return tn(back, gathered[at, lanes])

            if blocks == 1:
                both = scaled_at(pl.ds(0, keys))
                total = finish(pl.ds(0, keys), col(both[1]), both)
            else:
                at = lambda i: pl.ds(pl.multiple_of(i * size, 16), size)
                row_terms = lax.fori_loop(
                    0, blocks, lambda i, r: r + col(scaled_at(at(i))[1]), jnp.zeros((1, width), f32)
                )
                total = lax.fori_loop(
                    0, blocks, lambda i, q: q + finish(at(i), row_terms), jnp.zeros((width, 256), f32)
                )
            grad_query[:, lanes] = (fold_group(total, 8) * SCALING).astype(bf16)
            return carry

        if blocks == 1:
            group_half(0, 0)
            group_half(1, 0)
        else:
            lax.fori_loop(0, 2, group_half, 0)
        sums[:, :D] += col(grad_query[...].astype(f32))
        sums[:, D:] += col(terms[...].astype(f32))
        region_in_all = gathered[:, 2 * D :]
        own_in = gathered[pl.ds(pl.multiple_of(place.win * region_triple.shape[0], 16), region_triple.shape[0]), 2 * D :]
        shape = low_first.shape[:3] + (D,)
        low_first[:, :, :, :D] = (qkv_acc[:, :D] + tn(own_in, grad_query[...])).astype(bf16).reshape(shape)
        low_first[:, :, :, D:] = (qkv_acc[:, D : 2 * D] + tn(region_in_all, terms[:, :D])).astype(bf16).reshape(shape)
        low_second[:, :, :, :D] = (qkv_acc[:, 2 * D :] + tn(region_in_all, terms[:, D:])).astype(bf16).reshape(shape)
        low_second[:, :, :, D:] = out_low.reshape(shape)
        end()


def gelu_both(v):
    e = jnp.exp2(v * v * (-0.5 * LOG2E))
    cdf = 0.5 + 0.5 * lax.erf(v * (0.5**0.5))
    return v * cdf, cdf + v * e * 0.3989422804014327


def with_region(block, region, last):
    tokens, count, width = block.shape
    head = block[0 : tokens - 1].reshape((tokens - 1) * count, width)
    tail = jnp.where(last, region, block[tokens - 1])
    return jnp.concatenate([head, tail], axis=0)


def mlp_kernel(
    patches, region_mid, merged, patch_cot, region_cot, vecs, w_out, w_up, w_down,
    patch_out, region_out, grad_middle, grad_merged, up_grad, down_grad_t, out_grad, vec512, up_bias_grad,
    up_acc, down_acc,
):
    step = pl.program_id(0)
    last = step == pl.num_programs(0) - 1
    tokens, count, _ = patches.shape
    rows = tokens * count

    @pl.when(step == 0)
    def _():
        up_acc[...] = jnp.zeros_like(up_acc)
        down_acc[...] = jnp.zeros_like(down_acc)
        out_grad[...] = jnp.zeros_like(out_grad)
        vec512[...] = jnp.zeros_like(vec512)
        up_bias_grad[...] = jnp.zeros_like(up_bias_grad)

    x = with_region(patches[...].astype(f32), region_mid[...], last)
    grad_result = with_region(patch_cot[...], region_cot[...], last)
    low_merged = merged[...].reshape(rows, D)
    middle = x + nn(low_merged, w_out[...]) + row(vecs, OUT_BIAS)
    vhat, inverse = norm_stats(middle)
    mlp_in = normed_low(vhat, vecs, GAIN2, SHIFT2)
    mlp_in_t = mlp_in.T
    grad_result_t = grad_result.T
    result = middle + row(vecs, DOWN_BIAS)
    grad_in = jnp.zeros((rows, D), f32)
    up_row = jnp.concatenate([row(vecs, UP_BIAS + b) for b in range(FF // D)], axis=1)
    for f in range(FF // FB):
        at = slice(FB * f, FB * f + FB)
        hidden = nn(mlp_in, w_up[:, at]) + up_row[:, at]
        active, slope = gelu_both(hidden)
        active = active.astype(bf16)
        grad_hidden = (nt(grad_result, w_down[at, :]) * slope).astype(bf16)
        result += nn(active, w_down[at, :])
        grad_in += nt(grad_hidden, w_up[:, at])
        up_acc[:, at] += nn(mlp_in_t, grad_hidden)
        down_acc[:, at] += nn(grad_result_t, active)
        up_bias_grad[:, at] += col(grad_hidden.astype(f32))
    shown = result.astype(bf16)
    patch_out[...] = shown.reshape(tokens, count, D)
    region_out[...] = shown[rows - count :]
    gm = grad_result.astype(f32) + norm_back(vhat, inverse, row(vecs, GAIN2), grad_in)
    low_gm = gm.astype(bf16)
    grad_middle[...] = low_gm.reshape(tokens, count, D)
    out_grad[...] += nn(low_merged.T, low_gm)
    grad_merged[...] = nt(low_gm, w_out[...]).astype(bf16).reshape(tokens, count, D)
    vec512[0:1] += col(grad_in * vhat)
    vec512[1:2] += col(grad_in)
    vec512[2:3] += col(low_gm.astype(f32))
    vec512[3:4] += col(grad_result.astype(f32))

    @pl.when(last)
    def _():
        up_grad[...] = up_acc[...].astype(bf16)
        down_grad_t[...] = down_acc[...].astype(bf16)


def tail_kernel(
    wins, dps,
    patches, grad_triple, grad_middle, region_mid, vecs, w_qkv, terms, grad_query,
    regional, grad_mid, vec_mlp, up_bias_grad, sums, out_bias_part, up_part, down_part, first_source, second_source,
    patch_grad, region_grad, small_sum, up_sum, down_sum, first_sum, second_sum,
    vec, halves, half_sem, summed, pieces, piece_sem, pack, near, near_sem, total, far, far_sem, *streams,
):
    step = pl.program_id(0)
    tokens, count, _ = patches.shape
    rows = tokens * count
    place = Place(wins, dps)
    parts = [streams[Stream.PARTS * b : Stream.PARTS * (b + 1)] for b in range(4)]
    late = (Stream(place, first_source, first_sum, parts[0]), Stream(place, second_source, second_sum, parts[1]))
    early = (Stream(place, None, up_sum, parts[2]), Stream(place, None, down_sum, parts[3]))

    def window_rows(chip, core):
        return pl.ds(pl.multiple_of((chip * 2 + core) * count, 16), count)

    def to_core():
        return [pltpu.make_async_remote_copy(
            src_ref=terms.at[window_rows(chip, 1 - place.core)], dst_ref=halves.at[chip],
            send_sem=half_sem.at[2 * chip], recv_sem=half_sem.at[2 * chip + 1],
            device_id=place.other_core(), device_id_type=MESH,
        ) for chip in range(place.chips)]

    def to_owners():
        copies = []
        for j in range(1, place.chips):
            chip, to = place.at_chip(j)
            copies.append(pltpu.make_async_remote_copy(
                src_ref=summed.at[chip], dst_ref=pieces.at[j - 1],
                send_sem=piece_sem.at[2 * j - 2], recv_sem=piece_sem.at[2 * j - 1], device_id=to, device_id_type=MESH,
            ))
        return copies

    def to_near():
        return [pltpu.make_async_remote_copy(
            src_ref=pack, dst_ref=near.at[j - 1], send_sem=near_sem.at[2 * j - 2], recv_sem=near_sem.at[2 * j - 1],
            device_id={"win": lax.rem(place.win + j, wins)}, device_id_type=MESH,
        ) for j in range(1, wins)]

    def to_far():
        return [pltpu.make_async_remote_copy(
            src_ref=total, dst_ref=far.at[j - 1], send_sem=far_sem.at[2 * j - 2], recv_sem=far_sem.at[2 * j - 1],
            device_id=place.at_dp(j)[1], device_id_type=MESH,
        ) for j in range(1, dps)]

    def late_step(k):
        for s in late:
            s.step(k)

    def early_step(k):
        for s in early:
            s.step(k)

    def begin():
        place.greeted(all_wins=True)
        late_step(0)
        for c in to_core():
            c.start()
        for s, part in zip(early, (up_part, down_part)):
            s.begin_back(part)

    def owners_begin():
        for c in to_core():
            c.wait()

        def add(chip, carry):
            own = terms[window_rows(chip, place.core)].astype(f32)
            summed[chip] = (own + halves[chip].astype(f32)).astype(bf16)
            return carry

        lax.fori_loop(0, place.chips, add, 0)
        for c in to_owners():
            c.start()

    def region_end():
        for c in to_owners():
            c.wait()
        key_value = summed[place.chip].astype(f32)
        for j in range(place.chips - 1):
            key_value += pieces[j].astype(f32)
        vhat, inverse = norm_stats(regional[...].astype(f32))
        grad_in = nt(grad_query[...], w_qkv[:, :D]) + nt(key_value.astype(bf16), w_qkv[:, D:])
        region_grad[...] = (grad_mid[...] + norm_back(vhat, inverse, row(vecs, GAIN1), grad_in)).astype(bf16)
        vec[0:1] += col(grad_in * vhat)
        vec[1:2] += col(grad_in)

    def small_begin():
        pack[0:2] = vec[0:2]
        pack[2:3] = sums[:, :D]
        pack[3:4] = sums[:, 2 * D :]
        pack[4:5] = vec_mlp[2:3] + out_bias_part[...]
        pack[5:7] = vec_mlp[0:2]
        pack[7:8] = vec_mlp[3:4]
        for b in range(4):
            pack[8 + b : 9 + b] = up_bias_grad[:, D * b : D * (b + 1)]
        pack[12:16] = jnp.zeros((4, D), f32)
        for c in to_near():
            c.start()

    def small_middle():
        for c in to_near():
            c.wait()
        part = pack[...]
        for j in range(wins - 1):
            part += near[j]
        total[...] = part
        for c in to_far():
            c.start()

    def small_end():
        for c in to_far():
            c.wait()
        part = total[...]
        for j in range(dps - 1):
            part += far[j]
        small_sum[...] = part

    @pl.when(step == 0)
    def _():
        place.greet(all_wins=True)
        for s in late:
            s.load()
        vec[...] = jnp.zeros_like(vec)
        begin()

    x = with_region(patches[...].astype(f32), region_mid[...], step == pl.num_programs(0) - 1)
    vhat, inverse = norm_stats(x)
    grad_in = nt(grad_triple[...].reshape(rows, 3 * D), w_qkv[...])
    vec[0:1] += col(grad_in * vhat)
    vec[1:2] += col(grad_in)
    total_rows = grad_middle[...].reshape(rows, D).astype(f32) + norm_back(vhat, inverse, row(vecs, GAIN1), grad_in)
    patch_grad[...] = total_rows.astype(bf16).reshape(tokens, count, D)

    def end():
        late_step(3)
        owners_begin()
        early_step(6)
        late_step(4)
        region_end()
        small_begin()
        late_step(5)
        small_middle()
        late_step(6)
        early_step(7)
        small_end()
        late_step(7)
        early_step(8)
        late_step(8)

    def middle():
        late_step(2)
        early_step(5)

    hooks = {
        0: lambda: late_step(1),
        3: middle,
        4: end,
    }
    for when, todo in hooks.items():
        pl.when(step == when)(todo)


def last_kernel(
    up, down_t, first, second, small, patch_in, region_in,
    patch_grad, region_grad, in_gain, in_shift, qkv, qkv_bias, out_grad, out_bias, mlp_gain, mlp_shift,
    up_grad, up_bias, down_grad, down_bias,
):
    up_grad[...] = up[...].astype(f32)
    down_grad[...] = down_t[...].T.astype(f32)
    qkv[:, : 2 * D] = first[...].astype(f32)
    qkv[:, 2 * D :] = second[:, :D].astype(f32)
    out_grad[...] = second[:, D:].astype(f32)
    patch_grad[...] = patch_in[...]

    @pl.when(pl.program_id(0) == 0)
    def _():
        region_grad[...] = region_in[...]
        for at, v in ((0, in_gain), (1, in_shift), (4, out_bias), (5, mlp_gain), (6, mlp_shift), (7, down_bias)):
            v[...] = small[at : at + 1].reshape(D)
        qkv_bias[...] = small[2:4]
        up_bias[...] = jnp.concatenate([small[8 + b : 9 + b] for b in range(FF // D)], axis=1).reshape(FF)


def shards(
    wins, dps,
    patches, regional, window_image, in_gain, in_shift, w_qkv, qkv_bias, w_out, out_bias,
    mlp_gain, mlp_shift, w_up, up_bias, w_down, down_bias, patch_cot, region_cot,
):
    _, count, patch, _ = patches.shape
    group = window_image.shape[1]
    x = patches[0].transpose(1, 0, 2)
    cot = patch_cot[0].transpose(1, 0, 2)
    reg = regional[0]
    rcot = region_cot[0]
    const = lambda *arrays: [whole(a) for a in arrays]
    block = lambda a, n: (a, (n,) + a.shape[1:], lambda i: (i, 0, 0))
    block_out = lambda shape, n, dtype=bf16: ((shape, dtype), (n,) + shape[1:], lambda i: (i, 0, 0))
    triple, local_in, vecs, region_triple, gathered, probs_r, merged_r, region_mid, triple0, local_in0 = call(
        functools.partial(front_kernel, wins, dps), (pl.cdiv(patch, 7),),
        [block(x, 7)]
        + const(reg, window_image, in_gain, in_shift, w_qkv, qkv_bias, w_out, out_bias, mlp_gain, mlp_shift, up_bias, down_bias),
        [block_out((patch, count, 3 * D), 7), block_out((patch, count, D), 7), whole_out((16, D), f32), whole_out((count, 3 * D), bf16),
         whole_out((group, 3 * D), bf16), whole_out((2, group, 8 * count), bf16), whole_out((count, D), bf16),
         whole_out((count, D), f32), whole_out((count, 3 * D), bf16), whole_out((count, D), bf16)],
        [pltpu.VMEM((group, 3 * D), bf16), pltpu.VMEM((count, 3 * D), bf16), pltpu.VMEM((group, 128), f32),
         pltpu.SemaphoreType.DMA((8 * wins,))],
        name="front", collective_id=2,
    )
    steps = (count // WC,)
    mid = lambda a: (a, (a.shape[0], WC, a.shape[2]), lambda i: (0, i, 0))
    mid_out = lambda shape, dtype=bf16: ((shape, dtype), (shape[0], WC, shape[2]), lambda i: (0, i, 0))
    tail = lambda a: (a, (WC, a.shape[1]), lambda i: (i, 0))
    merged, probs = call(
        local_fwd_kernel, steps, [mid(triple), tail(triple0)],
        [mid_out((patch + 1, count, D)), ((((count, TP, HEADS * TP)), bf16), (WC, TP, HEADS * TP), lambda i: (i, 0, 0))],
        [pltpu.VMEM((12, TP * WC, 128), f32), pltpu.VMEM((4, TP * WC, 128), f32)], name="local_fwd",
    )
    n = 10
    rows_grid = ((patch + 1) // n,)
    patch_out, region_out, grad_middle, grad_merged, up_grad, down_grad_t, out_local, vec_mlp, up_bias_grad = call(
        mlp_kernel, rows_grid,
        [block(x, n), whole(region_mid), block(merged, n), block(cot, n)]
        + const(rcot, vecs, w_out, w_up, w_down),
        [block_out((patch, count, D), n), whole_out((count, D), bf16),
         block_out((patch + 1, count, D), n), block_out((patch + 1, count, D), n),
         whole_out((D, FF), bf16), whole_out((D, FF), bf16), whole_out((D, D), f32),
         whole_out((8, D), f32), whole_out((1, FF), f32)],
        [pltpu.VMEM((D, FF), f32), pltpu.VMEM((D, FF), f32)], name="mlp",
    )
    last_rows = rows_of(wins, dps)[1]
    grad_triple, up_part, down_part, terms, grad_query, low_first, low_second, sums, out_bias_part, grad_mid = call(
        functools.partial(back_kernel, wins, dps), steps,
        [mid(triple), tail(triple0), (probs, (WC, TP, HEADS * TP), lambda i: (i, 0, 0), group > 512), mid(grad_merged), mid(local_in), tail(local_in0)]
        + const(region_triple, gathered, probs_r, merged_r, region_mid)
        + [(grad_middle, (1, count, D), lambda i: (patch, 0, 0))]
        + const(vecs, w_qkv, w_out, out_local) + [left(a.reshape(stream_shape(wins, FF))) for a in (up_grad, down_grad_t)],
        [mid_out((patch + 1, count, 3 * D)), whole_out((last_rows, FF), bf16), whole_out((last_rows, FF), bf16),
         whole_out((group, 2 * D), bf16), whole_out((count, D), bf16), whole_out(stream_shape(wins, 2 * D), bf16),
         whole_out(stream_shape(wins, 2 * D), bf16),
         whole_out((1, 3 * D), f32), whole_out((1, D), f32), whole_out((count, D), f32)],
        [pltpu.VMEM((16, TP * WC, 128), f32), pltpu.VMEM((12, TP * WC, 128), f32), pltpu.VMEM((count, 3 * D), bf16),
         pltpu.VMEM((D, 3 * D), f32), pltpu.VMEM((count, D), bf16)]
        + stream_scratch(wins, dps, FF, "down") * 2,
        name="back", collective_id=0,
    )
    patch_grad, region_grad, small, up_sum, down_sum, first_sum, second_sum = call(
        functools.partial(tail_kernel, wins, dps), rows_grid,
        [block(x, n), block(grad_triple, n), block(grad_middle, n)]
        + const(region_mid, vecs, w_qkv, terms, grad_query, reg, grad_mid, vec_mlp, up_bias_grad, sums, out_bias_part, up_part, down_part)
        + [left(low_first), left(low_second)],
        [block_out((patch, count, D), n), whole_out((count, D), bf16), whole_out((16, D), f32)]
        + [left_out(stream_shape(wins, FF), bf16)] * 2 + [left_out(stream_shape(wins, 2 * D), bf16)] * 2,
        [pltpu.VMEM((8, D), f32),
         pltpu.VMEM((wins // 2, count, 2 * D), bf16), pltpu.SemaphoreType.DMA((wins,)), pltpu.VMEM((wins // 2, count, 2 * D), bf16),
         pltpu.VMEM((wins // 2, count, 2 * D), bf16), pltpu.SemaphoreType.DMA((wins,)),
         pltpu.VMEM((16, D), f32), pltpu.VMEM((wins - 1, 16, D), f32), pltpu.SemaphoreType.DMA((2 * wins,)),
         pltpu.VMEM((16, D), f32), pltpu.VMEM((max(dps - 1, 1), 16, D), f32), pltpu.SemaphoreType.DMA((2 * dps,))]
        + stream_scratch(wins, dps, 2 * D) * 2 + stream_scratch(wins, dps, FF, "back") * 2,
        name="tail", collective_id=1,
    )
    up_sum, down_sum = up_sum.reshape(D, FF), down_sum.reshape(D, FF)
    first_sum, second_sum = first_sum.reshape(D, 2 * D), second_sum.reshape(D, 2 * D)
    n = 4
    down = lambda i: (i, 0)
    vector = lambda size: ((((size,), f32)), (size,), lambda i: (0,))
    token = -(-patch // n)
    tokens = lambda i: (lax.min(i, (patch - 1) // token), 0, 0)
    (
        patch_grad, region_grad, in_gain_grad, in_shift_grad, qkv_grad, qkv_bias_grad, out_grad, out_bias_grad,
        mlp_gain_grad, mlp_shift_grad, up_grad, up_bias_grad, down_grad, down_bias_grad,
    ) = call(
        last_kernel, (n,),
        [(up_sum, (D // n, FF), down), (down_sum, (D, FF // n), lambda i: (0, i))]
        + [(a, (D // n, 2 * D), down) for a in (first_sum, second_sum)]
        + [whole(small), (patch_grad, (token, count, D), tokens), whole(region_grad)],
        [(((patch, count, D), bf16), (token, count, D), tokens), whole_out((count, D), bf16), vector(D), vector(D),
         (((D, 3 * D), f32), (D // n, 3 * D), down), whole_out((2, D), f32), (((D, D), f32), (D // n, D), down), vector(D),
         vector(D), vector(D), (((D, FF), f32), (D // n, FF), down), vector(FF), (((FF, D), f32), (FF // n, D), down), vector(D)],
        name="last",
    )
    return (
        patch_out.transpose(1, 0, 2)[None], region_out[None], patch_grad.transpose(1, 0, 2)[None], region_grad[None],
        in_gain_grad, in_shift_grad, qkv_grad, qkv_bias_grad, out_grad, out_bias_grad,
        mlp_gain_grad, mlp_shift_grad, up_grad, up_bias_grad, down_grad, down_bias_grad,
    )


def solution(mesh):
    wide = P("dp", "win", None, None)
    narrow = P("dp", "win", None)
    in_specs = (wide, narrow, P("dp", None)) + (P(),) * 12 + (wide, narrow)
    out_specs = (wide, narrow, wide, narrow) + (P(),) * 12
    return jax.shard_map(functools.partial(shards, mesh.shape["win"], mesh.shape["dp"]), mesh=mesh, in_specs=in_specs, out_specs=out_specs, check_vma=False)
```

```python
import functools

import jax
import jax.numpy as jnp
from jax import lax
from jax.experimental import pallas as pl
from jax.experimental.pallas import tpu as pltpu
from jax.sharding import PartitionSpec as P

D = 512
HEADS = 16
HD = 32
FF = 2048
EPSILON = 1e-06
MASKED_SCORE = -1e30
SCALING = HD ** (-0.5)
LOG2E = 1.4426950408889634
TP = 64
FB = 2048
WC = 16
f32 = jnp.float32
bf16 = jnp.bfloat16
VMEM_LIMIT = 60 * 2**20
MESH = pl.DeviceIdType.MESH
FRONT_SLOTS = (5, 6)
BACK_SLOTS = (
    (0, 0, (0,), (0,)), (0, 6, (1,), ()), (0, 16, (), (1,)), (1, 7, (2,), ()), (1, 16, (3,), (2,)), (2, 7, (), (3,)),
)


def nn(a, b):
    return lax.dot_general(a, b, (((1,), (0,)), ((), ())), preferred_element_type=f32)


def nt(a, b):
    return lax.dot_general(a, b, (((1,), (1,)), ((), ())), preferred_element_type=f32)


def tn(a, b):
    return lax.dot_general(a, b, (((0,), (0,)), ((), ())), preferred_element_type=f32)


def call(body, grid, ins, outs, scratch=(), name=None, collective_id=None, limit=VMEM_LIMIT):
    def spec(block, index, *single):
        if block is None:
            return pl.BlockSpec(memory_space=pl.ANY)
        if index is None:
            return pl.BlockSpec(block, lambda *_: (0,) * len(block), pipeline_mode=pl.Buffered(1))
        return pl.BlockSpec(block, index, pipeline_mode=pl.Buffered(1) if any(single) else None)

    return pl.pallas_call(
        body,
        grid=grid,
        in_specs=[spec(*entry[1:]) for entry in ins],
        out_specs=[spec(b, i) for _, b, i in outs],
        out_shape=[jax.ShapeDtypeStruct(s, d) for (s, d), _, _ in outs],
        scratch_shapes=list(scratch),
        compiler_params=pltpu.CompilerParams(
            vmem_limit_bytes=limit, collective_id=collective_id, has_side_effects=collective_id is not None
        ),
        name=name,
    )(*[entry[0] for entry in ins])


def whole(a):
    return (a, a.shape, None)


def whole_out(shape, dtype):
    return ((shape, dtype), shape, None)


def left(a):
    return (a, None, None)


def left_out(shape, dtype):
    return ((shape, dtype), None, None)


def norm_stats(rows):
    average = jnp.mean(rows, axis=-1, keepdims=True)
    centred = rows - average
    spread = jnp.mean(centred * centred, axis=-1, keepdims=True)
    inverse = lax.rsqrt(spread + EPSILON)
    return centred * inverse, inverse


def norm_back(vhat, inverse, gain, grad_out):
    scaled = grad_out * gain
    first = jnp.mean(scaled, axis=-1, keepdims=True)
    second = jnp.mean(scaled * vhat, axis=-1, keepdims=True)
    return inverse * (scaled - first - vhat * second)


def col(x):
    return jnp.sum(x, axis=0, keepdims=True)


class Place:
    def __init__(self, wins, dps):
        self.wins, self.dps = wins, dps
        self.win = lax.axis_index("win")
        self.dp = lax.axis_index("dp")
        self.core = lax.rem(self.win, 2)
        self.chip = self.win // 2
        self.chips = wins // 2
        self.square = self.chips == 4
        self.a = self.chip // 2
        self.b = lax.rem(self.chip, 2)

    def other_core(self):
        return {"win": self.chip * 2 + 1 - self.core}

    def other_a(self):
        return {"win": ((1 - self.a) * 2 + self.b) * 2 + self.core}

    def other_b(self):
        return {"win": (self.a * 2 + 1 - self.b) * 2 + self.core}

    def at_chip(self, j):
        chip = lax.rem(self.chip + j, self.chips)
        return chip, {"win": chip * 2 + self.core}

    def at_dp(self, j):
        dp = lax.rem(self.dp + j, self.dps)
        return dp, {"dp": dp}

    def near(self, all_wins, around=False):
        if all_wins:
            return [{"win": lax.rem(self.win + j, self.wins)} for j in range(1, self.wins)]
        if self.square and not around:
            return [self.other_core(), self.other_a(), self.other_b()]
        return [self.other_core()] + [self.at_chip(j)[1] for j in range(1, self.chips)]

    def partners(self, all_wins, along, around):
        return self.near(all_wins, around) + [self.at_dp(j)[1] for j in range(1, self.dps if along else 1)]

    def greet(self, all_wins=False, along=True, around=False):
        barrier = pltpu.get_barrier_semaphore()
        for to in self.partners(all_wins, along, around):
            pl.semaphore_signal(barrier, inc=1, device_id=to, device_id_type=MESH)

    def greeted(self, all_wins=False, along=True, around=False):
        pl.semaphore_wait(pltpu.get_barrier_semaphore(), len(self.partners(all_wins, along, around)))


def rows_of(wins, dps):
    piece = D // wins
    return piece, piece // dps if piece % (16 * dps) == 0 else piece


def stream_shape(wins, columns):
    return (2, wins // 2, D // wins, columns)


def stream_scratch(wins, dps, columns, kind="whole"):
    piece, last = rows_of(wins, dps)
    chips = wins // 2
    landing = (4, 2, piece, columns // 2) if chips == 4 else (max(chips - 1, 1), piece, columns)
    half, part, some = pltpu.VMEM((chips, piece, columns), bf16), pltpu.VMEM((piece, columns), bf16), pltpu.VMEM((16, 128), bf16)
    down = kind != "back"
    return [
        half if down else some,
        half,
        pltpu.VMEM(landing, bf16) if down else some,
        part if down else some,
        pltpu.VMEM((max(dps - 1, 1), last, columns), bf16) if down else some,
        some if kind == "down" else part,
        pltpu.SemaphoreType.DMA((20 + 4 * chips + 4 * dps,)),
    ]


def columns_of(refs):
    return refs[1].shape[2]


class Stream:
    PARTS = 7

    def __init__(self, place, source, final, refs):
        self.p = place
        self.source, self.final = source, final
        self.own, self.r1, self.r2, self.s, self.r3, self.s2, self.sem = refs
        self.piece, self.last = rows_of(place.wins, place.dps)
        self.split = self.last != self.piece
        columns = columns_of(refs)
        self.left, self.right = pl.ds(0, columns // 2), pl.ds(columns // 2, columns // 2)

    def rows(self, start, size):
        return pl.ds(pl.multiple_of(start, 16), size)

    def remote(self, src, dst, to, k):
        return pltpu.make_async_remote_copy(
            src_ref=src, dst_ref=dst, send_sem=self.sem.at[2 * k], recv_sem=self.sem.at[2 * k + 1],
            device_id=to, device_id_type=MESH,
        )

    def _own(self):
        return pltpu.make_async_copy(self.source.at[self.p.core], self.own, self.sem.at[0])

    def _put(self):
        return pltpu.make_async_copy(self.r1, self.final.at[self.p.core], self.sem.at[1])

    def _cores(self):
        return [self.remote(self.source.at[1 - self.p.core], self.r1, self.p.other_core(), 1)]

    def _cores_back(self):
        return [self.remote(self.r1, self.final.at[self.p.core], self.p.other_core(), 2)]

    def _chips_left(self, k):
        p = self.p
        if k == 0:
            return [self.remote(self.own.at[c * 2 + 1 - p.b, :, self.left], self.r2.at[0, c], p.other_b(), 3 + c) for c in range(2)]
        return [self.remote(self.own.at[(1 - p.a) * 2 + p.b, :, self.left], self.r2.at[2, 0], p.other_a(), 5)]

    def _chips_right(self, k):
        p = self.p
        if k == 0:
            return [self.remote(self.own.at[(1 - p.a) * 2 + c, :, self.right], self.r2.at[1, c], p.other_a(), 6 + c) for c in range(2)]
        return [self.remote(self.own.at[p.a * 2 + 1 - p.b, :, self.right], self.r2.at[3, 0], p.other_b(), 8)]

    def _back_left(self, k):
        p = self.p
        mine = self.r1
        if k == 0:
            return [self.remote(self.s2.at[:, self.left], mine.at[p.chip, :, self.left], p.other_a(), 9)]
        rows = [mine.at[c * 2 + p.b, :, self.left] for c in range(2)]
        return [self.remote(rows[c], rows[c], p.other_b(), 10 + c) for c in range(2)]

    def _back_right(self, k):
        p = self.p
        mine = self.r1
        if k == 0:
            return [self.remote(self.s2.at[:, self.right], mine.at[p.chip, :, self.right], p.other_b(), 12)]
        rows = [mine.at[p.a * 2 + c, :, self.right] for c in range(2)]
        return [self.remote(rows[c], rows[c], p.other_a(), 13 + c) for c in range(2)]

    def _chips(self):
        out = []
        for j in range(1, self.p.chips):
            chip, to = self.p.at_chip(j)
            out.append(self.remote(self.own.at[chip], self.r2.at[j - 1], to, 2 + j))
        return out

    def _chips_back(self):
        out = []
        for j in range(1, self.p.chips):
            mine = self.r1.at[self.p.chip]
            out.append(self.remote(self.s2, mine, self.p.at_chip(j)[1], 2 + self.p.chips + j))
        return out

    def _dps(self):
        out = []
        for j in range(1, self.p.dps):
            dp, to = self.p.at_dp(j)
            src = self.s.at[self.rows(dp * self.last, self.last)] if self.split else self.s
            out.append(self.remote(src, self.r3.at[j - 1], to, 8 + 2 * self.p.chips + j))
        return out

    def _dps_back(self):
        out = []
        if self.split:
            for j in range(1, self.p.dps):
                mine = self.s2.at[self.rows(self.p.dp * self.last, self.last)]
                out.append(self.remote(mine, mine, self.p.at_dp(j)[1], 8 + 2 * self.p.chips + self.p.dps + j))
        return out

    def start(self, copies):
        for c in copies:
            c.start()

    def wait(self, copies):
        for c in copies:
            c.wait()

    def load(self):
        self._own().start()

    def send_cores(self):
        self.start(self._cores())

    def send_chips(self):
        self._own().wait()
        self.wait(self._cores())

        def add(i, carry):
            self.own[i] = (self.own[i].astype(f32) + self.r1[i].astype(f32)).astype(bf16)
            return carry

        lax.fori_loop(0, self.p.chips, add, 0)
        if self.p.square:
            self.start(self._chips_left(0))
            self.start(self._chips_right(0))
        else:
            self.start(self._chips())

    def add_square(self, chip, lanes, slot, c):
        self.own[chip, :, lanes] = (self.own[chip, :, lanes].astype(f32) + self.r2[slot, c].astype(f32)).astype(bf16)

    def send_chips_again(self):
        p = self.p
        if p.square:
            self.wait(self._chips_left(0))
            for c in range(2):
                self.add_square(c * 2 + p.b, self.left, 0, c)
            self.start(self._chips_left(1))
            self.wait(self._chips_right(0))
            for c in range(2):
                self.add_square(p.a * 2 + c, self.right, 1, c)
            self.start(self._chips_right(1))

    def send_dps(self):
        p = self.p
        if p.square:
            for lanes, slot, copies in ((self.left, 2, self._chips_left(1)), (self.right, 3, self._chips_right(1))):
                self.wait(copies)
                self.s[:, lanes] = (self.own[p.chip, :, lanes].astype(f32) + self.r2[slot, 0].astype(f32)).astype(bf16)
        else:
            self.wait(self._chips())
            total = self.own[p.chip].astype(f32)
            for j in range(p.chips - 1):
                total += self.r2[j].astype(f32)
            self.s[...] = total.astype(bf16)
        self.start(self._dps())

    def sum_dps(self, out, at):
        self.wait(self._dps())
        mine = self.part()
        total = self.s[mine].astype(f32)
        for j in range(self.p.dps - 1):
            total += self.r3[j].astype(f32)
        out[at] = total.astype(bf16)

    def part(self):
        return self.rows(self.p.dp * self.last if self.split else 0, self.last)

    def send_dps_back(self):
        self.sum_dps(self.s2, self.part())
        self.start(self._dps_back())

    def end_dps_back(self):
        self.wait(self._dps_back())

    def begin_back(self, part):
        self.s2[self.part()] = part[...]
        self.start(self._dps_back())

    def send_chips_back(self):
        self.end_dps_back()
        self.start_chips_back()

    def start_chips_back(self):
        self.r1[self.p.chip] = self.s2[...]
        if self.p.square:
            self.start(self._back_left(0))
            self.start(self._back_right(0))
        else:
            self.start(self._chips_back())

    def send_chips_back_again(self):
        if self.p.square:
            self.wait(self._back_left(0))
            self.start(self._back_left(1))
            self.wait(self._back_right(0))
            self.start(self._back_right(1))
        else:
            self.wait(self._chips_back())

    def send_cores_back(self):
        if self.p.square:
            self.wait(self._back_left(1))
            self.wait(self._back_right(1))
        self.start(self._cores_back())
        self._put().start()

    def finish(self):
        self.wait(self._cores_back())
        self._put().wait()

    STEPS = (
        "send_cores", "send_chips", "send_chips_again", "send_dps", "send_dps_back",
        "send_chips_back", "send_chips_back_again", "send_cores_back", "finish",
    )

    def step(self, k):
        if 0 <= k < len(self.STEPS):
            getattr(self, self.STEPS[k])()


def expand_group(x, heads):
    lane = lax.broadcasted_iota(jnp.int32, (1, x.shape[1]), 1) // HD
    return jnp.concatenate([jnp.where(lane == i, x, jnp.zeros_like(x)) for i in range(heads)], axis=0)


def fold_group(y, heads):
    rows = y.shape[0] // heads
    lane = lax.broadcasted_iota(jnp.int32, (1, y.shape[1]), 1) // HD
    total = y[(heads - 1) * rows :]
    for i in range(heads - 2, -1, -1):
        total = jnp.where(lane == i, y[i * rows : (i + 1) * rows], total)
    return total


GAIN1, SHIFT1, GAIN2, SHIFT2, OUT_BIAS, DOWN_BIAS, QUERY_BIAS, KEY_BIAS, VALUE_BIAS, UP_BIAS = range(10)


def row(vecs, at):
    return vecs[at : at + 1]


def normed_low(vhat, vecs, gain, shift):
    return (vhat * row(vecs, gain) + row(vecs, shift)).astype(bf16)


def front_kernel(
    wins, dps,
    patches, regional, images, in_gain, in_shift, w_qkv, qkv_bias, w_out, out_bias, mlp_gain, mlp_shift, up_bias, down_bias,
    triple, local_in, vecs, region_triple, gathered_out, probs, merged, region_mid, triple0, local_in0,
    gathered, packed, image_col, sem,
):
    step = pl.program_id(0)
    place = Place(wins, dps)
    count = regional.shape[0]
    group = gathered.shape[0]
    mine = pl.ds(pl.multiple_of(place.win * count, 16), count)

    def project(normed):
        out = nn(normed, w_qkv[...])
        return jnp.concatenate(
            [out[:, :D] + row(vecs, QUERY_BIAS), out[:, D : 2 * D], out[:, 2 * D :] + row(vecs, VALUE_BIAS)], axis=1
        ).astype(bf16)

    parts = (pl.ds(0, 2 * D), pl.ds(2 * D, D))

    def remote(src, dst, to, k):
        return pltpu.make_async_remote_copy(
            src_ref=src, dst_ref=dst, send_sem=sem.at[2 * k], recv_sem=sem.at[2 * k + 1], device_id=to, device_id_type=MESH
        )

    def direct(part):
        lanes, first = parts[part], 2 * place.chips * part
        targets = [place.other_core()] + [place.at_chip(j)[1] for j in range(1, place.chips)]
        return [remote(packed.at[:, lanes], gathered.at[mine, lanes], to, first + j) for j, to in enumerate(targets)]

    def onward(part):
        lanes, first = parts[part], 2 * place.chips * part + place.chips
        copies = []
        for j in range(1, place.chips):
            chip = lax.rem(place.chip - j + place.chips, place.chips)
            theirs = gathered.at[pl.ds(pl.multiple_of((chip * 2 + place.core) * count, 16), count), lanes]
            copies.append(remote(theirs, theirs, place.other_core(), first + j))
        return copies

    def pass_on(part):
        for c in direct(part):
            c.wait()
        for c in onward(part):
            c.start()

    @pl.when(step == 0)
    def _():
        place.greet(around=True, along=False)
        for at, v in (
            (GAIN1, in_gain), (SHIFT1, in_shift), (GAIN2, mlp_gain), (SHIFT2, mlp_shift), (OUT_BIAS, out_bias), (DOWN_BIAS, down_bias),
        ):
            vecs[at : at + 1] = v[...].astype(f32).reshape(1, D)
        vecs[QUERY_BIAS : QUERY_BIAS + 1] = qkv_bias[0:1].astype(f32)
        vecs[KEY_BIAS : KEY_BIAS + 1] = jnp.zeros((1, D), f32)
        vecs[VALUE_BIAS : VALUE_BIAS + 1] = qkv_bias[1:2].astype(f32)
        up = up_bias[...].astype(f32).reshape(1, FF)
        for b in range(FF // D):
            vecs[UP_BIAS + b : UP_BIAS + b + 1] = up[:, D * b : D * (b + 1)]
        vecs[UP_BIAS + FF // D : 16] = jnp.zeros((16 - UP_BIAS - FF // D, D), f32)
        vhat, _ = norm_stats(regional[...].astype(f32))
        normed = normed_low(vhat, vecs, GAIN1, SHIFT1)
        own = project(normed)
        region_triple[...] = own
        packed[:, : 2 * D] = own[:, D:]
        packed[:, 2 * D :] = normed
        gathered[mine] = packed[...]
        place.greeted(around=True, along=False)
        for part in range(2):
            for c in direct(part):
                c.start()
        ids = images[...].astype(f32)
        image_col[...] = jnp.broadcast_to(ids, (128, group)).T

    rows = patches.shape[0] * count
    vhat, _ = norm_stats(patches[...].reshape(rows, D).astype(f32))
    normed_rows = normed_low(vhat, vecs, GAIN1, SHIFT1)
    local_in[...] = normed_rows.reshape(local_in.shape)
    triple[...] = project(normed_rows).reshape(triple.shape)

    for part, when in enumerate(FRONT_SLOTS):
        pl.when(step == when)(functools.partial(pass_on, part))

    @pl.when(step == pl.num_programs(0) - 1)
    def _():
        for c in onward(0):
            c.wait()
        own_ids = image_col[mine]
        own_row = jnp.concatenate([own_ids] * 8, axis=0).T[0:1]
        same = image_col[:, 0:1] == own_row
        for g in range(2):
            lanes = slice(256 * g, 256 * g + 256)
            scores = nt(gathered[:, lanes], expand_group(region_triple[:, lanes], 8))
            scores = jnp.where(same, scores * SCALING, MASKED_SCORE)
            top = jnp.max(scores, axis=0, keepdims=True)
            exps = jnp.exp2((scores - top) * LOG2E)
            low = (exps * (1.0 / col(exps))).astype(bf16)
            probs[g] = low
            merged[:, lanes] = fold_group(tn(low, gathered[:, D + 256 * g : D + 256 * g + 256]), 8).astype(bf16)
        mid = regional[...].astype(f32) + nn(merged[...], w_out[...]) + row(vecs, OUT_BIAS)
        region_mid[...] = mid
        vhat_mid, _ = norm_stats(mid)
        normed_mid = normed_low(vhat_mid, vecs, GAIN1, SHIFT1)
        local_in0[...] = normed_mid
        triple0[...] = project(normed_mid)
        for c in onward(1):
            c.wait()
        gathered_out[...] = gathered[...]


def expand(x):
    lane = lax.broadcasted_iota(jnp.int32, (1, 128), 1) // HD
    return jnp.concatenate([jnp.where(lane == i, x, jnp.zeros_like(x)) for i in range(4)], axis=0)


def query_side(rows, weights):
    return fold_group(tn(weights, rows), 4)


def load_triple(t, triple, triple0, patch):
    for b in range(12):
        lanes = slice(128 * b, 128 * b + 128)
        t[b, 0 : patch * WC] = triple[:, :, lanes].reshape(patch * WC, 128).astype(f32)
        t[b, patch * WC : (patch + 1) * WC] = triple0[:, lanes].astype(f32)
        t[b, (patch + 1) * WC :] = jnp.zeros(((TP - patch - 1) * WC, 128), f32)


def local_fwd_kernel(triple, triple0, merged, probs, t, m):
    patch = triple.shape[0]
    load_triple(t, triple, triple0, patch)
    row = lax.broadcasted_iota(jnp.int32, (TP, 1), 0)

    def one(w):
        for b in range(4):
            q = t[b, pl.ds(w, TP, stride=WC), :].astype(bf16)
            k = t[4 + b, pl.ds(w, TP, stride=WC), :].astype(bf16)
            v = t[8 + b, pl.ds(w, TP, stride=WC), :].astype(bf16)
            scores = nt(k, expand(q))
            scores = jnp.where(row <= patch, scores, MASKED_SCORE)
            top = jnp.max(scores, axis=0, keepdims=True)
            exps = jnp.exp2((scores - top) * (SCALING * LOG2E))
            low = (exps * (1.0 / col(exps))).astype(bf16)
            probs[w, :, 256 * b : 256 * b + 256] = low
            m[b, pl.ds(w, TP, stride=WC), :] = query_side(v, low)

    for w in range(WC):
        one(w)
    for b in range(4):
        merged[:, :, 128 * b : 128 * b + 128] = m[b, 0 : (patch + 1) * WC].astype(bf16).reshape(patch + 1, WC, 128)


def local_bwd_step(w, probs, t, d):
    at = pl.ds(w, TP, stride=WC)
    for b in range(4):
        q = t[b, at, :].astype(bf16)
        k = t[4 + b, at, :].astype(bf16)
        v = t[8 + b, at, :].astype(bf16)
        g = t[12 + b, at, :].astype(bf16)
        qx = expand(q)
        gx = expand(g)
        low = probs[w, :, 256 * b : 256 * b + 256]
        high = low.astype(f32)
        scaled = high * nt(v, gx)
        back = (scaled - high * col(scaled)).astype(bf16)
        d[4 + b, at, :] = nn(back, qx) * SCALING
        d[8 + b, at, :] = nn(low, gx)
        d[b, at, :] = query_side(k, back) * SCALING


def back_kernel(
    wins, dps,
    triple, triple0, probs, grad_merged, local_in, local_in0,
    region_triple, gathered, probs_r, merged_r, region_mid, grad_middle0, vecs, w_qkv, w_out, out_local,
    up_source, down_source,
    grad_triple, up_part, down_part, terms, grad_query, low_first, low_second, sums, out_bias_part, grad_mid,
    t, d, d0, qkv_acc, grad_merged_s, *streams,
):
    step = pl.program_id(0)
    place = Place(wins, dps)
    up = Stream(place, up_source, None, streams[: Stream.PARTS])
    down = Stream(place, down_source, None, streams[Stream.PARTS :])

    @pl.when(step == 0)
    def _():
        place.greet()
        up.load()
        down.load()
        qkv_acc[...] = jnp.zeros_like(qkv_acc)
        sums[...] = jnp.zeros_like(sums)

    patch = triple.shape[0]
    load_triple(t, triple, triple0, patch)
    rows = (patch + 1) * WC
    for b in range(4):
        t[12 + b, 0:rows] = grad_merged[:, :, 128 * b : 128 * b + 128].reshape(rows, 128).astype(f32)
        t[12 + b, rows:] = jnp.zeros((TP * WC - rows, 128), f32)

    def end():
        for s, part in ((up, up_part), (down, down_part)):
            s.sum_dps(part, slice(None))

    def reached(w):
        if w == 0:
            pl.when(step == 0)(place.greeted)
        for when, after, ups, downs in BACK_SLOTS:
            if after == w:

                @pl.when(step == when)
                def _(ups=ups, downs=downs):
                    for k in ups:
                        up.step(k)
                    for k in downs:
                        down.step(k)

    for w in range(WC):
        local_bwd_step(w, probs, t, d)
        reached(w)
    at = pl.ds(pl.multiple_of(step * WC, WC), WC)
    for b in range(12):
        lanes = slice(128 * b, 128 * b + 128)
        low = d[b, 0:rows].astype(bf16)
        grad_triple[:, :, lanes] = low.reshape(patch + 1, WC, 128)
        d0[at, lanes] = low[rows - WC :]
        sums[:, lanes] += col(low.astype(f32))
    normed = jnp.concatenate([local_in[...].reshape(patch * WC, D), local_in0[...]], axis=0).T
    for b in range(3):
        lanes = slice(D * b, D * (b + 1))
        qkv_acc[:, lanes] += nn(normed, grad_triple[:, :, lanes].reshape(rows, D))

    reached(WC)

    @pl.when(step == pl.num_programs(0) - 1)
    def _():
        vhat, inverse = norm_stats(region_mid[...])
        mid = grad_middle0[0].astype(f32) + norm_back(vhat, inverse, row(vecs, GAIN1), nt(d0[...], w_qkv[...]))
        grad_mid[...] = mid
        grad_attn = mid.astype(bf16)
        out_low = (out_local[...] + tn(merged_r[...], grad_attn)).astype(bf16)
        out_bias_part[...] = col(grad_attn.astype(f32))
        grad_merged_r = nt(grad_attn, w_out[...]).astype(bf16)
        grad_merged_s[...] = grad_merged_r

        keys = gathered.shape[0]
        width = 8 * region_triple.shape[0]
        blocks = max(keys // width, 1) if keys % width == 0 else 1
        size = keys // blocks

        def group_half(g, carry):
            lanes = pl.ds(pl.multiple_of(256 * g, 256), 256)
            value_lanes = pl.ds(pl.multiple_of(D + 256 * g, 256), 256)
            qx = expand_group(region_triple[:, lanes], 8)
            gx = expand_group(grad_merged_s[:, lanes], 8)

            def scaled_at(at):
                high = probs_r[g, at].astype(f32)
                return high, high * nt(gathered[at, value_lanes], gx)

            def finish(at, row_terms, scaled=None):
                high, scaled = scaled_at(at) if scaled is None else scaled
                back = (scaled - high * row_terms).astype(bf16)
                terms[at, lanes] = (nn(back, qx) * SCALING).astype(bf16)
                terms[at, value_lanes] = nn(probs_r[g, at], gx).astype(bf16)
                return tn(back, gathered[at, lanes])

            if blocks == 1:
                both = scaled_at(pl.ds(0, keys))
                total = finish(pl.ds(0, keys), col(both[1]), both)
            else:
                at = lambda i: pl.ds(pl.multiple_of(i * size, 16), size)
                row_terms = lax.fori_loop(
                    0, blocks, lambda i, r: r + col(scaled_at(at(i))[1]), jnp.zeros((1, width), f32)
                )
                total = lax.fori_loop(
                    0, blocks, lambda i, q: q + finish(at(i), row_terms), jnp.zeros((width, 256), f32)
                )
            grad_query[:, lanes] = (fold_group(total, 8) * SCALING).astype(bf16)
            return carry

        if blocks == 1:
            group_half(0, 0)
            group_half(1, 0)
        else:
            lax.fori_loop(0, 2, group_half, 0)
        sums[:, :D] += col(grad_query[...].astype(f32))
        sums[:, D:] += col(terms[...].astype(f32))
        region_in_all = gathered[:, 2 * D :]
        own_in = gathered[pl.ds(pl.multiple_of(place.win * region_triple.shape[0], 16), region_triple.shape[0]), 2 * D :]
        shape = low_first.shape[:3] + (D,)
        low_first[:, :, :, :D] = (qkv_acc[:, :D] + tn(own_in, grad_query[...])).astype(bf16).reshape(shape)
        low_first[:, :, :, D:] = (qkv_acc[:, D : 2 * D] + tn(region_in_all, terms[:, :D])).astype(bf16).reshape(shape)
        low_second[:, :, :, :D] = (qkv_acc[:, 2 * D :] + tn(region_in_all, terms[:, D:])).astype(bf16).reshape(shape)
        low_second[:, :, :, D:] = out_low.reshape(shape)
        end()


def gelu_both(v):
    e = jnp.exp2(v * v * (-0.5 * LOG2E))
    cdf = 0.5 + 0.5 * lax.erf(v * (0.5**0.5))
    return v * cdf, cdf + v * e * 0.3989422804014327


def with_region(block, region, last):
    tokens, count, width = block.shape
    head = block[0 : tokens - 1].reshape((tokens - 1) * count, width)
    tail = jnp.where(last, region, block[tokens - 1])
    return jnp.concatenate([head, tail], axis=0)


def mlp_kernel(
    patches, region_mid, merged, patch_cot, region_cot, vecs, w_out, w_up, w_down,
    patch_out, region_out, grad_middle, grad_merged, up_grad, down_grad_t, out_grad, vec512, up_bias_grad,
    up_acc, down_acc,
):
    step = pl.program_id(0)
    last = step == pl.num_programs(0) - 1
    tokens, count, _ = patches.shape
    rows = tokens * count

    @pl.when(step == 0)
    def _():
        up_acc[...] = jnp.zeros_like(up_acc)
        down_acc[...] = jnp.zeros_like(down_acc)
        out_grad[...] = jnp.zeros_like(out_grad)
        vec512[...] = jnp.zeros_like(vec512)
        up_bias_grad[...] = jnp.zeros_like(up_bias_grad)

    x = with_region(patches[...].astype(f32), region_mid[...], last)
    grad_result = with_region(patch_cot[...], region_cot[...], last)
    low_merged = merged[...].reshape(rows, D)
    middle = x + nn(low_merged, w_out[...]) + row(vecs, OUT_BIAS)
    vhat, inverse = norm_stats(middle)
    mlp_in = normed_low(vhat, vecs, GAIN2, SHIFT2)
    mlp_in_t = mlp_in.T
    grad_result_t = grad_result.T
    result = middle + row(vecs, DOWN_BIAS)
    grad_in = jnp.zeros((rows, D), f32)
    up_row = jnp.concatenate([row(vecs, UP_BIAS + b) for b in range(FF // D)], axis=1)
    for f in range(FF // FB):
        at = slice(FB * f, FB * f + FB)
        hidden = nn(mlp_in, w_up[:, at]) + up_row[:, at]
        active, slope = gelu_both(hidden)
        active = active.astype(bf16)
        grad_hidden = (nt(grad_result, w_down[at, :]) * slope).astype(bf16)
        result += nn(active, w_down[at, :])
        grad_in += nt(grad_hidden, w_up[:, at])
        up_acc[:, at] += nn(mlp_in_t, grad_hidden)
        down_acc[:, at] += nn(grad_result_t, active)
        up_bias_grad[:, at] += col(grad_hidden.astype(f32))
    shown = result.astype(bf16)
    patch_out[...] = shown.reshape(tokens, count, D)
    region_out[...] = shown[rows - count :]
    gm = grad_result.astype(f32) + norm_back(vhat, inverse, row(vecs, GAIN2), grad_in)
    low_gm = gm.astype(bf16)
    grad_middle[...] = low_gm.reshape(tokens, count, D)
    out_grad[...] += nn(low_merged.T, low_gm)
    grad_merged[...] = nt(low_gm, w_out[...]).astype(bf16).reshape(tokens, count, D)
    vec512[0:1] += col(grad_in * vhat)
    vec512[1:2] += col(grad_in)
    vec512[2:3] += col(low_gm.astype(f32))
    vec512[3:4] += col(grad_result.astype(f32))

    @pl.when(last)
    def _():
        up_grad[...] = up_acc[...].astype(bf16)
        down_grad_t[...] = down_acc[...].astype(bf16)


def tail_kernel(
    wins, dps,
    patches, grad_triple, grad_middle, region_mid, vecs, w_qkv, terms, grad_query,
    regional, grad_mid, vec_mlp, up_bias_grad, sums, out_bias_part, up_part, down_part, first_source, second_source,
    patch_grad, region_grad, small_sum, up_sum, down_sum, first_sum, second_sum,
    vec, halves, half_sem, summed, pieces, piece_sem, pack, near, near_sem, total, far, far_sem, *streams,
):
    step = pl.program_id(0)
    tokens, count, _ = patches.shape
    rows = tokens * count
    place = Place(wins, dps)
    parts = [streams[Stream.PARTS * b : Stream.PARTS * (b + 1)] for b in range(4)]
    late = (Stream(place, first_source, first_sum, parts[0]), Stream(place, second_source, second_sum, parts[1]))
    early = (Stream(place, None, up_sum, parts[2]), Stream(place, None, down_sum, parts[3]))

    def window_rows(chip, core):
        return pl.ds(pl.multiple_of((chip * 2 + core) * count, 16), count)

    def to_core():
        return [pltpu.make_async_remote_copy(
            src_ref=terms.at[window_rows(chip, 1 - place.core)], dst_ref=halves.at[chip],
            send_sem=half_sem.at[2 * chip], recv_sem=half_sem.at[2 * chip + 1],
            device_id=place.other_core(), device_id_type=MESH,
        ) for chip in range(place.chips)]

    def to_owners():
        copies = []
        for j in range(1, place.chips):
            chip, to = place.at_chip(j)
            copies.append(pltpu.make_async_remote_copy(
                src_ref=summed.at[chip], dst_ref=pieces.at[j - 1],
                send_sem=piece_sem.at[2 * j - 2], recv_sem=piece_sem.at[2 * j - 1], device_id=to, device_id_type=MESH,
            ))
        return copies

    def to_near():
        return [pltpu.make_async_remote_copy(
            src_ref=pack, dst_ref=near.at[j - 1], send_sem=near_sem.at[2 * j - 2], recv_sem=near_sem.at[2 * j - 1],
            device_id={"win": lax.rem(place.win + j, wins)}, device_id_type=MESH,
        ) for j in range(1, wins)]

    def to_far():
        return [pltpu.make_async_remote_copy(
            src_ref=total, dst_ref=far.at[j - 1], send_sem=far_sem.at[2 * j - 2], recv_sem=far_sem.at[2 * j - 1],
            device_id=place.at_dp(j)[1], device_id_type=MESH,
        ) for j in range(1, dps)]

    def late_step(k):
        for s in late:
            s.step(k)

    def early_step(k):
        for s in early:
            s.step(k)

    def begin():
        place.greeted(all_wins=True)
        late_step(0)
        for c in to_core():
            c.start()
        for s, part in zip(early, (up_part, down_part)):
            s.begin_back(part)

    def owners_begin():
        for c in to_core():
            c.wait()

        def add(chip, carry):
            own = terms[window_rows(chip, place.core)].astype(f32)
            summed[chip] = (own + halves[chip].astype(f32)).astype(bf16)
            return carry

        lax.fori_loop(0, place.chips, add, 0)
        for c in to_owners():
            c.start()

    def region_end():
        for c in to_owners():
            c.wait()
        key_value = summed[place.chip].astype(f32)
        for j in range(place.chips - 1):
            key_value += pieces[j].astype(f32)
        vhat, inverse = norm_stats(regional[...].astype(f32))
        grad_in = nt(grad_query[...], w_qkv[:, :D]) + nt(key_value.astype(bf16), w_qkv[:, D:])
        region_grad[...] = (grad_mid[...] + norm_back(vhat, inverse, row(vecs, GAIN1), grad_in)).astype(bf16)
        vec[0:1] += col(grad_in * vhat)
        vec[1:2] += col(grad_in)

    def small_begin():
        pack[0:2] = vec[0:2]
        pack[2:3] = sums[:, :D]
        pack[3:4] = sums[:, 2 * D :]
        pack[4:5] = vec_mlp[2:3] + out_bias_part[...]
        pack[5:7] = vec_mlp[0:2]
        pack[7:8] = vec_mlp[3:4]
        for b in range(4):
            pack[8 + b : 9 + b] = up_bias_grad[:, D * b : D * (b + 1)]
        pack[12:16] = jnp.zeros((4, D), f32)
        for c in to_near():
            c.start()

    def small_middle():
        for c in to_near():
            c.wait()
        part = pack[...]
        for j in range(wins - 1):
            part += near[j]
        total[...] = part
        for c in to_far():
            c.start()

    def small_end():
        for c in to_far():
            c.wait()
        part = total[...]
        for j in range(dps - 1):
            part += far[j]
        small_sum[...] = part

    @pl.when(step == 0)
    def _():
        place.greet(all_wins=True)
        for s in late:
            s.load()
        vec[...] = jnp.zeros_like(vec)
        begin()

    x = with_region(patches[...].astype(f32), region_mid[...], step == pl.num_programs(0) - 1)
    vhat, inverse = norm_stats(x)
    grad_in = nt(grad_triple[...].reshape(rows, 3 * D), w_qkv[...])
    vec[0:1] += col(grad_in * vhat)
    vec[1:2] += col(grad_in)
    total_rows = grad_middle[...].reshape(rows, D).astype(f32) + norm_back(vhat, inverse, row(vecs, GAIN1), grad_in)
    patch_grad[...] = total_rows.astype(bf16).reshape(tokens, count, D)

    def end():
        late_step(3)
        owners_begin()
        early_step(6)
        late_step(4)
        region_end()
        small_begin()
        late_step(5)
        small_middle()
        late_step(6)
        early_step(7)
        small_end()
        late_step(7)
        early_step(8)
        late_step(8)

    def middle():
        late_step(2)
        early_step(5)

    hooks = {
        0: lambda: late_step(1),
        3: middle,
        4: end,
    }
    for when, todo in hooks.items():
        pl.when(step == when)(todo)


def last_kernel(
    up, down_t, first, second, small, patch_in, region_in,
    patch_grad, region_grad, in_gain, in_shift, qkv, qkv_bias, out_grad, out_bias, mlp_gain, mlp_shift,
    up_grad, up_bias, down_grad, down_bias,
):
    up_grad[...] = up[...].astype(f32)
    down_grad[...] = down_t[...].T.astype(f32)
    qkv[:, : 2 * D] = first[...].astype(f32)
    qkv[:, 2 * D :] = second[:, :D].astype(f32)
    out_grad[...] = second[:, D:].astype(f32)
    patch_grad[...] = patch_in[...]

    @pl.when(pl.program_id(0) == 0)
    def _():
        region_grad[...] = region_in[...]
        for at, v in ((0, in_gain), (1, in_shift), (4, out_bias), (5, mlp_gain), (6, mlp_shift), (7, down_bias)):
            v[...] = small[at : at + 1].reshape(D)
        qkv_bias[...] = small[2:4]
        up_bias[...] = jnp.concatenate([small[8 + b : 9 + b] for b in range(FF // D)], axis=1).reshape(FF)


def shards(
    wins, dps,
    patches, regional, window_image, in_gain, in_shift, w_qkv, qkv_bias, w_out, out_bias,
    mlp_gain, mlp_shift, w_up, up_bias, w_down, down_bias, patch_cot, region_cot,
):
    _, count, patch, _ = patches.shape
    group = window_image.shape[1]
    x = patches[0].transpose(1, 0, 2)
    cot = patch_cot[0].transpose(1, 0, 2)
    reg = regional[0]
    rcot = region_cot[0]
    const = lambda *arrays: [whole(a) for a in arrays]
    block = lambda a, n: (a, (n,) + a.shape[1:], lambda i: (i, 0, 0))
    block_out = lambda shape, n, dtype=bf16: ((shape, dtype), (n,) + shape[1:], lambda i: (i, 0, 0))
    triple, local_in, vecs, region_triple, gathered, probs_r, merged_r, region_mid, triple0, local_in0 = call(
        functools.partial(front_kernel, wins, dps), (pl.cdiv(patch, 7),),
        [block(x, 7)]
        + const(reg, window_image, in_gain, in_shift, w_qkv, qkv_bias, w_out, out_bias, mlp_gain, mlp_shift, up_bias, down_bias),
        [block_out((patch, count, 3 * D), 7), block_out((patch, count, D), 7), whole_out((16, D), f32), whole_out((count, 3 * D), bf16),
         whole_out((group, 3 * D), bf16), whole_out((2, group, 8 * count), bf16), whole_out((count, D), bf16),
         whole_out((count, D), f32), whole_out((count, 3 * D), bf16), whole_out((count, D), bf16)],
        [pltpu.VMEM((group, 3 * D), bf16), pltpu.VMEM((count, 3 * D), bf16), pltpu.VMEM((group, 128), f32),
         pltpu.SemaphoreType.DMA((8 * wins,))],
        name="front", collective_id=2,
    )
    steps = (count // WC,)
    mid = lambda a: (a, (a.shape[0], WC, a.shape[2]), lambda i: (0, i, 0))
    mid_out = lambda shape, dtype=bf16: ((shape, dtype), (shape[0], WC, shape[2]), lambda i: (0, i, 0))
    tail = lambda a: (a, (WC, a.shape[1]), lambda i: (i, 0))
    merged, probs = call(
        local_fwd_kernel, steps, [mid(triple), tail(triple0)],
        [mid_out((patch + 1, count, D)), ((((count, TP, HEADS * TP)), bf16), (WC, TP, HEADS * TP), lambda i: (i, 0, 0))],
        [pltpu.VMEM((12, TP * WC, 128), f32), pltpu.VMEM((4, TP * WC, 128), f32)], name="local_fwd",
    )
    n = 10
    rows_grid = ((patch + 1) // n,)
    patch_out, region_out, grad_middle, grad_merged, up_grad, down_grad_t, out_local, vec_mlp, up_bias_grad = call(
        mlp_kernel, rows_grid,
        [block(x, n), whole(region_mid), block(merged, n), block(cot, n)]
        + const(rcot, vecs, w_out, w_up, w_down),
        [block_out((patch, count, D), n), whole_out((count, D), bf16),
         block_out((patch + 1, count, D), n), block_out((patch + 1, count, D), n),
         whole_out((D, FF), bf16), whole_out((D, FF), bf16), whole_out((D, D), f32),
         whole_out((8, D), f32), whole_out((1, FF), f32)],
        [pltpu.VMEM((D, FF), f32), pltpu.VMEM((D, FF), f32)], name="mlp",
    )
    last_rows = rows_of(wins, dps)[1]
    grad_triple, up_part, down_part, terms, grad_query, low_first, low_second, sums, out_bias_part, grad_mid = call(
        functools.partial(back_kernel, wins, dps), steps,
        [mid(triple), tail(triple0), (probs, (WC, TP, HEADS * TP), lambda i: (i, 0, 0), group > 512), mid(grad_merged), mid(local_in), tail(local_in0)]
        + const(region_triple, gathered, probs_r, merged_r, region_mid)
        + [(grad_middle, (1, count, D), lambda i: (patch, 0, 0))]
        + const(vecs, w_qkv, w_out, out_local) + [left(a.reshape(stream_shape(wins, FF))) for a in (up_grad, down_grad_t)],
        [mid_out((patch + 1, count, 3 * D)), whole_out((last_rows, FF), bf16), whole_out((last_rows, FF), bf16),
         whole_out((group, 2 * D), bf16), whole_out((count, D), bf16), whole_out(stream_shape(wins, 2 * D), bf16),
         whole_out(stream_shape(wins, 2 * D), bf16),
         whole_out((1, 3 * D), f32), whole_out((1, D), f32), whole_out((count, D), f32)],
        [pltpu.VMEM((16, TP * WC, 128), f32), pltpu.VMEM((12, TP * WC, 128), f32), pltpu.VMEM((count, 3 * D), bf16),
         pltpu.VMEM((D, 3 * D), f32), pltpu.VMEM((count, D), bf16)]
        + stream_scratch(wins, dps, FF, "down") * 2,
        name="back", collective_id=0,
    )
    patch_grad, region_grad, small, up_sum, down_sum, first_sum, second_sum = call(
        functools.partial(tail_kernel, wins, dps), rows_grid,
        [block(x, n), block(grad_triple, n), block(grad_middle, n)]
        + const(region_mid, vecs, w_qkv, terms, grad_query, reg, grad_mid, vec_mlp, up_bias_grad, sums, out_bias_part, up_part, down_part)
        + [left(low_first), left(low_second)],
        [block_out((patch, count, D), n), whole_out((count, D), bf16), whole_out((16, D), f32)]
        + [left_out(stream_shape(wins, FF), bf16)] * 2 + [left_out(stream_shape(wins, 2 * D), bf16)] * 2,
        [pltpu.VMEM((8, D), f32),
         pltpu.VMEM((wins // 2, count, 2 * D), bf16), pltpu.SemaphoreType.DMA((wins,)), pltpu.VMEM((wins // 2, count, 2 * D), bf16),
         pltpu.VMEM((wins // 2, count, 2 * D), bf16), pltpu.SemaphoreType.DMA((wins,)),
         pltpu.VMEM((16, D), f32), pltpu.VMEM((wins - 1, 16, D), f32), pltpu.SemaphoreType.DMA((2 * wins,)),
         pltpu.VMEM((16, D), f32), pltpu.VMEM((max(dps - 1, 1), 16, D), f32), pltpu.SemaphoreType.DMA((2 * dps,))]
        + stream_scratch(wins, dps, 2 * D) * 2 + stream_scratch(wins, dps, FF, "back") * 2,
        name="tail", collective_id=1,
    )
    up_sum, down_sum = up_sum.reshape(D, FF), down_sum.reshape(D, FF)
    first_sum, second_sum = first_sum.reshape(D, 2 * D), second_sum.reshape(D, 2 * D)
    n = 2
    down = lambda i: (i, 0)
    vector = lambda size: ((((size,), f32)), (size,), lambda i: (0,))
    token = -(-patch // n)
    tokens = lambda i: (lax.min(i, (patch - 1) // token), 0, 0)
    (
        patch_grad, region_grad, in_gain_grad, in_shift_grad, qkv_grad, qkv_bias_grad, out_grad, out_bias_grad,
        mlp_gain_grad, mlp_shift_grad, up_grad, up_bias_grad, down_grad, down_bias_grad,
    ) = call(
        last_kernel, (n,),
        [(up_sum, (D // n, FF), down), (down_sum, (D, FF // n), lambda i: (0, i))]
        + [(a, (D // n, 2 * D), down) for a in (first_sum, second_sum)]
        + [whole(small), (patch_grad, (token, count, D), tokens), whole(region_grad)],
        [(((patch, count, D), bf16), (token, count, D), tokens), whole_out((count, D), bf16), vector(D), vector(D),
         (((D, 3 * D), f32), (D // n, 3 * D), down), whole_out((2, D), f32), (((D, D), f32), (D // n, D), down), vector(D),
         vector(D), vector(D), (((D, FF), f32), (D // n, FF), down), vector(FF), (((FF, D), f32), (FF // n, D), down), vector(D)],
        name="last",
    )
    return (
        patch_out.transpose(1, 0, 2)[None], region_out[None], patch_grad.transpose(1, 0, 2)[None], region_grad[None],
        in_gain_grad, in_shift_grad, qkv_grad, qkv_bias_grad, out_grad, out_bias_grad,
        mlp_gain_grad, mlp_shift_grad, up_grad, up_bias_grad, down_grad, down_bias_grad,
    )


def solution(mesh):
    wide = P("dp", "win", None, None)
    narrow = P("dp", "win", None)
    in_specs = (wide, narrow, P("dp", None)) + (P(),) * 12 + (wide, narrow)
    out_specs = (wide, narrow, wide, narrow) + (P(),) * 12
    return jax.shard_map(functools.partial(shards, mesh.shape["win"], mesh.shape["dp"]), mesh=mesh, in_specs=in_specs, out_specs=out_specs, check_vma=False)
```

```python
import functools

import jax
import jax.numpy as jnp
from jax import lax
from jax.experimental import pallas as pl
from jax.experimental.pallas import tpu as pltpu
from jax.sharding import PartitionSpec as P

D = 512
HEADS = 16
HD = 32
FF = 2048
EPSILON = 1e-06
MASKED_SCORE = -1e30
SCALING = HD ** (-0.5)
LOG2E = 1.4426950408889634
TP = 64
FB = 2048
WC = 16
f32 = jnp.float32
bf16 = jnp.bfloat16
VMEM_LIMIT = 60 * 2**20
MESH = pl.DeviceIdType.MESH
FRONT_SLOTS = (5, 6)
BACK_SLOTS = (
    (0, 0, (0,), (0,)), (0, 6, (1,), ()), (0, 16, (), (1,)), (1, 7, (2,), ()), (1, 16, (3,), (2,)), (2, 7, (), (3,)),
)


def nn(a, b):
    return lax.dot_general(a, b, (((1,), (0,)), ((), ())), preferred_element_type=f32)


def nt(a, b):
    return lax.dot_general(a, b, (((1,), (1,)), ((), ())), preferred_element_type=f32)


def tn(a, b):
    return lax.dot_general(a, b, (((0,), (0,)), ((), ())), preferred_element_type=f32)


def call(body, grid, ins, outs, scratch=(), name=None, collective_id=None, limit=VMEM_LIMIT):
    def spec(block, index, *single):
        if block is None:
            return pl.BlockSpec(memory_space=pl.ANY)
        if index is None:
            return pl.BlockSpec(block, lambda *_: (0,) * len(block), pipeline_mode=pl.Buffered(1))
        return pl.BlockSpec(block, index, pipeline_mode=pl.Buffered(1) if any(single) else None)

    return pl.pallas_call(
        body,
        grid=grid,
        in_specs=[spec(*entry[1:]) for entry in ins],
        out_specs=[spec(b, i) for _, b, i in outs],
        out_shape=[jax.ShapeDtypeStruct(s, d) for (s, d), _, _ in outs],
        scratch_shapes=list(scratch),
        compiler_params=pltpu.CompilerParams(
            vmem_limit_bytes=limit, collective_id=collective_id, has_side_effects=collective_id is not None
        ),
        name=name,
    )(*[entry[0] for entry in ins])


def whole(a):
    return (a, a.shape, None)


def whole_out(shape, dtype):
    return ((shape, dtype), shape, None)


def left(a):
    return (a, None, None)


def left_out(shape, dtype):
    return ((shape, dtype), None, None)


def norm_stats(rows):
    average = jnp.mean(rows, axis=-1, keepdims=True)
    centred = rows - average
    spread = jnp.mean(centred * centred, axis=-1, keepdims=True)
    inverse = lax.rsqrt(spread + EPSILON)
    return centred * inverse, inverse


def norm_back(vhat, inverse, gain, grad_out):
    scaled = grad_out * gain
    first = jnp.mean(scaled, axis=-1, keepdims=True)
    second = jnp.mean(scaled * vhat, axis=-1, keepdims=True)
    return inverse * (scaled - first - vhat * second)


def col(x):
    return jnp.sum(x, axis=0, keepdims=True)


class Place:
    def __init__(self, wins, dps):
        self.wins, self.dps = wins, dps
        self.win = lax.axis_index("win")
        self.dp = lax.axis_index("dp")
        self.core = lax.rem(self.win, 2)
        self.chip = self.win // 2
        self.chips = wins // 2
        self.square = self.chips == 4
        self.a = self.chip // 2
        self.b = lax.rem(self.chip, 2)

    def other_core(self):
        return {"win": self.chip * 2 + 1 - self.core}

    def other_a(self):
        return {"win": ((1 - self.a) * 2 + self.b) * 2 + self.core}

    def other_b(self):
        return {"win": (self.a * 2 + 1 - self.b) * 2 + self.core}

    def at_chip(self, j):
        chip = lax.rem(self.chip + j, self.chips)
        return chip, {"win": chip * 2 + self.core}

    def at_dp(self, j):
        dp = lax.rem(self.dp + j, self.dps)
        return dp, {"dp": dp}

    def near(self, all_wins, around=False):
        if all_wins:
            return [{"win": lax.rem(self.win + j, self.wins)} for j in range(1, self.wins)]
        if self.square and not around:
            return [self.other_core(), self.other_a(), self.other_b()]
        return [self.other_core()] + [self.at_chip(j)[1] for j in range(1, self.chips)]

    def partners(self, all_wins, along, around):
        return self.near(all_wins, around) + [self.at_dp(j)[1] for j in range(1, self.dps if along else 1)]

    def greet(self, all_wins=False, along=True, around=False):
        barrier = pltpu.get_barrier_semaphore()
        for to in self.partners(all_wins, along, around):
            pl.semaphore_signal(barrier, inc=1, device_id=to, device_id_type=MESH)

    def greeted(self, all_wins=False, along=True, around=False):
        pl.semaphore_wait(pltpu.get_barrier_semaphore(), len(self.partners(all_wins, along, around)))


def rows_of(wins, dps):
    piece = D // wins
    return piece, piece // dps if piece % (16 * dps) == 0 else piece


def stream_shape(wins, columns):
    return (2, wins // 2, D // wins, columns)


def stream_scratch(wins, dps, columns, kind="whole"):
    piece, last = rows_of(wins, dps)
    chips = wins // 2
    landing = (4, 2, piece, columns // 2) if chips == 4 else (max(chips - 1, 1), piece, columns)
    half, part, some = pltpu.VMEM((chips, piece, columns), bf16), pltpu.VMEM((piece, columns), bf16), pltpu.VMEM((16, 128), bf16)
    down = kind != "back"
    return [
        half if down else some,
        half,
        pltpu.VMEM(landing, bf16) if down else some,
        part if down else some,
        pltpu.VMEM((max(dps - 1, 1), last, columns), bf16) if down else some,
        some if kind == "down" else part,
        pltpu.SemaphoreType.DMA((20 + 4 * chips + 4 * dps,)),
    ]


def columns_of(refs):
    return refs[1].shape[2]


class Stream:
    PARTS = 7

    def __init__(self, place, source, final, refs):
        self.p = place
        self.source, self.final = source, final
        self.own, self.r1, self.r2, self.s, self.r3, self.s2, self.sem = refs
        self.piece, self.last = rows_of(place.wins, place.dps)
        self.split = self.last != self.piece
        columns = columns_of(refs)
        self.left, self.right = pl.ds(0, columns // 2), pl.ds(columns // 2, columns // 2)

    def rows(self, start, size):
        return pl.ds(pl.multiple_of(start, 16), size)

    def remote(self, src, dst, to, k):
        return pltpu.make_async_remote_copy(
            src_ref=src, dst_ref=dst, send_sem=self.sem.at[2 * k], recv_sem=self.sem.at[2 * k + 1],
            device_id=to, device_id_type=MESH,
        )

    def _own(self):
        return pltpu.make_async_copy(self.source.at[self.p.core], self.own, self.sem.at[0])

    def _put(self):
        return pltpu.make_async_copy(self.r1, self.final.at[self.p.core], self.sem.at[1])

    def _cores(self):
        return [self.remote(self.source.at[1 - self.p.core], self.r1, self.p.other_core(), 1)]

    def _cores_back(self):
        return [self.remote(self.r1, self.final.at[self.p.core], self.p.other_core(), 2)]

    def _chips_left(self, k):
        p = self.p
        if k == 0:
            return [self.remote(self.own.at[c * 2 + 1 - p.b, :, self.left], self.r2.at[0, c], p.other_b(), 3 + c) for c in range(2)]
        return [self.remote(self.own.at[(1 - p.a) * 2 + p.b, :, self.left], self.r2.at[2, 0], p.other_a(), 5)]

    def _chips_right(self, k):
        p = self.p
        if k == 0:
            return [self.remote(self.own.at[(1 - p.a) * 2 + c, :, self.right], self.r2.at[1, c], p.other_a(), 6 + c) for c in range(2)]
        return [self.remote(self.own.at[p.a * 2 + 1 - p.b, :, self.right], self.r2.at[3, 0], p.other_b(), 8)]

    def _back_left(self, k):
        p = self.p
        mine = self.r1
        if k == 0:
            return [self.remote(self.s2.at[:, self.left], mine.at[p.chip, :, self.left], p.other_a(), 9)]
        rows = [mine.at[c * 2 + p.b, :, self.left] for c in range(2)]
        return [self.remote(rows[c], rows[c], p.other_b(), 10 + c) for c in range(2)]

    def _back_right(self, k):
        p = self.p
        mine = self.r1
        if k == 0:
            return [self.remote(self.s2.at[:, self.right], mine.at[p.chip, :, self.right], p.other_b(), 12)]
        rows = [mine.at[p.a * 2 + c, :, self.right] for c in range(2)]
        return [self.remote(rows[c], rows[c], p.other_a(), 13 + c) for c in range(2)]

    def _chips(self):
        out = []
        for j in range(1, self.p.chips):
            chip, to = self.p.at_chip(j)
            out.append(self.remote(self.own.at[chip], self.r2.at[j - 1], to, 2 + j))
        return out

    def _chips_back(self):
        out = []
        for j in range(1, self.p.chips):
            mine = self.r1.at[self.p.chip]
            out.append(self.remote(self.s2, mine, self.p.at_chip(j)[1], 2 + self.p.chips + j))
        return out

    def _dps(self):
        out = []
        for j in range(1, self.p.dps):
            dp, to = self.p.at_dp(j)
            src = self.s.at[self.rows(dp * self.last, self.last)] if self.split else self.s
            out.append(self.remote(src, self.r3.at[j - 1], to, 8 + 2 * self.p.chips + j))
        return out

    def _dps_back(self):
        out = []
        if self.split:
            for j in range(1, self.p.dps):
                mine = self.s2.at[self.rows(self.p.dp * self.last, self.last)]
                out.append(self.remote(mine, mine, self.p.at_dp(j)[1], 8 + 2 * self.p.chips + self.p.dps + j))
        return out

    def start(self, copies):
        for c in copies:
            c.start()

    def wait(self, copies):
        for c in copies:
            c.wait()

    def load(self):
        self._own().start()

    def send_cores(self):
        self.start(self._cores())

    def send_chips(self):
        self._own().wait()
        self.wait(self._cores())

        def add(i, carry):
            self.own[i] = (self.own[i].astype(f32) + self.r1[i].astype(f32)).astype(bf16)
            return carry

        lax.fori_loop(0, self.p.chips, add, 0)
        if self.p.square:
            self.start(self._chips_left(0))
            self.start(self._chips_right(0))
        else:
            self.start(self._chips())

    def add_square(self, chip, lanes, slot, c):
        self.own[chip, :, lanes] = (self.own[chip, :, lanes].astype(f32) + self.r2[slot, c].astype(f32)).astype(bf16)

    def send_chips_again(self):
        p = self.p
        if p.square:
            self.wait(self._chips_left(0))
            for c in range(2):
                self.add_square(c * 2 + p.b, self.left, 0, c)
            self.start(self._chips_left(1))
            self.wait(self._chips_right(0))
            for c in range(2):
                self.add_square(p.a * 2 + c, self.right, 1, c)
            self.start(self._chips_right(1))

    def send_dps(self):
        p = self.p
        if p.square:
            for lanes, slot, copies in ((self.left, 2, self._chips_left(1)), (self.right, 3, self._chips_right(1))):
                self.wait(copies)
                self.s[:, lanes] = (self.own[p.chip, :, lanes].astype(f32) + self.r2[slot, 0].astype(f32)).astype(bf16)
        else:
            self.wait(self._chips())
            total = self.own[p.chip].astype(f32)
            for j in range(p.chips - 1):
                total += self.r2[j].astype(f32)
            self.s[...] = total.astype(bf16)
        self.start(self._dps())

    def sum_dps(self, out, at):
        self.wait(self._dps())
        mine = self.part()
        total = self.s[mine].astype(f32)
        for j in range(self.p.dps - 1):
            total += self.r3[j].astype(f32)
        out[at] = total.astype(bf16)

    def part(self):
        return self.rows(self.p.dp * self.last if self.split else 0, self.last)

    def send_dps_back(self):
        self.sum_dps(self.s2, self.part())
        self.start(self._dps_back())

    def end_dps_back(self):
        self.wait(self._dps_back())

    def begin_back(self, part):
        self.s2[self.part()] = part[...]
        self.start(self._dps_back())

    def send_chips_back(self):
        self.end_dps_back()
        self.start_chips_back()

    def start_chips_back(self):
        self.r1[self.p.chip] = self.s2[...]
        if self.p.square:
            self.start(self._back_left(0))
            self.start(self._back_right(0))
        else:
            self.start(self._chips_back())

    def send_chips_back_again(self):
        if self.p.square:
            self.wait(self._back_left(0))
            self.start(self._back_left(1))
            self.wait(self._back_right(0))
            self.start(self._back_right(1))
        else:
            self.wait(self._chips_back())

    def send_cores_back(self):
        if self.p.square:
            self.wait(self._back_left(1))
            self.wait(self._back_right(1))
        self.start(self._cores_back())
        self._put().start()

    def finish(self):
        self.wait(self._cores_back())
        self._put().wait()

    STEPS = (
        "send_cores", "send_chips", "send_chips_again", "send_dps", "send_dps_back",
        "send_chips_back", "send_chips_back_again", "send_cores_back", "finish",
    )

    def step(self, k):
        if 0 <= k < len(self.STEPS):
            getattr(self, self.STEPS[k])()


def expand_group(x, heads):
    lane = lax.broadcasted_iota(jnp.int32, (1, x.shape[1]), 1) // HD
    return jnp.concatenate([jnp.where(lane == i, x, jnp.zeros_like(x)) for i in range(heads)], axis=0)


def fold_group(y, heads):
    rows = y.shape[0] // heads
    lane = lax.broadcasted_iota(jnp.int32, (1, y.shape[1]), 1) // HD
    total = y[(heads - 1) * rows :]
    for i in range(heads - 2, -1, -1):
        total = jnp.where(lane == i, y[i * rows : (i + 1) * rows], total)
    return total


GAIN1, SHIFT1, GAIN2, SHIFT2, OUT_BIAS, DOWN_BIAS, QUERY_BIAS, KEY_BIAS, VALUE_BIAS, UP_BIAS = range(10)


def row(vecs, at):
    return vecs[at : at + 1]


def normed_low(vhat, vecs, gain, shift):
    return (vhat * row(vecs, gain) + row(vecs, shift)).astype(bf16)


def front_kernel(
    wins, dps,
    patches, regional, images, in_gain, in_shift, w_qkv, qkv_bias, w_out, out_bias, mlp_gain, mlp_shift, up_bias, down_bias,
    triple, local_in, vecs, region_triple, gathered_out, probs, merged, region_mid, triple0, local_in0,
    gathered, packed, image_col, sem,
):
    step = pl.program_id(0)
    place = Place(wins, dps)
    count = regional.shape[0]
    group = gathered.shape[0]
    mine = pl.ds(pl.multiple_of(place.win * count, 16), count)

    def project(normed):
        out = nn(normed, w_qkv[...])
        return jnp.concatenate(
            [out[:, :D] + row(vecs, QUERY_BIAS), out[:, D : 2 * D], out[:, 2 * D :] + row(vecs, VALUE_BIAS)], axis=1
        ).astype(bf16)

    parts = (pl.ds(0, 2 * D), pl.ds(2 * D, D))

    def remote(src, dst, to, k):
        return pltpu.make_async_remote_copy(
            src_ref=src, dst_ref=dst, send_sem=sem.at[2 * k], recv_sem=sem.at[2 * k + 1], device_id=to, device_id_type=MESH
        )

    def direct(part):
        lanes, first = parts[part], 2 * place.chips * part
        targets = [place.other_core()] + [place.at_chip(j)[1] for j in range(1, place.chips)]
        return [remote(packed.at[:, lanes], gathered.at[mine, lanes], to, first + j) for j, to in enumerate(targets)]

    def onward(part):
        lanes, first = parts[part], 2 * place.chips * part + place.chips
        copies = []
        for j in range(1, place.chips):
            chip = lax.rem(place.chip - j + place.chips, place.chips)
            theirs = gathered.at[pl.ds(pl.multiple_of((chip * 2 + place.core) * count, 16), count), lanes]
            copies.append(remote(theirs, theirs, place.other_core(), first + j))
        return copies

    def pass_on(part):
        for c in direct(part):
            c.wait()
        for c in onward(part):
            c.start()

    @pl.when(step == 0)
    def _():
        place.greet(around=True, along=False)
        for at, v in (
            (GAIN1, in_gain), (SHIFT1, in_shift), (GAIN2, mlp_gain), (SHIFT2, mlp_shift), (OUT_BIAS, out_bias), (DOWN_BIAS, down_bias),
        ):
            vecs[at : at + 1] = v[...].astype(f32).reshape(1, D)
        vecs[QUERY_BIAS : QUERY_BIAS + 1] = qkv_bias[0:1].astype(f32)
        vecs[KEY_BIAS : KEY_BIAS + 1] = jnp.zeros((1, D), f32)
        vecs[VALUE_BIAS : VALUE_BIAS + 1] = qkv_bias[1:2].astype(f32)
        up = up_bias[...].astype(f32).reshape(1, FF)
        for b in range(FF // D):
            vecs[UP_BIAS + b : UP_BIAS + b + 1] = up[:, D * b : D * (b + 1)]
        vecs[UP_BIAS + FF // D : 16] = jnp.zeros((16 - UP_BIAS - FF // D, D), f32)
        vhat, _ = norm_stats(regional[...].astype(f32))
        normed = normed_low(vhat, vecs, GAIN1, SHIFT1)
        own = project(normed)
        region_triple[...] = own
        packed[:, : 2 * D] = own[:, D:]
        packed[:, 2 * D :] = normed
        gathered[mine] = packed[...]
        place.greeted(around=True, along=False)
        for part in range(2):
            for c in direct(part):
                c.start()
        ids = images[...].astype(f32)
        image_col[...] = jnp.broadcast_to(ids, (128, group)).T

    rows = patches.shape[0] * count
    vhat, _ = norm_stats(patches[...].reshape(rows, D).astype(f32))
    normed_rows = normed_low(vhat, vecs, GAIN1, SHIFT1)
    local_in[...] = normed_rows.reshape(local_in.shape)
    triple[...] = project(normed_rows).reshape(triple.shape)

    for part, when in enumerate(FRONT_SLOTS):
        pl.when(step == when)(functools.partial(pass_on, part))

    @pl.when(step == pl.num_programs(0) - 1)
    def _():
        for c in onward(0):
            c.wait()
        own_ids = image_col[mine]
        own_row = jnp.concatenate([own_ids] * 8, axis=0).T[0:1]
        same = image_col[:, 0:1] == own_row
        for g in range(2):
            lanes = slice(256 * g, 256 * g + 256)
            scores = nt(gathered[:, lanes], expand_group(region_triple[:, lanes], 8))
            scores = jnp.where(same, scores * SCALING, MASKED_SCORE)
            top = jnp.max(scores, axis=0, keepdims=True)
            exps = jnp.exp2((scores - top) * LOG2E)
            low = (exps * (1.0 / col(exps))).astype(bf16)
            probs[g] = low
            merged[:, lanes] = fold_group(tn(low, gathered[:, D + 256 * g : D + 256 * g + 256]), 8).astype(bf16)
        mid = regional[...].astype(f32) + nn(merged[...], w_out[...]) + row(vecs, OUT_BIAS)
        region_mid[...] = mid
        vhat_mid, _ = norm_stats(mid)
        normed_mid = normed_low(vhat_mid, vecs, GAIN1, SHIFT1)
        local_in0[...] = normed_mid
        triple0[...] = project(normed_mid)
        for c in onward(1):
            c.wait()
        gathered_out[...] = gathered[...]


def expand(x):
    lane = lax.broadcasted_iota(jnp.int32, (1, 128), 1) // HD
    return jnp.concatenate([jnp.where(lane == i, x, jnp.zeros_like(x)) for i in range(4)], axis=0)


def query_side(rows, weights):
    return fold_group(tn(weights, rows), 4)


def load_triple(t, triple, triple0, patch):
    for b in range(12):
        lanes = slice(128 * b, 128 * b + 128)
        t[b, 0 : patch * WC] = triple[:, :, lanes].reshape(patch * WC, 128).astype(f32)
        t[b, patch * WC : (patch + 1) * WC] = triple0[:, lanes].astype(f32)
        t[b, (patch + 1) * WC :] = jnp.zeros(((TP - patch - 1) * WC, 128), f32)


def local_fwd_kernel(triple, triple0, merged, probs, t, m):
    patch = triple.shape[0]
    load_triple(t, triple, triple0, patch)
    row = lax.broadcasted_iota(jnp.int32, (TP, 1), 0)

    def one(w):
        for b in range(4):
            q = t[b, pl.ds(w, TP, stride=WC), :].astype(bf16)
            k = t[4 + b, pl.ds(w, TP, stride=WC), :].astype(bf16)
            v = t[8 + b, pl.ds(w, TP, stride=WC), :].astype(bf16)
            scores = nt(k, expand(q))
            scores = jnp.where(row <= patch, scores, MASKED_SCORE)
            top = jnp.max(scores, axis=0, keepdims=True)
            exps = jnp.exp2((scores - top) * (SCALING * LOG2E))
            low = (exps * (1.0 / col(exps))).astype(bf16)
            probs[w, :, 256 * b : 256 * b + 256] = low
            m[b, pl.ds(w, TP, stride=WC), :] = query_side(v, low)

    for w in range(WC):
        one(w)
    for b in range(4):
        merged[:, :, 128 * b : 128 * b + 128] = m[b, 0 : (patch + 1) * WC].astype(bf16).reshape(patch + 1, WC, 128)


def local_bwd_step(w, probs, t, d):
    at = pl.ds(w, TP, stride=WC)
    for b in range(4):
        q = t[b, at, :].astype(bf16)
        k = t[4 + b, at, :].astype(bf16)
        v = t[8 + b, at, :].astype(bf16)
        g = t[12 + b, at, :].astype(bf16)
        qx = expand(q)
        gx = expand(g)
        low = probs[w, :, 256 * b : 256 * b + 256]
        high = low.astype(f32)
        scaled = high * nt(v, gx)
        back = (scaled - high * col(scaled)).astype(bf16)
        d[4 + b, at, :] = nn(back, qx) * SCALING
        d[8 + b, at, :] = nn(low, gx)
        d[b, at, :] = query_side(k, back) * SCALING


def back_kernel(
    wins, dps,
    triple, triple0, probs, grad_merged, local_in, local_in0,
    region_triple, gathered, probs_r, merged_r, region_mid, grad_middle0, vecs, w_qkv, w_out, out_local,
    up_source, down_source,
    grad_triple, up_part, down_part, terms, grad_query, low_first, low_second, sums, out_bias_part, grad_mid,
    t, d, d0, qkv_acc, grad_merged_s, *streams,
):
    step = pl.program_id(0)
    place = Place(wins, dps)
    up = Stream(place, up_source, None, streams[: Stream.PARTS])
    down = Stream(place, down_source, None, streams[Stream.PARTS :])

    @pl.when(step == 0)
    def _():
        place.greet()
        up.load()
        down.load()
        qkv_acc[...] = jnp.zeros_like(qkv_acc)
        sums[...] = jnp.zeros_like(sums)

    patch = triple.shape[0]
    load_triple(t, triple, triple0, patch)
    rows = (patch + 1) * WC
    for b in range(4):
        t[12 + b, 0:rows] = grad_merged[:, :, 128 * b : 128 * b + 128].reshape(rows, 128).astype(f32)
        t[12 + b, rows:] = jnp.zeros((TP * WC - rows, 128), f32)

    def end():
        for s, part in ((up, up_part), (down, down_part)):
            s.sum_dps(part, slice(None))

    def reached(w):
        if w == 0:
            pl.when(step == 0)(place.greeted)
        for when, after, ups, downs in BACK_SLOTS:
            if after == w:

                @pl.when(step == when)
                def _(ups=ups, downs=downs):
                    for k in ups:
                        up.step(k)
                    for k in downs:
                        down.step(k)

    for w in range(WC):
        local_bwd_step(w, probs, t, d)
        reached(w)
    at = pl.ds(pl.multiple_of(step * WC, WC), WC)
    for b in range(12):
        lanes = slice(128 * b, 128 * b + 128)
        low = d[b, 0:rows].astype(bf16)
        grad_triple[:, :, lanes] = low.reshape(patch + 1, WC, 128)
        d0[at, lanes] = low[rows - WC :]
        sums[:, lanes] += col(low.astype(f32))
    normed = jnp.concatenate([local_in[...].reshape(patch * WC, D), local_in0[...]], axis=0).T
    for b in range(3):
        lanes = slice(D * b, D * (b + 1))
        qkv_acc[:, lanes] += nn(normed, grad_triple[:, :, lanes].reshape(rows, D))

    reached(WC)

    @pl.when(step == pl.num_programs(0) - 1)
    def _():
        vhat, inverse = norm_stats(region_mid[...])
        mid = grad_middle0[0].astype(f32) + norm_back(vhat, inverse, row(vecs, GAIN1), nt(d0[...], w_qkv[...]))
        grad_mid[...] = mid
        grad_attn = mid.astype(bf16)
        out_low = (out_local[...] + tn(merged_r[...], grad_attn)).astype(bf16)
        out_bias_part[...] = col(grad_attn.astype(f32))
        grad_merged_r = nt(grad_attn, w_out[...]).astype(bf16)
        grad_merged_s[...] = grad_merged_r

        keys = gathered.shape[0]
        width = 8 * region_triple.shape[0]
        blocks = max(keys // width, 1) if keys % width == 0 else 1
        size = keys // blocks

        def group_half(g, carry):
            lanes = pl.ds(pl.multiple_of(256 * g, 256), 256)
            value_lanes = pl.ds(pl.multiple_of(D + 256 * g, 256), 256)
            qx = expand_group(region_triple[:, lanes], 8)
            gx = expand_group(grad_merged_s[:, lanes], 8)

            def scaled_at(at):
                high = probs_r[g, at].astype(f32)
                return high, high * nt(gathered[at, value_lanes], gx)

            def finish(at, row_terms, scaled=None):
                high, scaled = scaled_at(at) if scaled is None else scaled
                back = (scaled - high * row_terms).astype(bf16)
                terms[at, lanes] = (nn(back, qx) * SCALING).astype(bf16)
                terms[at, value_lanes] = nn(probs_r[g, at], gx).astype(bf16)
                return tn(back, gathered[at, lanes])

            if blocks == 1:
                both = scaled_at(pl.ds(0, keys))
                total = finish(pl.ds(0, keys), col(both[1]), both)
            else:
                at = lambda i: pl.ds(pl.multiple_of(i * size, 16), size)
                row_terms = lax.fori_loop(
                    0, blocks, lambda i, r: r + col(scaled_at(at(i))[1]), jnp.zeros((1, width), f32)
                )
                total = lax.fori_loop(
                    0, blocks, lambda i, q: q + finish(at(i), row_terms), jnp.zeros((width, 256), f32)
                )
            grad_query[:, lanes] = (fold_group(total, 8) * SCALING).astype(bf16)
            return carry

        if blocks == 1:
            group_half(0, 0)
            group_half(1, 0)
        else:
            lax.fori_loop(0, 2, group_half, 0)
        sums[:, :D] += col(grad_query[...].astype(f32))
        sums[:, D:] += col(terms[...].astype(f32))
        region_in_all = gathered[:, 2 * D :]
        own_in = gathered[pl.ds(pl.multiple_of(place.win * region_triple.shape[0], 16), region_triple.shape[0]), 2 * D :]
        shape = low_first.shape[:3] + (D,)
        low_first[:, :, :, :D] = (qkv_acc[:, :D] + tn(own_in, grad_query[...])).astype(bf16).reshape(shape)
        low_first[:, :, :, D:] = (qkv_acc[:, D : 2 * D] + tn(region_in_all, terms[:, :D])).astype(bf16).reshape(shape)
        low_second[:, :, :, :D] = (qkv_acc[:, 2 * D :] + tn(region_in_all, terms[:, D:])).astype(bf16).reshape(shape)
        low_second[:, :, :, D:] = out_low.reshape(shape)
        end()


def gelu_both(v):
    e = jnp.exp2(v * v * (-0.5 * LOG2E))
    cdf = 0.5 + 0.5 * lax.erf(v * (0.5**0.5))
    return v * cdf, cdf + v * e * 0.3989422804014327


def with_region(block, region, last):
    tokens, count, width = block.shape
    head = block[0 : tokens - 1].reshape((tokens - 1) * count, width)
    tail = jnp.where(last, region, block[tokens - 1])
    return jnp.concatenate([head, tail], axis=0)


def mlp_kernel(
    patches, region_mid, merged, patch_cot, region_cot, vecs, w_out, w_up, w_down,
    patch_out, region_out, grad_middle, grad_merged, up_grad, down_grad_t, out_grad, vec512, up_bias_grad,
    up_acc, down_acc,
):
    step = pl.program_id(0)
    last = step == pl.num_programs(0) - 1
    tokens, count, _ = patches.shape
    rows = tokens * count

    @pl.when(step == 0)
    def _():
        up_acc[...] = jnp.zeros_like(up_acc)
        down_acc[...] = jnp.zeros_like(down_acc)
        out_grad[...] = jnp.zeros_like(out_grad)
        vec512[...] = jnp.zeros_like(vec512)
        up_bias_grad[...] = jnp.zeros_like(up_bias_grad)

    x = with_region(patches[...].astype(f32), region_mid[...], last)
    grad_result = with_region(patch_cot[...], region_cot[...], last)
    low_merged = merged[...].reshape(rows, D)
    middle = x + nn(low_merged, w_out[...]) + row(vecs, OUT_BIAS)
    vhat, inverse = norm_stats(middle)
    mlp_in = normed_low(vhat, vecs, GAIN2, SHIFT2)
    mlp_in_t = mlp_in.T
    grad_result_t = grad_result.T
    result = middle + row(vecs, DOWN_BIAS)
    grad_in = jnp.zeros((rows, D), f32)
    up_row = jnp.concatenate([row(vecs, UP_BIAS + b) for b in range(FF // D)], axis=1)
    for f in range(FF // FB):
        at = slice(FB * f, FB * f + FB)
        hidden = nn(mlp_in, w_up[:, at]) + up_row[:, at]
        grad_active = nt(grad_result, w_down[at, :])
        active, slope = gelu_both(hidden)
        active = active.astype(bf16)
        grad_hidden = (grad_active * slope).astype(bf16)
        result += nn(active, w_down[at, :])
        grad_in += nt(grad_hidden, w_up[:, at])
        up_acc[:, at] += nn(mlp_in_t, grad_hidden)
        down_acc[:, at] += nn(grad_result_t, active)
        up_bias_grad[:, at] += col(grad_hidden.astype(f32))
    shown = result.astype(bf16)
    patch_out[...] = shown.reshape(tokens, count, D)
    region_out[...] = shown[rows - count :]
    gm = grad_result.astype(f32) + norm_back(vhat, inverse, row(vecs, GAIN2), grad_in)
    low_gm = gm.astype(bf16)
    grad_middle[...] = low_gm.reshape(tokens, count, D)
    out_grad[...] += nn(low_merged.T, low_gm)
    grad_merged[...] = nt(low_gm, w_out[...]).astype(bf16).reshape(tokens, count, D)
    vec512[0:1] += col(grad_in * vhat)
    vec512[1:2] += col(grad_in)
    vec512[2:3] += col(low_gm.astype(f32))
    vec512[3:4] += col(grad_result.astype(f32))

    @pl.when(last)
    def _():
        up_grad[...] = up_acc[...].astype(bf16)
        down_grad_t[...] = down_acc[...].astype(bf16)


def tail_kernel(
    wins, dps,
    patches, grad_triple, grad_middle, region_mid, vecs, w_qkv, terms, grad_query,
    regional, grad_mid, vec_mlp, up_bias_grad, sums, out_bias_part, up_part, down_part, first_source, second_source,
    patch_grad, region_grad, small_sum, up_sum, down_sum, first_sum, second_sum,
    vec, halves, half_sem, summed, pieces, piece_sem, pack, near, near_sem, total, far, far_sem, *streams,
):
    step = pl.program_id(0)
    tokens, count, _ = patches.shape
    rows = tokens * count
    place = Place(wins, dps)
    parts = [streams[Stream.PARTS * b : Stream.PARTS * (b + 1)] for b in range(4)]
    late = (Stream(place, first_source, first_sum, parts[0]), Stream(place, second_source, second_sum, parts[1]))
    early = (Stream(place, None, up_sum, parts[2]), Stream(place, None, down_sum, parts[3]))

    def window_rows(chip, core):
        return pl.ds(pl.multiple_of((chip * 2 + core) * count, 16), count)

    def to_core():
        return [pltpu.make_async_remote_copy(
            src_ref=terms.at[window_rows(chip, 1 - place.core)], dst_ref=halves.at[chip],
            send_sem=half_sem.at[2 * chip], recv_sem=half_sem.at[2 * chip + 1],
            device_id=place.other_core(), device_id_type=MESH,
        ) for chip in range(place.chips)]

    def to_owners():
        copies = []
        for j in range(1, place.chips):
            chip, to = place.at_chip(j)
            copies.append(pltpu.make_async_remote_copy(
                src_ref=summed.at[chip], dst_ref=pieces.at[j - 1],
                send_sem=piece_sem.at[2 * j - 2], recv_sem=piece_sem.at[2 * j - 1], device_id=to, device_id_type=MESH,
            ))
        return copies

    def to_near():
        return [pltpu.make_async_remote_copy(
            src_ref=pack, dst_ref=near.at[j - 1], send_sem=near_sem.at[2 * j - 2], recv_sem=near_sem.at[2 * j - 1],
            device_id={"win": lax.rem(place.win + j, wins)}, device_id_type=MESH,
        ) for j in range(1, wins)]

    def to_far():
        return [pltpu.make_async_remote_copy(
            src_ref=total, dst_ref=far.at[j - 1], send_sem=far_sem.at[2 * j - 2], recv_sem=far_sem.at[2 * j - 1],
            device_id=place.at_dp(j)[1], device_id_type=MESH,
        ) for j in range(1, dps)]

    def late_step(k):
        for s in late:
            s.step(k)

    def early_step(k):
        for s in early:
            s.step(k)

    def begin():
        place.greeted(all_wins=True)
        late_step(0)
        for c in to_core():
            c.start()
        for s, part in zip(early, (up_part, down_part)):
            s.begin_back(part)

    def owners_begin():
        for c in to_core():
            c.wait()

        def add(chip, carry):
            own = terms[window_rows(chip, place.core)].astype(f32)
            summed[chip] = (own + halves[chip].astype(f32)).astype(bf16)
            return carry

        lax.fori_loop(0, place.chips, add, 0)
        for c in to_owners():
            c.start()

    def region_end():
        for c in to_owners():
            c.wait()
        key_value = summed[place.chip].astype(f32)
        for j in range(place.chips - 1):
            key_value += pieces[j].astype(f32)
        vhat, inverse = norm_stats(regional[...].astype(f32))
        grad_in = nt(grad_query[...], w_qkv[:, :D]) + nt(key_value.astype(bf16), w_qkv[:, D:])
        region_grad[...] = (grad_mid[...] + norm_back(vhat, inverse, row(vecs, GAIN1), grad_in)).astype(bf16)
        vec[0:1] += col(grad_in * vhat)
        vec[1:2] += col(grad_in)

    def small_begin():
        pack[0:2] = vec[0:2]
        pack[2:3] = sums[:, :D]
        pack[3:4] = sums[:, 2 * D :]
        pack[4:5] = vec_mlp[2:3] + out_bias_part[...]
        pack[5:7] = vec_mlp[0:2]
        pack[7:8] = vec_mlp[3:4]
        for b in range(4):
            pack[8 + b : 9 + b] = up_bias_grad[:, D * b : D * (b + 1)]
        pack[12:16] = jnp.zeros((4, D), f32)
        for c in to_near():
            c.start()

    def small_middle():
        for c in to_near():
            c.wait()
        part = pack[...]
        for j in range(wins - 1):
            part += near[j]
        total[...] = part
        for c in to_far():
            c.start()

    def small_end():
        for c in to_far():
            c.wait()
        part = total[...]
        for j in range(dps - 1):
            part += far[j]
        small_sum[...] = part

    @pl.when(step == 0)
    def _():
        place.greet(all_wins=True)
        for s in late:
            s.load()
        vec[...] = jnp.zeros_like(vec)
        begin()

    x = with_region(patches[...].astype(f32), region_mid[...], step == pl.num_programs(0) - 1)
    vhat, inverse = norm_stats(x)
    grad_in = nt(grad_triple[...].reshape(rows, 3 * D), w_qkv[...])
    vec[0:1] += col(grad_in * vhat)
    vec[1:2] += col(grad_in)
    total_rows = grad_middle[...].reshape(rows, D).astype(f32) + norm_back(vhat, inverse, row(vecs, GAIN1), grad_in)
    patch_grad[...] = total_rows.astype(bf16).reshape(tokens, count, D)

    def end():
        late_step(3)
        owners_begin()
        early_step(6)
        late_step(4)
        region_end()
        small_begin()
        late_step(5)
        small_middle()
        late_step(6)
        early_step(7)
        small_end()
        late_step(7)
        early_step(8)
        late_step(8)

    def middle():
        late_step(2)
        early_step(5)

    hooks = {
        0: lambda: late_step(1),
        3: middle,
        4: end,
    }
    for when, todo in hooks.items():
        pl.when(step == when)(todo)


def last_kernel(
    up, down_t, first, second, small, patch_in, region_in,
    patch_grad, region_grad, in_gain, in_shift, qkv, qkv_bias, out_grad, out_bias, mlp_gain, mlp_shift,
    up_grad, up_bias, down_grad, down_bias,
):
    up_grad[...] = up[...].astype(f32)
    down_grad[...] = down_t[...].T.astype(f32)
    qkv[:, : 2 * D] = first[...].astype(f32)
    qkv[:, 2 * D :] = second[:, :D].astype(f32)
    out_grad[...] = second[:, D:].astype(f32)
    patch_grad[...] = patch_in[...]

    @pl.when(pl.program_id(0) == 0)
    def _():
        region_grad[...] = region_in[...]
        for at, v in ((0, in_gain), (1, in_shift), (4, out_bias), (5, mlp_gain), (6, mlp_shift), (7, down_bias)):
            v[...] = small[at : at + 1].reshape(D)
        qkv_bias[...] = small[2:4]
        up_bias[...] = jnp.concatenate([small[8 + b : 9 + b] for b in range(FF // D)], axis=1).reshape(FF)


def shards(
    wins, dps,
    patches, regional, window_image, in_gain, in_shift, w_qkv, qkv_bias, w_out, out_bias,
    mlp_gain, mlp_shift, w_up, up_bias, w_down, down_bias, patch_cot, region_cot,
):
    _, count, patch, _ = patches.shape
    group = window_image.shape[1]
    x = patches[0].transpose(1, 0, 2)
    cot = patch_cot[0].transpose(1, 0, 2)
    reg = regional[0]
    rcot = region_cot[0]
    const = lambda *arrays: [whole(a) for a in arrays]
    block = lambda a, n: (a, (n,) + a.shape[1:], lambda i: (i, 0, 0))
    block_out = lambda shape, n, dtype=bf16: ((shape, dtype), (n,) + shape[1:], lambda i: (i, 0, 0))
    triple, local_in, vecs, region_triple, gathered, probs_r, merged_r, region_mid, triple0, local_in0 = call(
        functools.partial(front_kernel, wins, dps), (pl.cdiv(patch, 7),),
        [block(x, 7)]
        + const(reg, window_image, in_gain, in_shift, w_qkv, qkv_bias, w_out, out_bias, mlp_gain, mlp_shift, up_bias, down_bias),
        [block_out((patch, count, 3 * D), 7), block_out((patch, count, D), 7), whole_out((16, D), f32), whole_out((count, 3 * D), bf16),
         whole_out((group, 3 * D), bf16), whole_out((2, group, 8 * count), bf16), whole_out((count, D), bf16),
         whole_out((count, D), f32), whole_out((count, 3 * D), bf16), whole_out((count, D), bf16)],
        [pltpu.VMEM((group, 3 * D), bf16), pltpu.VMEM((count, 3 * D), bf16), pltpu.VMEM((group, 128), f32),
         pltpu.SemaphoreType.DMA((8 * wins,))],
        name="front", collective_id=2,
    )
    steps = (count // WC,)
    mid = lambda a: (a, (a.shape[0], WC, a.shape[2]), lambda i: (0, i, 0))
    mid_out = lambda shape, dtype=bf16: ((shape, dtype), (shape[0], WC, shape[2]), lambda i: (0, i, 0))
    tail = lambda a: (a, (WC, a.shape[1]), lambda i: (i, 0))
    merged, probs = call(
        local_fwd_kernel, steps, [mid(triple), tail(triple0)],
        [mid_out((patch + 1, count, D)), ((((count, TP, HEADS * TP)), bf16), (WC, TP, HEADS * TP), lambda i: (i, 0, 0))],
        [pltpu.VMEM((12, TP * WC, 128), f32), pltpu.VMEM((4, TP * WC, 128), f32)], name="local_fwd",
    )
    n = 10
    rows_grid = ((patch + 1) // n,)
    patch_out, region_out, grad_middle, grad_merged, up_grad, down_grad_t, out_local, vec_mlp, up_bias_grad = call(
        mlp_kernel, rows_grid,
        [block(x, n), whole(region_mid), block(merged, n), block(cot, n)]
        + const(rcot, vecs, w_out, w_up, w_down),
        [block_out((patch, count, D), n), whole_out((count, D), bf16),
         block_out((patch + 1, count, D), n), block_out((patch + 1, count, D), n),
         whole_out((D, FF), bf16), whole_out((D, FF), bf16), whole_out((D, D), f32),
         whole_out((8, D), f32), whole_out((1, FF), f32)],
        [pltpu.VMEM((D, FF), f32), pltpu.VMEM((D, FF), f32)], name="mlp",
    )
    last_rows = rows_of(wins, dps)[1]
    grad_triple, up_part, down_part, terms, grad_query, low_first, low_second, sums, out_bias_part, grad_mid = call(
        functools.partial(back_kernel, wins, dps), steps,
        [mid(triple), tail(triple0), (probs, (WC, TP, HEADS * TP), lambda i: (i, 0, 0), group > 512), mid(grad_merged), mid(local_in), tail(local_in0)]
        + const(region_triple, gathered, probs_r, merged_r, region_mid)
        + [(grad_middle, (1, count, D), lambda i: (patch, 0, 0))]
        + const(vecs, w_qkv, w_out, out_local) + [left(a.reshape(stream_shape(wins, FF))) for a in (up_grad, down_grad_t)],
        [mid_out((patch + 1, count, 3 * D)), whole_out((last_rows, FF), bf16), whole_out((last_rows, FF), bf16),
         whole_out((group, 2 * D), bf16), whole_out((count, D), bf16), whole_out(stream_shape(wins, 2 * D), bf16),
         whole_out(stream_shape(wins, 2 * D), bf16),
         whole_out((1, 3 * D), f32), whole_out((1, D), f32), whole_out((count, D), f32)],
        [pltpu.VMEM((16, TP * WC, 128), f32), pltpu.VMEM((12, TP * WC, 128), f32), pltpu.VMEM((count, 3 * D), bf16),
         pltpu.VMEM((D, 3 * D), f32), pltpu.VMEM((count, D), bf16)]
        + stream_scratch(wins, dps, FF, "down") * 2,
        name="back", collective_id=0,
    )
    patch_grad, region_grad, small, up_sum, down_sum, first_sum, second_sum = call(
        functools.partial(tail_kernel, wins, dps), rows_grid,
        [block(x, n), block(grad_triple, n), block(grad_middle, n)]
        + const(region_mid, vecs, w_qkv, terms, grad_query, reg, grad_mid, vec_mlp, up_bias_grad, sums, out_bias_part, up_part, down_part)
        + [left(low_first), left(low_second)],
        [block_out((patch, count, D), n), whole_out((count, D), bf16), whole_out((16, D), f32)]
        + [left_out(stream_shape(wins, FF), bf16)] * 2 + [left_out(stream_shape(wins, 2 * D), bf16)] * 2,
        [pltpu.VMEM((8, D), f32),
         pltpu.VMEM((wins // 2, count, 2 * D), bf16), pltpu.SemaphoreType.DMA((wins,)), pltpu.VMEM((wins // 2, count, 2 * D), bf16),
         pltpu.VMEM((wins // 2, count, 2 * D), bf16), pltpu.SemaphoreType.DMA((wins,)),
         pltpu.VMEM((16, D), f32), pltpu.VMEM((wins - 1, 16, D), f32), pltpu.SemaphoreType.DMA((2 * wins,)),
         pltpu.VMEM((16, D), f32), pltpu.VMEM((max(dps - 1, 1), 16, D), f32), pltpu.SemaphoreType.DMA((2 * dps,))]
        + stream_scratch(wins, dps, 2 * D) * 2 + stream_scratch(wins, dps, FF, "back") * 2,
        name="tail", collective_id=1,
    )
    up_sum, down_sum = up_sum.reshape(D, FF), down_sum.reshape(D, FF)
    first_sum, second_sum = first_sum.reshape(D, 2 * D), second_sum.reshape(D, 2 * D)
    n = 2
    down = lambda i: (i, 0)
    vector = lambda size: ((((size,), f32)), (size,), lambda i: (0,))
    token = -(-patch // n)
    tokens = lambda i: (lax.min(i, (patch - 1) // token), 0, 0)
    (
        patch_grad, region_grad, in_gain_grad, in_shift_grad, qkv_grad, qkv_bias_grad, out_grad, out_bias_grad,
        mlp_gain_grad, mlp_shift_grad, up_grad, up_bias_grad, down_grad, down_bias_grad,
    ) = call(
        last_kernel, (n,),
        [(up_sum, (D // n, FF), down), (down_sum, (D, FF // n), lambda i: (0, i))]
        + [(a, (D // n, 2 * D), down) for a in (first_sum, second_sum)]
        + [whole(small), (patch_grad, (token, count, D), tokens), whole(region_grad)],
        [(((patch, count, D), bf16), (token, count, D), tokens), whole_out((count, D), bf16), vector(D), vector(D),
         (((D, 3 * D), f32), (D // n, 3 * D), down), whole_out((2, D), f32), (((D, D), f32), (D // n, D), down), vector(D),
         vector(D), vector(D), (((D, FF), f32), (D // n, FF), down), vector(FF), (((FF, D), f32), (FF // n, D), down), vector(D)],
        name="last",
    )
    return (
        patch_out.transpose(1, 0, 2)[None], region_out[None], patch_grad.transpose(1, 0, 2)[None], region_grad[None],
        in_gain_grad, in_shift_grad, qkv_grad, qkv_bias_grad, out_grad, out_bias_grad,
        mlp_gain_grad, mlp_shift_grad, up_grad, up_bias_grad, down_grad, down_bias_grad,
    )


def solution(mesh):
    wide = P("dp", "win", None, None)
    narrow = P("dp", "win", None)
    in_specs = (wide, narrow, P("dp", None)) + (P(),) * 12 + (wide, narrow)
    out_specs = (wide, narrow, wide, narrow) + (P(),) * 12
    return jax.shard_map(functools.partial(shards, mesh.shape["win"], mesh.shape["dp"]), mesh=mesh, in_specs=in_specs, out_specs=out_specs, check_vma=False)
```
